128 devices in a mesh: pas: 32 (over y, z, core), tp: 4 (over x).
Axes of the slice: x: 4, y: 4, z: 4, core: 2. Of those that a mesh axis runs over, the one named last changes fastest.
Arguments:
- passage_hidden: bfloat16 [32768, 8192], P('pas', 'tp'), may hold values from -6 to 6
- kv_weight: bfloat16 [1024, 8192], P('pas', 'tp'), may hold values from -0.0625 to 0.0625
- queries: bfloat16 [16384, 4096], P('pas', 'tp'), may hold values from -600 to 600
- query_kv: bfloat16 [16384, 1024], P('pas', 'tp'), may hold values from -6 to 6
- out_grad: bfloat16 [16384, 4096], P('pas', 'tp'), may hold values from -6 to 6
- source_device: int32 [128, 8], P('pas'), may hold values from 0 to 31, all different within a row; in each aligned block of 4 rows (0 to 3, 4 to 7, ...) at most 2 rows name the same one
- source_slot: int32 [128, 8], P('pas'), may hold values from 0 to 7
Outputs:
- query_grad: bfloat16 [16384, 4096], P('pas', 'tp')
- query_kv_grad: bfloat16 [16384, 1024], P('pas', 'tp')
- weight_grad: float32 [1024, 8192], P('pas', 'tp')
The draws below stay inside these ranges and needn't reach their ends.
Inputs may be any that keep to these rules, and one draw needn't show every extreme that they name: `source_device`: each query names 8 different owners; among the 4 queries of one index of pas no owner is named more than 2 times, and one owner exactly 2 times.
All inputs are finite; a program needn't handle non-finite values.
Results may differ from the reference program's by a relative error of at most 0.0095.
Values may be sent and summed in bfloat16 or wider, within the bound.
No kernel may reach another device: no remote copies, remote signals or barrier semaphores. Data moves between devices by JAX's collectives and lax.ppermute only.
A program may use at most 128 MiB of HBM per device.

```python
import math
import jax
import jax.numpy as jnp
import numpy as np
from jax import lax

D = 8192
HD = 128
PLEN = 128
PAS_DEV = 8
Q_DEV = 4
QLEN = 128
TOPR = 8
OWNERS = 32
CAP = 2
PASSAGES = 256
QUERIES = 128
QH = 32
KVW = 1024


def shared_pairs(key):
    values = jax.random.normal(key, (QUERIES * QLEN, KVW), jnp.float32)
    return jnp.clip(values, -6.0, 6.0).astype(jnp.bfloat16).astype(jnp.float32)


def draw_query_kv(key, part):
    pairs = shared_pairs(key)
    return pairs.astype(jnp.bfloat16)


def draw_queries(key, part):
    key = jax.random.fold_in(key, 11)
    base = jax.random.normal(key, (QUERIES * QLEN, QH * HD), jnp.float32)
    return jnp.clip(base, -600.0, 600.0).astype(jnp.bfloat16)


def plant(drawn, stream_key, least, top_value):
    longest = drawn.shape.index(max(drawn.shape))
    spots = []
    for shift in (0, 1):
        where = [jax.random.randint(jax.random.fold_in(stream_key, axis), (), 0, length) for axis, length in enumerate(drawn.shape)]
        where[longest] = (where[longest] + shift) % drawn.shape[longest]
        spots.append(tuple(where))
    return drawn.at[spots[0]].set(least).at[spots[1]].set(top_value)


def block_levels(own_key, extent, cuts, least, high):
    def one(position, blocks):
        steps = jax.random.uniform(jax.random.fold_in(jax.random.fold_in(own_key, 6), position), (blocks,), jnp.float32, least / len(cuts), high / len(cuts))
        return jnp.repeat(jnp.exp(steps), extent[position] // blocks).reshape((-1,) + (1,) * (len(extent) - position - 1))

    loudness = one(*cuts[0])
    for cut in cuts[1:]:
        loudness = loudness * one(*cut)
    return loudness


def routed_block(stream_key, own, number, rows, count, top, bound, slope):
    ranking = jax.random.permutation(stream_key, count)
    heavy_load, usual = load_shares(count, rows * top, bound, slope, True), load_shares(count, rows * top, bound, slope, False)
    places = jnp.arange(count)

    def named(sizes, offset_by):
        used = int((sizes > 0).sum())
        fixed = max(1, used // 4)
        passed = fixed + (places - fixed + offset_by * (used - fixed)) % max(1, count - fixed)
        return jnp.zeros((count,), jnp.int32).at[ranking[jnp.where(places < fixed, places, passed)]].set(jnp.asarray(sizes, jnp.int32))

    sizes = jnp.where(number % 4 == 0, named(heavy_load, number // 4), named(usual, number - number // 4 - 1))
    mixed = jax.random.permutation(jax.random.fold_in(own, 3), count)
    source_of, sink = mixed[0:count // 2 * 2:2], mixed[1:count // 2 * 2:2]
    margin = jnp.minimum(sizes[source_of] - 1, bound - sizes[sink]) // 2
    margin = jnp.where((source_of == ranking[0]) | (sink == ranking[0]) | (sizes[sink] == 0), 0, jnp.maximum(margin, 0))
    passed = jax.random.randint(jax.random.fold_in(own, 4), (count // 2,), 0, 1 << 20) % (margin + 1)
    sizes = sizes.at[source_of].add(-passed).at[sink].add(passed)
    members = jnp.searchsorted(jnp.cumsum(sizes), jnp.arange(rows * top), side="right").astype(jnp.int32)
    listing = members.reshape(top, rows).T
    listing = listing[jax.random.permutation(jax.random.fold_in(own, 1), rows)]
    offset_by = jax.random.randint(jax.random.fold_in(own, 2), (rows, 1), 0, top)
    return jnp.take_along_axis(listing, (jnp.arange(top)[None, :] + offset_by) % top, axis=1)


def load_shares(amount, total, reach, lean, full):
    loads = [(1 << 20) // math.isqrt(grade ** lean) + 1 for grade in range(1, amount + 1)]
    largest = reach if full else min(reach, max(-(-total // amount), total * loads[0] // sum(loads)))
    least = 1 if total - largest >= amount - 1 else 0
    counts, rest = [largest] + [least] * (amount - 1), total - largest - least * (amount - 1)
    while rest > 0:
        candidates = [i for i in range(1, amount) if counts[i] < largest] or [i for i in range(1, amount) if counts[i] < reach]
        mass, remaining = sum([loads[i] for i in candidates]), rest
        for i in candidates:
            more = min(reach - counts[i], max(1, remaining * loads[i] // mass), rest)
            counts[i] = counts[i] + more
            rest = rest - more
    return np.array(counts)


def gaussian(own_key, extent, scale, bound, shards=(), held_as=jnp.bfloat16):
    values = scale * jax.random.normal(own_key, extent, jnp.float32)
    if shards:
        values = values * block_levels(own_key, extent, shards, -0.22, 0.18)
    return jnp.clip(values, -bound, bound).astype(held_as)


def setup_inputs(seed: int = 0) -> dict:
    arg_keys = jax.random.split(jax.random.key(seed), 8)
    passage_hidden = gaussian(arg_keys[0], (PASSAGES * PLEN, D), 1.0, 6.0, ((0, 32), (1, 4)))
    kv_weight = gaussian(arg_keys[1], (KVW, D), D ** -0.5, 0.0625, ((0, 32), (1, 4)))
    queries = draw_queries(jax.random.fold_in(arg_keys[7], 71), 0)
    query_kv = draw_query_kv(jax.random.fold_in(arg_keys[7], 71), 0)
    out_grad = gaussian(arg_keys[4], (QUERIES * QLEN, QH * HD), 1.0, 6.0, ((0, 32), (1, 4)))
    source_device_keys = jax.random.split(jax.random.fold_in(arg_keys[5], 1), QUERIES // Q_DEV)
    source_device_turns = jax.random.permutation(jax.random.fold_in(arg_keys[5], 3), QUERIES // Q_DEV)
    source_device = jax.vmap(lambda own, number: routed_block(jax.random.fold_in(arg_keys[5], 2), own, number, Q_DEV, OWNERS, TOPR, CAP, 2))(source_device_keys, source_device_turns).reshape((QUERIES, TOPR))
    source_slot = plant(jax.random.randint(arg_keys[6], (QUERIES, TOPR), 0, PAS_DEV), jax.random.fold_in(arg_keys[6], 1), 0, PAS_DEV - 1).astype(jnp.int32)
    return {"passage_hidden": passage_hidden, "kv_weight": kv_weight, "queries": queries, "query_kv": query_kv, "out_grad": out_grad, "source_device": source_device, "source_slot": source_slot}


def attend_block(query_rows, keys_values, grad_out, prefix):
    highest = lax.Precision.HIGHEST
    query_len = query_rows.shape[0]
    key_len = keys_values.shape[0]
    kv_heads = keys_values.shape[1] // (2 * HD)
    group_size = query_rows.shape[1] // (HD * kv_heads)
    paired = keys_values.astype(jnp.float32).reshape(key_len, kv_heads, 2, HD)
    key_heads = paired[:, :, 0, :]
    value_heads = paired[:, :, 1, :]
    query_heads = query_rows.astype(jnp.float32).reshape(query_len, kv_heads, group_size, HD)
    grad_heads = grad_out.astype(jnp.float32).reshape(query_len, kv_heads, group_size, HD)
    scaling = HD ** -0.5
    scores = jnp.einsum('qhgd,khd->hgqk', query_heads, key_heads, precision=highest) * scaling
    row_index = jnp.arange(query_len)[:, None]
    col_index = jnp.arange(key_len)[None, :]
    visible = jnp.logical_or(col_index < prefix, col_index - prefix <= row_index)
    scores = jnp.where(visible, scores, jnp.float32(-1e30))
    largest = jnp.max(scores, axis=-1, keepdims=True)
    exponent = jnp.exp(scores - largest)
    weights = exponent / jnp.sum(exponent, axis=-1, keepdims=True)
    weights_low = lax.optimization_barrier(weights.astype(jnp.bfloat16)).astype(jnp.float32)
    outputs = jnp.einsum('hgqk,khd->hgqd', weights_low, value_heads, precision=highest)
    delta_rows = jnp.sum(outputs * grad_heads.transpose(1, 2, 0, 3), axis=-1, keepdims=True)
    grad_weights = jnp.einsum('qhgd,khd->hgqk', grad_heads, value_heads, precision=highest)
    grad_scores = weights * (grad_weights - delta_rows)
    grad_low = lax.optimization_barrier(grad_scores.astype(jnp.bfloat16)).astype(jnp.float32)
    grad_query = jnp.einsum('hgqk,khd->qhgd', grad_low, key_heads, precision=highest) * scaling
    grad_query = grad_query.astype(jnp.bfloat16).reshape(query_len, kv_heads * group_size * HD)
    grad_keys = jnp.einsum('hgqk,qhgd->khd', grad_low, query_heads, precision=highest) * scaling
    grad_values = jnp.einsum('hgqk,qhgd->khd', weights_low, grad_heads, precision=highest)
    grad_pairs = jnp.stack([grad_keys, grad_values], axis=2).reshape(key_len, kv_heads * 2 * HD)
    return grad_query, grad_pairs


def reference(passage_hidden, kv_weight, queries, query_kv, out_grad, source_device, source_slot):
    width = kv_weight.shape[0]
    projected = jnp.dot(passage_hidden, kv_weight.T, preferred_element_type=jnp.float32).astype(jnp.bfloat16)
    passage_kv = projected.reshape(PASSAGES, PLEN, width)
    passage_ids = (source_device * PAS_DEV + source_slot).astype(jnp.int32)
    remote_rows = TOPR * PLEN

    def one_query(grad_total, inputs):
        query_rows, own_pairs, grad_out, chosen = inputs
        fetched = passage_kv[chosen].reshape(remote_rows, width)
        keys_values = jnp.concatenate([fetched, own_pairs], axis=0)
        grad_query, grad_pairs = attend_block(query_rows, keys_values, grad_out, remote_rows)
        remote_grad = lax.optimization_barrier(grad_pairs[:remote_rows].astype(jnp.bfloat16))
        remote_grad = remote_grad.astype(jnp.float32).reshape(TOPR, PLEN, width)
        grad_total = grad_total.at[chosen].add(remote_grad)
        own_grad = grad_pairs[remote_rows:].astype(jnp.bfloat16)
        return grad_total, (grad_query, own_grad)

    initial = jnp.zeros((PASSAGES, PLEN, width), jnp.float32)
    inputs = (queries.reshape(QUERIES, QLEN, queries.shape[1]),
              query_kv.reshape(QUERIES, QLEN, width),
              out_grad.reshape(QUERIES, QLEN, out_grad.shape[1]),
              passage_ids)
    grad_total, (grad_queries, own_grads) = lax.scan(one_query, initial, inputs)
    grad_kv = grad_total.astype(jnp.bfloat16).reshape(PASSAGES * PLEN, width)
    weight_grad = jnp.dot(grad_kv.T, passage_hidden, preferred_element_type=jnp.float32)
    return (grad_queries.reshape(QUERIES * QLEN, queries.shape[1]),
            own_grads.reshape(QUERIES * QLEN, width),
            weight_grad)
```

```python
import functools
import math

import jax
import jax.numpy as jnp
from jax import lax
from jax.experimental import pallas as pl
from jax.experimental.pallas import tpu as pltpu
from jax.sharding import PartitionSpec as P

HD = 128
PLEN = 128
BF = jnp.bfloat16
F32 = jnp.float32
NT = (((1,), (1,)), ((), ()))
TN = (((0,), (0,)), ((), ()))


def attention_kernel(
    n_src, src_buf, src_row, dst_row, q_ref, do_ref, own_ref, *rest
):
    srcs = rest[:n_src]
    dq_ref, down_ref, out_ref = rest[n_src : n_src + 3]
    kv, stage, q_st, do_st, p_t, ds_t, in_sem, out_sem = rest[n_src + 3 :]
    step = pl.program_id(0)
    steps = pl.num_programs(0)
    group = q_ref.shape[1] // HD
    retrieved = in_sem.shape[1]
    rows = retrieved * PLEN
    keys = rows + own_ref.shape[0]
    slot = lax.rem(step, 2)
    scaling = HD ** (-0.5)

    def fetch(query, into):
        for j in range(retrieved):
            at = query * retrieved + j
            for b in range(n_src):

                @pl.when(src_buf[at] == b)
                def _():
                    pltpu.make_async_copy(
                        srcs[b].at[src_row[at]],
                        kv.at[into, pl.ds(j * PLEN, PLEN)],
                        in_sem.at[into, j],
                    ).start()

    @pl.when(step == 0)
    def _():
        fetch(0, 0)

    @pl.when(step + 1 < steps)
    def _():
        fetch(step + 1, 1 - slot)

    for g in range(group):
        q_st[pl.ds(g * HD, HD), :] = q_ref[:, g * HD : (g + 1) * HD]
        do_st[pl.ds(g * HD, HD), :] = do_ref[:, g * HD : (g + 1) * HD]
    kv[slot, pl.ds(rows, keys - rows), :] = own_ref[...]
    for j in range(retrieved):
        pltpu.make_async_copy(
            srcs[0].at[0], kv.at[slot, pl.ds(j * PLEN, PLEN)], in_sem.at[slot, j]
        ).wait()

    k_all = kv[slot, :, :HD]
    v_all = kv[slot, :, HD:]
    width = 2 * HD
    key_at = lax.broadcasted_iota(jnp.int32, (keys - rows, width), 0)
    tok_at = lax.broadcasted_iota(jnp.int32, (keys - rows, width), 1) % HD
    visible = key_at <= tok_at
    for g in range(0, group, 2):
        cols = pl.ds(g * HD, width)
        s = lax.dot_general(k_all, q_st[cols, :], NT, preferred_element_type=F32)
        s = jnp.concatenate(
            [s[:rows], jnp.where(visible, s[rows:], F32(-1e30))], axis=0
        )
        largest = jnp.max(s, axis=0, keepdims=True)
        e = jnp.exp2((s - largest) * F32(scaling * math.log2(math.e)))
        w = e * (1.0 / jnp.sum(e, axis=0, keepdims=True))
        w_low = w.astype(BF)
        p_t[:, cols] = w_low
        gw = lax.dot_general(v_all, do_st[cols, :], NT, preferred_element_type=F32)
        delta = jnp.sum(w_low.astype(F32) * gw, axis=0, keepdims=True)
        ds_t[:, cols] = (w * (gw - delta)).astype(BF)
    d_v = jnp.dot(p_t[...], do_st[...], preferred_element_type=F32)
    d_k = jnp.dot(ds_t[...], q_st[...], preferred_element_type=F32) * F32(scaling)
    dq_t = lax.dot_general(k_all, ds_t[...], TN, preferred_element_type=F32) * F32(scaling)
    for g in range(group):
        dq_ref[:, g * HD : (g + 1) * HD] = dq_t[:, g * HD : (g + 1) * HD].T.astype(BF)

    down_ref[:, :HD] = d_k[rows:].astype(BF)
    down_ref[:, HD:] = d_v[rows:].astype(BF)

    def sent(query, at_slot, j):
        return pltpu.make_async_copy(
            stage.at[at_slot, pl.ds(j * PLEN, PLEN)],
            out_ref.at[dst_row[query * retrieved + j]],
            out_sem.at[at_slot, j],
        )

    @pl.when(step >= 2)
    def _():
        for j in range(retrieved):
            sent(step - 2, slot, j).wait()

    stage[slot, :, :HD] = d_k[:rows].astype(BF)
    stage[slot, :, HD:] = d_v[:rows].astype(BF)
    for j in range(retrieved):
        sent(step, slot, j).start()

    @pl.when(step == steps - 1)
    def _():
        for j in range(retrieved):
            if steps > 1:
                sent(step - 1, 1 - slot, j).wait()
            sent(step, slot, j).wait()


def attention(queries, out_grad, query_kv, sources, src_buf, src_row, dst_row, slots, n_query):
    rows, width = queries.shape
    qlen = rows // n_query
    retrieved = src_buf.shape[0] // n_query
    keys = retrieved * PLEN + qlen
    local = query_kv.shape[1]
    block = lambda w: pl.BlockSpec((qlen, w), lambda i, *_: (i, 0))
    hbm = pl.BlockSpec(memory_space=pl.ANY)
    return pl.pallas_call(
        functools.partial(attention_kernel, len(sources)),
        out_shape=(
            jax.ShapeDtypeStruct((rows, width), BF),
            jax.ShapeDtypeStruct((rows, local), BF),
            jax.ShapeDtypeStruct((slots, PLEN, local), BF),
        ),
        grid_spec=pltpu.PrefetchScalarGridSpec(
            num_scalar_prefetch=3,
            grid=(n_query,),
            in_specs=[block(width), block(width), block(local)] + [hbm] * len(sources),
            out_specs=(block(width), block(local), hbm),
            scratch_shapes=[
                pltpu.VMEM((2, keys, local), BF),
                pltpu.VMEM((2, retrieved * PLEN, local), BF),
                pltpu.VMEM((width, HD), BF),
                pltpu.VMEM((width, HD), BF),
                pltpu.VMEM((keys, width), BF),
                pltpu.VMEM((keys, width), BF),
                pltpu.SemaphoreType.DMA((2, retrieved)),
                pltpu.SemaphoreType.DMA((2, retrieved)),
            ],
        ),
        compiler_params=pltpu.CompilerParams(vmem_limit_bytes=48 * 2**20),
        cost_estimate=pl.CostEstimate(
            flops=10 * n_query * keys * qlen * width,
            bytes_accessed=8 * rows * width + 4 * n_query * keys * local,
            transcendentals=n_query * keys * width,
        ),
        name="attention",
    )(src_buf, src_row, dst_row, queries, out_grad, query_kv, *sources)


def add_returned_kernel(slot_of, got_ref, out_ref, total):
    total[...] = jnp.zeros_like(total)

    @pl.loop(0, got_ref.shape[0])
    def _(n):
        place = slot_of[n]

        @pl.when(place >= 0)
        def _():
            total[place] += got_ref[n].astype(F32)

    out_ref[...] = total[...].astype(BF)


def add_returned(slot_of, returned, passages):
    shape = (passages,) + returned.shape[1:]
    return pl.pallas_call(
        add_returned_kernel,
        out_shape=jax.ShapeDtypeStruct(shape, BF),
        grid_spec=pltpu.PrefetchScalarGridSpec(
            num_scalar_prefetch=1,
            in_specs=[pl.BlockSpec(memory_space=pltpu.VMEM)],
            out_specs=pl.BlockSpec(memory_space=pltpu.VMEM),
            scratch_shapes=[pltpu.VMEM(shape, F32)],
        ),
        compiler_params=pltpu.CompilerParams(vmem_limit_bytes=32 * 2**20),
        cost_estimate=pl.CostEstimate(
            flops=returned.size, bytes_accessed=2 * returned.size, transcendentals=0
        ),
        name="add_returned",
    )(slot_of, returned)


def requests(source_device, source_slot, owners, capacity):
    flat_device = source_device.reshape(-1)
    flat_slot = source_slot.reshape(-1)
    owner_hits = (flat_device[:, None] == jnp.arange(owners, dtype=jnp.int32)[None, :]).astype(
        jnp.int32
    )
    at = jnp.arange(flat_device.shape[0])
    earlier_same = jnp.logical_and(
        flat_device[:, None] == flat_device[None, :], at[None, :] < at[:, None]
    )
    ranking = jnp.sum(earlier_same.astype(jnp.int32), axis=1)
    slot_hits = (ranking[:, None] == jnp.arange(capacity, dtype=jnp.int32)[None, :]).astype(
        jnp.int32
    )
    placed = owner_hits[:, :, None] * slot_hits[:, None, :]
    table = jnp.sum(placed * (flat_slot + 1)[:, None, None], axis=0) - 1
    return flat_device, flat_slot, ranking, table


def per_device(passage_hidden, kv_weight, queries, query_kv, out_grad, source_device, source_slot):
    owners = lax.axis_size("pas")
    rows_local = passage_hidden.shape[0]
    local_width = query_kv.shape[1]
    passages_here = rows_local // PLEN
    queries_here = source_device.shape[0]
    requests_total = queries_here * source_device.shape[1]
    capacity = min(queries_here, max(2, 2 * requests_total // owners))
    flat_device, flat_slot, ranking, table = requests(
        source_device, source_slot, owners, capacity
    )
    wanted = lax.all_to_all(table, "pas", split_axis=0, concat_axis=0, tiled=True)
    partial_kv = jnp.einsum(
        "rd,cd->rc",
        passage_hidden,
        lax.all_gather(kv_weight, "pas", axis=0, tiled=True),
        preferred_element_type=F32,
    )
    passage_kv = lax.psum_scatter(partial_kv, "tp", scatter_dimension=1, tiled=True).astype(BF)
    passage_kv = passage_kv.reshape(passages_here, PLEN, local_width)
    piece_rows = lax.all_gather(passage_kv, "pas", axis=0, tiled=True)
    grad_queries, own_grads, outgoing = attention(
        queries,
        out_grad,
        query_kv,
        [piece_rows],
        jnp.zeros_like(flat_device),
        flat_device * passages_here + flat_slot,
        flat_device * capacity + ranking,
        owners * capacity,
        queries_here,
    )
    returned = lax.all_to_all(outgoing, "pas", split_axis=0, concat_axis=0, tiled=True)
    grad_kv = add_returned(wanted.reshape(-1), returned, passages_here)
    full_grad = lax.all_gather(grad_kv.reshape(rows_local, local_width), "tp", axis=1, tiled=True)
    weight_grad = lax.psum_scatter(
        jnp.einsum("rc,rd->cd", full_grad, passage_hidden, preferred_element_type=F32),
        "pas",
        scatter_dimension=0,
        tiled=True,
    )
    return grad_queries, own_grads, weight_grad


def solution(mesh):
    in_specs = (
        P("pas", "tp"),
        P("pas", "tp"),
        P("pas", "tp"),
        P("pas", "tp"),
        P("pas", "tp"),
        P("pas", None),
        P("pas", None),
    )
    out_specs = (P("pas", "tp"), P("pas", "tp"), P("pas", "tp"))
    return jax.shard_map(
        per_device, mesh=mesh, in_specs=in_specs, out_specs=out_specs, check_vma=False
    )
```

```python
import functools
import math

import jax
import jax.numpy as jnp
from jax import lax
from jax.experimental import pallas as pl
from jax.experimental.pallas import tpu as pltpu
from jax.sharding import PartitionSpec as P

HD = 128
PLEN = 128
BF = jnp.bfloat16
F32 = jnp.float32
NT = (((1,), (1,)), ((), ()))
TN = (((0,), (0,)), ((), ()))
SIDE = 4
OUT_ROWS = 32


def device_at(y, z, core):
    return (y * SIDE + z) * 2 + core


def ring_pairs(order, k):
    pairs = []
    for y in range(SIDE):
        for z in range(SIDE):
            for core in range(2):
                if (order + core) % 2 == 0:
                    to = device_at(y, (z + k) % SIDE, core)
                else:
                    to = device_at((y + k) % SIDE, z, core)
                pairs.append((device_at(y, z, core), to))
    return pairs


def send_first(x, k):
    return lax.ppermute(x, "pas", ring_pairs(0, k))


def send_second(x, k):
    return lax.ppermute(x, "pas", ring_pairs(1, k))


def send_tp(x, k):
    return lax.ppermute(x, "tp", [(i, (i + k) % SIDE) for i in range(SIDE)])


def swap_cores(x):
    return lax.ppermute(x, "pas", [(i, i ^ 1) for i in range(2 * SIDE * SIDE)])


def ring_gather(x, send):
    half = x.shape[0] // 2
    left = send(x, 1)
    right = send(x, -1)
    return [x, left, send(left[:half], 1), send(right[half:], -1), right]


def here():
    pas = lax.axis_index("pas")
    return pas // (2 * SIDE), (pas // 2) % SIDE, pas % 2, lax.axis_index("tp")


def here_in_kernel():
    pas = lax.axis_index("pas")
    return (
        lax.div(pas, 2 * SIDE),
        lax.rem(lax.div(pas, 2), SIDE),
        lax.rem(pas, 2),
        lax.axis_index("tp"),
    )


def ring_mod(n):
    return lax.rem(n + 2 * SIDE, SIDE)


def project_kernel(chunk_rows, h_ref, *rest):
    pieces = rest[:10]
    outs = rest[10 : 10 + 4 * SIDE]
    weights, result, w_sem, out_sem = rest[10 + 4 * SIDE :]
    step = pl.program_id(0)
    y, z, core, tp = here_in_kernel()
    head_rows = weights.shape[0] // SIDE

    def shard_copies():
        copies = []
        for src in range(2):
            which = core if src == 0 else 1 - core
            first = jnp.where(which == 0, z, y)
            second = jnp.where(which == 0, y, z)
            for jb in range(SIDE):
                for ja in range(SIDE):
                    a = ring_mod(first - ja)
                    b = ring_mod(second - jb)
                    y_of = jnp.where(which == 0, b, a)
                    z_of = jnp.where(which == 0, a, b)
                    place = ring_mod(y_of - tp)
                    to = place * head_rows + z_of * 2 * OUT_ROWS + which * OUT_ROWS
                    if jb == 2:
                        piece, row = (2, ja) if ja < 2 else (3, ja - 2)
                    else:
                        piece, row = {0: 0, 1: 1, 3: 4}[jb], ja
                    copies.append(
                        pltpu.make_async_copy(
                            pieces[5 * src + piece].at[pl.ds(row * OUT_ROWS, OUT_ROWS)],
                            weights.at[pl.ds(pl.multiple_of(to, OUT_ROWS), OUT_ROWS)],
                            w_sem.at[src * SIDE * SIDE + jb * SIDE + ja],
                        )
                    )
        return copies

    @pl.when(step == 0)
    def _():
        for copy in shard_copies():
            copy.start()
        for copy in shard_copies():
            copy.wait()

    for j in range(SIDE):
        result[step * SIDE + j] = lax.dot_general(
            h_ref[...],
            weights[j * head_rows : (j + 1) * head_rows, :],
            NT,
            preferred_element_type=F32,
        )
    for i in range(4):
        for j in range(SIDE):

            @pl.when(step == i)
            def _():
                pltpu.make_async_copy(
                    result.at[i * SIDE + j], outs[i * SIDE + j], out_sem.at[i * SIDE + j]
                ).start()

    @pl.when(step == 3)
    def _():
        for n in range(4 * SIDE):
            pltpu.make_async_copy(result.at[n], outs[n], out_sem.at[n]).wait()


def project(hidden, pieces):
    rows, depth = hidden.shape
    quarter = rows // 4
    columns = 2 * SIDE * SIDE * OUT_ROWS
    head = columns // SIDE
    hbm = pl.BlockSpec(memory_space=pl.ANY)
    outs = [jax.ShapeDtypeStruct((quarter, head), F32)] * (4 * SIDE)
    return pl.pallas_call(
        functools.partial(project_kernel, quarter),
        out_shape=outs,
        grid=(4,),
        in_specs=[pl.BlockSpec((quarter, depth), lambda i: (i, 0))] + [hbm] * 10,
        out_specs=[hbm] * (4 * SIDE),
        scratch_shapes=[
            pltpu.VMEM((columns, depth), BF),
            pltpu.VMEM((4 * SIDE, quarter, head), F32),
            pltpu.SemaphoreType.DMA((2 * SIDE * SIDE,)),
            pltpu.SemaphoreType.DMA((4 * SIDE,)),
        ],
        compiler_params=pltpu.CompilerParams(vmem_limit_bytes=40 * 2**20),
        cost_estimate=pl.CostEstimate(
            flops=2 * rows * columns * depth,
            bytes_accessed=2 * rows * depth + 2 * columns * depth + 4 * rows * columns,
            transcendentals=0,
        ),
        name="project",
    )(hidden, *pieces)


def reduce_heads(parts):
    down, up = parts[0][3], parts[1][1]
    for first, second in ((2, 2), (1, 3), (0, 0)):
        down = send_tp(down, 1) + parts[0][first]
        up = send_tp(up, -1) + parts[1][second]
    return jnp.concatenate([down.astype(BF), up.astype(BF)], axis=0)


def weight_kernel(*refs):
    mine, theirs = refs[:5], refs[5:10]
    h_mine, h_theirs = refs[10:12]
    outs = refs[12:19]
    left, result = refs[19:]
    y, z, core, tp = here_in_kernel()
    rows = mine[0].shape[1]

    @pl.when(pl.program_id(0) == 0)
    def _():
        for half, refs_of in enumerate((mine, theirs)):
            at = 0
            for piece in refs_of:
                left[pl.ds(at, piece.shape[0]), half * rows : (half + 1) * rows] = piece[...]
                at += piece.shape[0]

    result[...] = jnp.dot(
        left[:, :rows], h_mine[...], preferred_element_type=F32
    ) + jnp.dot(left[:, rows:], h_theirs[...], preferred_element_type=F32)

    def block(ja, jb):
        a_z, a_y = ring_mod(z + ja), ring_mod(y + ja)
        b_z, b_y = ring_mod(z + jb), ring_mod(y + jb)
        y_of = jnp.where(core == 0, b_y, a_y)
        z_of = jnp.where(core == 0, a_z, b_z)
        at = ring_mod(tp - y_of) * SIDE * OUT_ROWS + z_of * OUT_ROWS
        return result[pl.ds(pl.multiple_of(at, OUT_ROWS), OUT_ROWS), :]

    for jb in range(SIDE):
        outs[0][jb] = block(0, jb)
    for ja in range(1, SIDE):
        for jb in range(SIDE):
            outs[2 * ja - 1 + jb // 2][jb % 2] = block(ja, jb).astype(BF)


def weight_product(mine, theirs, h_mine, h_theirs):
    rows, depth = h_mine.shape
    tile = 512
    heads_rows = SIDE * SIDE * OUT_ROWS
    whole = pl.BlockSpec(memory_space=pltpu.VMEM)
    out = lambda n: pl.BlockSpec((n, OUT_ROWS, tile), lambda i: (0, 0, i))
    halves = 2 * (SIDE - 1)
    return pl.pallas_call(
        weight_kernel,
        out_shape=[jax.ShapeDtypeStruct((SIDE, OUT_ROWS, depth), F32)]
        + [jax.ShapeDtypeStruct((SIDE // 2, OUT_ROWS, depth), BF)] * halves,
        grid=(depth // tile,),
        in_specs=[whole] * 10 + [pl.BlockSpec((rows, tile), lambda i: (0, i))] * 2,
        out_specs=[out(SIDE)] + [out(SIDE // 2)] * halves,
        scratch_shapes=[
            pltpu.VMEM((heads_rows, 2 * rows), BF),
            pltpu.VMEM((heads_rows, tile), F32),
        ],
        compiler_params=pltpu.CompilerParams(vmem_limit_bytes=40 * 2**20),
        cost_estimate=pl.CostEstimate(
            flops=4 * heads_rows * rows * depth,
            bytes_accessed=4 * rows * depth + 4 * heads_rows * depth,
            transcendentals=0,
        ),
        name="weight_product",
    )(*mine, *theirs, h_mine, h_theirs)


def reduce_owners(blocks):
    own, one_a, one_b, two_a, two_b, three_a, three_b = blocks
    from_left = send_first(two_a, 1)
    from_right = send_first(two_b, -1)
    left_b = send_first(one_b, 1)
    right_a = send_first(three_a, -1)
    left_a = send_first((one_a.astype(F32) + from_left).astype(BF), 1)
    right_b = send_first((three_b.astype(F32) + from_right).astype(BF), -1)
    total = (
        own
        + jnp.concatenate([left_a, left_b], axis=0).astype(F32)
        + jnp.concatenate([right_a, right_b], axis=0).astype(F32)
    )
    low = total[1:].astype(BF)
    left = send_second(low[0], 1)
    right = send_second(low[2], -1)
    far = send_second(low[1], 2)
    return total[0] + left.astype(F32) + right.astype(F32) + far.astype(F32)


def attention_kernel(
    n_src, src_buf, src_row, dst_row, q_ref, do_ref, own_ref, *rest
):
    srcs = rest[:n_src]
    dq_ref, down_ref, out_ref = rest[n_src : n_src + 3]
    kv, stage, q_st, do_st, p_t, ds_t, in_sem, out_sem = rest[n_src + 3 :]
    step = pl.program_id(0)
    steps = pl.num_programs(0)
    group = q_ref.shape[1] // HD
    retrieved = in_sem.shape[1]
    rows = retrieved * PLEN
    keys = rows + own_ref.shape[0]
    slot = lax.rem(step, 2)
    scaling = HD ** (-0.5)

    def fetch(query, into):
        for j in range(retrieved):
            at = query * retrieved + j
            for b in range(n_src):

                @pl.when(src_buf[at] == b)
                def _():
                    pltpu.make_async_copy(
                        srcs[b].at[src_row[at]],
                        kv.at[into, pl.ds(j * PLEN, PLEN)],
                        in_sem.at[into, j],
                    ).start()

    @pl.when(step == 0)
    def _():
        fetch(0, 0)

    @pl.when(step + 1 < steps)
    def _():
        fetch(step + 1, 1 - slot)

    for g in range(group):
        q_st[pl.ds(g * HD, HD), :] = q_ref[:, g * HD : (g + 1) * HD]
        do_st[pl.ds(g * HD, HD), :] = do_ref[:, g * HD : (g + 1) * HD]
    kv[slot, pl.ds(rows, keys - rows), :] = own_ref[...]
    for j in range(retrieved):
        pltpu.make_async_copy(
            srcs[0].at[0], kv.at[slot, pl.ds(j * PLEN, PLEN)], in_sem.at[slot, j]
        ).wait()

    k_all = kv[slot, :, :HD]
    v_all = kv[slot, :, HD:]
    width = 2 * HD
    key_at = lax.broadcasted_iota(jnp.int32, (keys - rows, width), 0)
    tok_at = lax.broadcasted_iota(jnp.int32, (keys - rows, width), 1) % HD
    visible = key_at <= tok_at
    for g in range(0, group, 2):
        cols = pl.ds(g * HD, width)
        s = lax.dot_general(k_all, q_st[cols, :], NT, preferred_element_type=F32)
        s = jnp.concatenate(
            [s[:rows], jnp.where(visible, s[rows:], F32(-1e30))], axis=0
        )
        largest = jnp.max(s, axis=0, keepdims=True)
        e = jnp.exp2((s - largest) * F32(scaling * math.log2(math.e)))
        w = e * (1.0 / jnp.sum(e, axis=0, keepdims=True))
        w_low = w.astype(BF)
        p_t[:, cols] = w_low
        gw = lax.dot_general(v_all, do_st[cols, :], NT, preferred_element_type=F32)
        delta = jnp.sum(w_low.astype(F32) * gw, axis=0, keepdims=True)
        ds_t[:, cols] = (w * (gw - delta)).astype(BF)
    d_v = jnp.dot(p_t[...], do_st[...], preferred_element_type=F32)
    d_k = jnp.dot(ds_t[...], q_st[...], preferred_element_type=F32) * F32(scaling)
    dq_t = lax.dot_general(k_all, ds_t[...], TN, preferred_element_type=F32) * F32(scaling)
    for g in range(group):
        dq_ref[:, g * HD : (g + 1) * HD] = dq_t[:, g * HD : (g + 1) * HD].T.astype(BF)

    down_ref[:, :HD] = d_k[rows:].astype(BF)
    down_ref[:, HD:] = d_v[rows:].astype(BF)

    def sent(query, at_slot, j):
        return pltpu.make_async_copy(
            stage.at[at_slot, pl.ds(j * PLEN, PLEN)],
            out_ref.at[dst_row[query * retrieved + j]],
            out_sem.at[at_slot, j],
        )

    @pl.when(step >= 2)
    def _():
        for j in range(retrieved):
            sent(step - 2, slot, j).wait()

    stage[slot, :, :HD] = d_k[:rows].astype(BF)
    stage[slot, :, HD:] = d_v[:rows].astype(BF)
    for j in range(retrieved):
        sent(step, slot, j).start()

    @pl.when(step == steps - 1)
    def _():
        for j in range(retrieved):
            if steps > 1:
                sent(step - 1, 1 - slot, j).wait()
            sent(step, slot, j).wait()


def attention(queries, out_grad, query_kv, sources, src_buf, src_row, dst_row, slots, n_query):
    rows, width = queries.shape
    qlen = rows // n_query
    retrieved = src_buf.shape[0] // n_query
    keys = retrieved * PLEN + qlen
    local = query_kv.shape[1]
    block = lambda w: pl.BlockSpec((qlen, w), lambda i, *_: (i, 0))
    hbm = pl.BlockSpec(memory_space=pl.ANY)
    return pl.pallas_call(
        functools.partial(attention_kernel, len(sources)),
        out_shape=(
            jax.ShapeDtypeStruct((rows, width), BF),
            jax.ShapeDtypeStruct((rows, local), BF),
            jax.ShapeDtypeStruct((slots, PLEN, local), BF),
        ),
        grid_spec=pltpu.PrefetchScalarGridSpec(
            num_scalar_prefetch=3,
            grid=(n_query,),
            in_specs=[block(width), block(width), block(local)] + [hbm] * len(sources),
            out_specs=(block(width), block(local), hbm),
            scratch_shapes=[
                pltpu.VMEM((2, keys, local), BF),
                pltpu.VMEM((2, retrieved * PLEN, local), BF),
                pltpu.VMEM((width, HD), BF),
                pltpu.VMEM((width, HD), BF),
                pltpu.VMEM((keys, width), BF),
                pltpu.VMEM((keys, width), BF),
                pltpu.SemaphoreType.DMA((2, retrieved)),
                pltpu.SemaphoreType.DMA((2, retrieved)),
            ],
        ),
        compiler_params=pltpu.CompilerParams(vmem_limit_bytes=48 * 2**20),
        cost_estimate=pl.CostEstimate(
            flops=10 * n_query * keys * qlen * width,
            bytes_accessed=8 * rows * width + 4 * n_query * keys * local,
            transcendentals=n_query * keys * width,
        ),
        name="attention",
    )(src_buf, src_row, dst_row, queries, out_grad, query_kv, *sources)


def add_returned_kernel(slot_of, got_ref, mine_ref, theirs_ref, total, turned):
    core = lax.rem(lax.axis_index("pas"), 2)
    total[...] = jnp.zeros_like(total)

    @pl.loop(0, got_ref.shape[0])
    def _(n):
        place = slot_of[n]

        @pl.when(place >= 0)
        def _():
            total[place] += got_ref[n].astype(F32)

    for p in range(total.shape[0]):
        turned[:, p * PLEN : (p + 1) * PLEN] = total[p].T.astype(BF)
    for z in range(SIDE):
        for ref, which in ((mine_ref, core), (theirs_ref, 1 - core)):
            at = pl.multiple_of(z * 2 * OUT_ROWS + which * OUT_ROWS, OUT_ROWS)
            ref[z * OUT_ROWS : (z + 1) * OUT_ROWS, :] = turned[pl.ds(at, OUT_ROWS), :]


def add_returned(slot_of, returned, passages):
    shape = (passages,) + returned.shape[1:]
    half = jax.ShapeDtypeStruct((shape[2] // 2, passages * PLEN), BF)
    whole = pl.BlockSpec(memory_space=pltpu.VMEM)
    return pl.pallas_call(
        add_returned_kernel,
        out_shape=(half, half),
        grid_spec=pltpu.PrefetchScalarGridSpec(
            num_scalar_prefetch=1,
            in_specs=[whole],
            out_specs=(whole, whole),
            scratch_shapes=[
                pltpu.VMEM(shape, F32),
                pltpu.VMEM((shape[2], passages * PLEN), BF),
            ],
        ),
        compiler_params=pltpu.CompilerParams(vmem_limit_bytes=32 * 2**20),
        cost_estimate=pl.CostEstimate(
            flops=returned.size, bytes_accessed=2 * returned.size, transcendentals=0
        ),
        name="add_returned",
    )(slot_of, returned)


def requests(source_device, source_slot, owners, capacity):
    flat_device = source_device.reshape(-1)
    flat_slot = source_slot.reshape(-1)
    owner_hits = (flat_device[:, None] == jnp.arange(owners, dtype=jnp.int32)[None, :]).astype(
        jnp.int32
    )
    at = jnp.arange(flat_device.shape[0])
    earlier_same = jnp.logical_and(
        flat_device[:, None] == flat_device[None, :], at[None, :] < at[:, None]
    )
    ranking = jnp.sum(earlier_same.astype(jnp.int32), axis=1)
    slot_hits = (ranking[:, None] == jnp.arange(capacity, dtype=jnp.int32)[None, :]).astype(
        jnp.int32
    )
    placed = owner_hits[:, :, None] * slot_hits[:, None, :]
    table = jnp.sum(placed * (flat_slot + 1)[:, None, None], axis=0) - 1
    return flat_device, flat_slot, ranking, table


def find_passages(flat_device, flat_slot, chunk):
    y, z, core, _ = here()
    owner_core = flat_device % 2
    z_of, y_of = (flat_device // 2) % SIDE, flat_device // (2 * SIDE)
    back_z, back_y = (z - z_of) % SIDE, (y - y_of) % SIDE
    ja = jnp.where(owner_core == 0, back_z, back_y)
    jb = jnp.where(owner_core == 0, back_y, back_z)
    piece = jnp.where(jb == 2, jnp.where(ja < 2, 2, 3), jnp.where(jb == 3, 4, jb))
    block = jnp.where(jb == 2, ja % 2, ja) * chunk + flat_slot % chunk
    group = (flat_slot // chunk) * 2 + (owner_core != core).astype(jnp.int32)
    return group * 5 + piece, block


def per_device(passage_hidden, kv_weight, queries, query_kv, out_grad, source_device, source_slot):
    owners = lax.axis_size("pas")
    rows_local = passage_hidden.shape[0]
    local_width = query_kv.shape[1]
    passages_here = rows_local // PLEN
    queries_here = source_device.shape[0]
    requests_total = queries_here * source_device.shape[1]
    capacity = min(queries_here, max(2, 2 * requests_total // owners))

    shards = ring_gather(kv_weight, send_first)
    shards = ring_gather(jnp.concatenate(shards, axis=0), send_second)
    partial = project(passage_hidden, shards + [swap_cores(s) for s in shards])
    hidden_theirs = swap_cores(passage_hidden)
    flat_device, flat_slot, ranking, table = requests(
        source_device, source_slot, owners, capacity
    )
    wanted = lax.all_to_all(table, "pas", split_axis=0, concat_axis=0, tiled=True)

    sources = []
    chunk = passages_here // 2
    for n in range(2):
        quarters = [partial[(2 * n + h) * SIDE : (2 * n + h + 1) * SIDE] for h in range(2)]
        own = reduce_heads(quarters).reshape(chunk, PLEN, local_width)
        pieces = ring_gather(own, send_first)
        pieces = ring_gather(jnp.concatenate(pieces, axis=0), send_second)
        sources += pieces + [swap_cores(p) for p in pieces]
    src_buf, src_row = find_passages(flat_device, flat_slot, chunk)
    grad_queries, own_grads, outgoing = attention(
        queries,
        out_grad,
        query_kv,
        sources,
        src_buf,
        src_row,
        flat_device * capacity + ranking,
        owners * capacity,
        queries_here,
    )
    returned = lax.all_to_all(outgoing, "pas", split_axis=0, concat_axis=0, tiled=True)
    mine, theirs = add_returned(wanted.reshape(-1), returned, passages_here)
    mine_heads = ring_gather(mine, send_tp)
    theirs_heads = ring_gather(swap_cores(theirs), send_tp)
    blocks = weight_product(mine_heads, theirs_heads, passage_hidden, hidden_theirs)
    return grad_queries, own_grads, reduce_owners(blocks)


def solution(mesh):
    in_specs = (
        P("pas", "tp"),
        P("pas", "tp"),
        P("pas", "tp"),
        P("pas", "tp"),
        P("pas", "tp"),
        P("pas", None),
        P("pas", None),
    )
    out_specs = (P("pas", "tp"), P("pas", "tp"), P("pas", "tp"))
    return jax.shard_map(
        per_device, mesh=mesh, in_specs=in_specs, out_specs=out_specs, check_vma=False
    )
```

```python
import functools
import math

import jax
import jax.numpy as jnp
from jax import lax
from jax.experimental import pallas as pl
from jax.experimental.pallas import tpu as pltpu
from jax.sharding import PartitionSpec as P

HD = 128
PLEN = 128
BF = jnp.bfloat16
F32 = jnp.float32
NT = (((1,), (1,)), ((), ()))
TN = (((0,), (0,)), ((), ()))
SIDE = 4
OUT_ROWS = 32
CHUNKS = 4


def device_at(y, z, core):
    return (y * SIDE + z) * 2 + core


def ring_pairs(order, k):
    pairs = []
    for y in range(SIDE):
        for z in range(SIDE):
            for core in range(2):
                if (order + core) % 2 == 0:
                    to = device_at(y, (z + k) % SIDE, core)
                else:
                    to = device_at((y + k) % SIDE, z, core)
                pairs.append((device_at(y, z, core), to))
    return pairs


def send_first(x, k):
    return lax.ppermute(x, "pas", ring_pairs(0, k))


def send_second(x, k):
    return lax.ppermute(x, "pas", ring_pairs(1, k))


def send_tp(x, k):
    return lax.ppermute(x, "tp", [(i, (i + k) % SIDE) for i in range(SIDE)])


def swap_cores(x):
    return lax.ppermute(x, "pas", [(i, i ^ 1) for i in range(2 * SIDE * SIDE)])


def ring_gather(x, send):
    left = send(x, 1)
    right = send(x, -1)
    return [x, left, send(x, 2), right]


def ring_gather_halves(x, send):
    half = x.shape[0] // 2
    left = send(x, 1)
    right = send(x, -1)
    return [x, left, send(left[:half], 1), send(right[half:], -1), right]


def here():
    pas = lax.axis_index("pas")
    return pas // (2 * SIDE), (pas // 2) % SIDE, pas % 2, lax.axis_index("tp")


def here_in_kernel():
    pas = lax.axis_index("pas")
    return (
        lax.div(pas, 2 * SIDE),
        lax.rem(lax.div(pas, 2), SIDE),
        lax.rem(pas, 2),
        lax.axis_index("tp"),
    )


def ring_mod(n):
    return lax.rem(n + 2 * SIDE, SIDE)


def project_kernel(chunks, h_ref, *rest):
    n_out = chunks * SIDE
    pieces = rest[: 2 * SIDE]
    outs = rest[2 * SIDE : 2 * SIDE + n_out]
    weights, result, w_sem, out_sem = rest[2 * SIDE + n_out :]
    step = pl.program_id(0)
    y, z, core, tp = here_in_kernel()
    head_rows = weights.shape[1]
    chunk = h_ref.shape[0] // chunks

    @pl.when(step == 0)
    def _():
        for src in range(2):
            which = core if src == 0 else 1 - core
            first = jnp.where(which == 0, z, y)
            second = jnp.where(which == 0, y, z)
            for jb in range(SIDE):
                for ja in range(SIDE):
                    a = ring_mod(first - ja)
                    b = ring_mod(second - jb)
                    place = ring_mod(jnp.where(which == 0, b, a) - tp)
                    part = jnp.where(which == 0, a, b) * 2 + which
                    pltpu.make_async_copy(
                        pieces[SIDE * src + jb].at[pl.ds(ja * OUT_ROWS, OUT_ROWS)],
                        weights.at[place, pl.ds(pl.multiple_of(part * OUT_ROWS, OUT_ROWS), OUT_ROWS)],
                        w_sem.at[place, part],
                    ).start()

    for n in range(2 * SIDE):
        pltpu.make_async_copy(
            pieces[0].at[pl.ds(0, OUT_ROWS)],
            weights.at[step, pl.ds(n * OUT_ROWS, OUT_ROWS)],
            w_sem.at[step, n],
        ).wait()
    result[step] = lax.dot_general(
        h_ref[...], weights[step], NT, preferred_element_type=F32
    )
    for j in range(SIDE):

        @pl.when(step == j)
        def _():
            for n in range(chunks):
                pltpu.make_async_copy(
                    result.at[j, pl.ds(n * chunk, chunk)],
                    outs[n * SIDE + j],
                    out_sem.at[n * SIDE + j],
                ).start()

    @pl.when(step == SIDE - 1)
    def _():
        for j in range(SIDE):
            for n in range(chunks):
                pltpu.make_async_copy(
                    result.at[j, pl.ds(n * chunk, chunk)],
                    outs[n * SIDE + j],
                    out_sem.at[n * SIDE + j],
                ).wait()


def project(hidden, pieces, chunks):
    rows, depth = hidden.shape
    columns = 2 * SIDE * SIDE * OUT_ROWS
    head = columns // SIDE
    hbm = pl.BlockSpec(memory_space=pl.ANY)
    return pl.pallas_call(
        functools.partial(project_kernel, chunks),
        out_shape=[jax.ShapeDtypeStruct((rows // chunks, head), F32)] * (chunks * SIDE),
        grid=(SIDE,),
        in_specs=[pl.BlockSpec((rows, depth), lambda i: (0, 0))] + [hbm] * (2 * SIDE),
        out_specs=[hbm] * (chunks * SIDE),
        scratch_shapes=[
            pltpu.VMEM((SIDE, head, depth), BF),
            pltpu.VMEM((SIDE, rows, head), F32),
            pltpu.SemaphoreType.DMA((SIDE, 2 * SIDE)),
            pltpu.SemaphoreType.DMA((chunks * SIDE,)),
        ],
        compiler_params=pltpu.CompilerParams(vmem_limit_bytes=40 * 2**20),
        cost_estimate=pl.CostEstimate(
            flops=2 * rows * columns * depth,
            bytes_accessed=2 * rows * depth + 2 * columns * depth + 4 * rows * columns,
            transcendentals=0,
        ),
        name="project",
    )(hidden, *pieces)


def reduce_heads(parts):
    down, up = parts[0][3], parts[1][1]
    for first, second in ((2, 2), (1, 3), (0, 0)):
        down = send_tp(down, 1) + parts[0][first]
        up = send_tp(up, -1) + parts[1][second]
    return jnp.concatenate([down.astype(BF), up.astype(BF)], axis=0)


def weight_kernel(*refs):
    mine, theirs = refs[:5], refs[5:10]
    h_mine, h_theirs = refs[10:12]
    outs = refs[12 : 12 + SIDE]
    left, result = refs[12 + SIDE :]
    y, z, core, tp = here_in_kernel()
    rows = mine[0].shape[1]

    @pl.when(pl.program_id(0) == 0)
    def _():
        for half, refs_of in enumerate((mine, theirs)):
            at = 0
            for piece in refs_of:
                left[pl.ds(at, piece.shape[0]), half * rows : (half + 1) * rows] = piece[...]
                at += piece.shape[0]

    result[...] = jnp.dot(
        left[:, :rows], h_mine[...], preferred_element_type=F32
    ) + jnp.dot(left[:, rows:], h_theirs[...], preferred_element_type=F32)

    def block(ja, jb):
        a_z, a_y = ring_mod(z + ja), ring_mod(y + ja)
        b_z, b_y = ring_mod(z + jb), ring_mod(y + jb)
        y_of = jnp.where(core == 0, b_y, a_y)
        z_of = jnp.where(core == 0, a_z, b_z)
        at = ring_mod(tp - y_of) * SIDE * OUT_ROWS + z_of * OUT_ROWS
        return result[pl.ds(pl.multiple_of(at, OUT_ROWS), OUT_ROWS), :]

    for jb in range(SIDE):
        outs[0][jb] = block(0, jb)
    for ja in range(1, SIDE):
        for jb in range(SIDE):
            outs[ja][jb] = block(ja, jb).astype(BF)


def weight_product(mine, theirs, h_mine, h_theirs):
    rows, depth = h_mine.shape
    tile = 512
    heads_rows = SIDE * SIDE * OUT_ROWS
    whole = pl.BlockSpec(memory_space=pltpu.VMEM)
    out = pl.BlockSpec((SIDE, OUT_ROWS, tile), lambda i: (0, 0, i))
    return pl.pallas_call(
        weight_kernel,
        out_shape=[jax.ShapeDtypeStruct((SIDE, OUT_ROWS, depth), F32)]
        + [jax.ShapeDtypeStruct((SIDE, OUT_ROWS, depth), BF)] * (SIDE - 1),
        grid=(depth // tile,),
        in_specs=[whole] * 10 + [pl.BlockSpec((rows, tile), lambda i: (0, i))] * 2,
        out_specs=[out] * SIDE,
        scratch_shapes=[
            pltpu.VMEM((heads_rows, 2 * rows), BF),
            pltpu.VMEM((heads_rows, tile), F32),
        ],
        compiler_params=pltpu.CompilerParams(vmem_limit_bytes=40 * 2**20),
        cost_estimate=pl.CostEstimate(
            flops=4 * heads_rows * rows * depth,
            bytes_accessed=4 * rows * depth + 4 * heads_rows * depth,
            transcendentals=0,
        ),
        name="weight_product",
    )(*mine, *theirs, h_mine, h_theirs)


def reduce_owners(blocks):
    own, one, two, three = blocks
    left = send_first(one, 1)
    right = send_first(three, -1)
    far = send_first(two, 2)
    total = (own + left.astype(F32)) + (right.astype(F32) + far.astype(F32))
    low = total[1:].astype(BF)
    left = send_second(low[0], 1)
    right = send_second(low[2], -1)
    far = send_second(low[1], 2)
    return (total[0] + left.astype(F32)) + (right.astype(F32) + far.astype(F32))


def attention_kernel(
    n_src, buf_of, row_of, q_ref, do_ref, own_ref, *rest
):
    srcs = rest[:n_src]
    dq_ref, down_ref = rest[n_src : n_src + 2]
    outs = rest[n_src + 2 : 2 * n_src + 2]
    kv, stage, q_st, do_st, p_t, ds_t, in_sem, out_sem = rest[2 * n_src + 2 :]
    step = pl.program_id(0)
    steps = pl.num_programs(0)
    group = q_ref.shape[1] // HD
    retrieved = in_sem.shape[1]
    rows = retrieved * PLEN
    keys = rows + own_ref.shape[0]
    slot = lax.rem(step, 2)
    scaling = HD ** (-0.5)

    def fetch(query, into):
        @pl.loop(0, retrieved)
        def _(j):
            at = query * retrieved + j
            for b in range(n_src):

                @pl.when(buf_of[at] == b)
                def _():
                    pltpu.make_async_copy(
                        srcs[b].at[row_of[at]],
                        kv.at[into, pl.ds(pl.multiple_of(j * PLEN, PLEN), PLEN)],
                        in_sem.at[into, j],
                    ).start()

    @pl.when(step == 0)
    def _():
        fetch(0, 0)

    @pl.when(step + 1 < steps)
    def _():
        fetch(step + 1, 1 - slot)

    for g in range(group):
        q_st[pl.ds(g * HD, HD), :] = q_ref[:, g * HD : (g + 1) * HD]
        do_st[pl.ds(g * HD, HD), :] = do_ref[:, g * HD : (g + 1) * HD]
    kv[slot, pl.ds(rows, keys - rows), :] = own_ref[...]
    for j in range(retrieved):
        pltpu.make_async_copy(
            srcs[0].at[0], kv.at[slot, pl.ds(j * PLEN, PLEN)], in_sem.at[slot, j]
        ).wait()

    k_all = kv[slot, :, :HD]
    v_all = kv[slot, :, HD:]
    width = 2 * HD
    key_at = lax.broadcasted_iota(jnp.int32, (keys - rows, width), 0)
    tok_at = lax.broadcasted_iota(jnp.int32, (keys - rows, width), 1) % HD
    visible = key_at <= tok_at
    for g in range(0, group, 2):
        cols = pl.ds(g * HD, width)
        s = lax.dot_general(k_all, q_st[cols, :], NT, preferred_element_type=F32)
        s = jnp.concatenate(
            [s[:rows], jnp.where(visible, s[rows:], F32(-1e30))], axis=0
        )
        largest = jnp.max(s, axis=0, keepdims=True)
        e = jnp.exp2((s - largest) * F32(scaling * math.log2(math.e)))
        w = e * (1.0 / jnp.sum(e, axis=0, keepdims=True))
        w_low = w.astype(BF)
        p_t[:, cols] = w_low
        gw = lax.dot_general(v_all, do_st[cols, :], NT, preferred_element_type=F32)
        delta = jnp.sum(w_low.astype(F32) * gw, axis=0, keepdims=True)
        ds_t[:, cols] = (w * (gw - delta)).astype(BF)
    d_v = jnp.dot(p_t[...], do_st[...], preferred_element_type=F32)
    d_k = jnp.dot(ds_t[...], q_st[...], preferred_element_type=F32) * F32(scaling)
    dq_t = lax.dot_general(k_all, ds_t[...], TN, preferred_element_type=F32) * F32(scaling)
    for g in range(group):
        dq_ref[:, g * HD : (g + 1) * HD] = dq_t[:, g * HD : (g + 1) * HD].T.astype(BF)

    down_ref[:, :HD] = d_k[rows:].astype(BF)
    down_ref[:, HD:] = d_v[rows:].astype(BF)

    def sent(at_slot, j):
        return pltpu.make_async_copy(
            stage.at[at_slot, pl.ds(j * PLEN, PLEN)], outs[0].at[0], out_sem.at[at_slot, j]
        )

    @pl.when(step >= 2)
    def _():
        for j in range(retrieved):
            sent(slot, j).wait()

    stage[slot, :, :HD] = d_k[:rows].astype(BF)
    stage[slot, :, HD:] = d_v[:rows].astype(BF)

    @pl.loop(0, retrieved)
    def _(j):
        at = step * retrieved + j
        for b in range(n_src):

            @pl.when(buf_of[at] == b)
            def _():
                pltpu.make_async_copy(
                    stage.at[slot, pl.ds(pl.multiple_of(j * PLEN, PLEN), PLEN)],
                    outs[b].at[row_of[at]],
                    out_sem.at[slot, j],
                ).start()

    @pl.when(step == steps - 1)
    def _():
        for j in range(retrieved):
            if steps > 1:
                sent(1 - slot, j).wait()
            sent(slot, j).wait()


def attention(queries, out_grad, query_kv, sources, out_blocks, buf_of, row_of, n_query):
    rows, width = queries.shape
    qlen = rows // n_query
    retrieved = buf_of.shape[0] // n_query
    keys = retrieved * PLEN + qlen
    local = query_kv.shape[1]
    block = lambda w: pl.BlockSpec((qlen, w), lambda i, *_: (i, 0))
    hbm = pl.BlockSpec(memory_space=pl.ANY)
    return pl.pallas_call(
        functools.partial(attention_kernel, len(sources)),
        out_shape=(
            jax.ShapeDtypeStruct((rows, width), BF),
            jax.ShapeDtypeStruct((rows, local), BF),
        )
        + tuple(jax.ShapeDtypeStruct((n, PLEN, local), BF) for n in out_blocks),
        grid_spec=pltpu.PrefetchScalarGridSpec(
            num_scalar_prefetch=2,
            grid=(n_query,),
            in_specs=[block(width), block(width), block(local)] + [hbm] * len(sources),
            out_specs=(block(width), block(local)) + (hbm,) * len(sources),
            scratch_shapes=[
                pltpu.VMEM((2, keys, local), BF),
                pltpu.VMEM((2, retrieved * PLEN, local), BF),
                pltpu.VMEM((width, HD), BF),
                pltpu.VMEM((width, HD), BF),
                pltpu.VMEM((keys, width), BF),
                pltpu.VMEM((keys, width), BF),
                pltpu.SemaphoreType.DMA((2, retrieved)),
                pltpu.SemaphoreType.DMA((2, retrieved)),
            ],
        ),
        compiler_params=pltpu.CompilerParams(vmem_limit_bytes=48 * 2**20),
        cost_estimate=pl.CostEstimate(
            flops=10 * n_query * keys * qlen * width,
            bytes_accessed=8 * rows * width + 4 * n_query * keys * local,
            transcendentals=n_query * keys * width,
        ),
        name="attention",
    )(buf_of, row_of, queries, out_grad, query_kv, *sources)


def pick_kernel(slot_of, *rest):
    ring, outs, sem = rest[:SIDE], rest[SIDE : 2 * SIDE], rest[2 * SIDE]
    n = outs[0].shape[0]
    copies = []
    for k in range(SIDE):
        for m in range(n):
            place = jnp.maximum(slot_of[k * n + m], 0)
            copies.append(
                pltpu.make_async_copy(
                    ring[(m // 2) % SIDE].at[place], outs[k].at[m], sem.at[k * n + m]
                )
            )
    for copy in copies:
        copy.start()
    for copy in copies:
        copy.wait()


def pick(slot_of, ring):
    n = slot_of.shape[0] // SIDE
    hbm = pl.BlockSpec(memory_space=pl.ANY)
    shape = jax.ShapeDtypeStruct((n,) + ring[0].shape[1:], BF)
    return pl.pallas_call(
        pick_kernel,
        out_shape=[shape] * SIDE,
        grid_spec=pltpu.PrefetchScalarGridSpec(
            num_scalar_prefetch=1,
            in_specs=[hbm] * SIDE,
            out_specs=[pl.BlockSpec(memory_space=pltpu.VMEM)] * SIDE,
            scratch_shapes=[pltpu.SemaphoreType.DMA((SIDE * n,))],
        ),
        compiler_params=pltpu.CompilerParams(vmem_limit_bytes=24 * 2**20),
        cost_estimate=pl.CostEstimate(
            flops=0, bytes_accessed=4 * SIDE * n * PLEN * 2 * HD, transcendentals=0
        ),
        name="pick",
    )(slot_of, *ring)


def add_blocks_kernel(slot_of, *rest):
    parts, outs, total = rest[: 2 * SIDE], rest[2 * SIDE : 3 * SIDE], rest[3 * SIDE]
    n = parts[0].shape[0]
    total[...] = jnp.zeros_like(total)
    for p, part in enumerate(parts):

        @pl.loop(0, n)
        def _(m):
            place = slot_of[p * n + m]

            @pl.when(place >= 0)
            def _():
                total[lax.div(m, 2), place] += part[m].astype(F32)

    outs[0][...] = total[0]
    for j in range(1, SIDE):
        outs[j][...] = total[j].astype(BF)


def add_blocks(slot_of, parts, passages):
    shape = (passages,) + parts[0].shape[1:]
    whole = pl.BlockSpec(memory_space=pltpu.VMEM)
    return pl.pallas_call(
        add_blocks_kernel,
        out_shape=[jax.ShapeDtypeStruct(shape, F32)]
        + [jax.ShapeDtypeStruct(shape, BF)] * (SIDE - 1),
        grid_spec=pltpu.PrefetchScalarGridSpec(
            num_scalar_prefetch=1,
            in_specs=[whole] * (2 * SIDE),
            out_specs=[whole] * SIDE,
            scratch_shapes=[pltpu.VMEM((SIDE,) + shape, F32)],
        ),
        compiler_params=pltpu.CompilerParams(vmem_limit_bytes=32 * 2**20),
        cost_estimate=pl.CostEstimate(
            flops=8 * parts[0].size, bytes_accessed=32 * parts[0].size, transcendentals=0
        ),
        name="add_blocks",
    )(slot_of, *parts)


def add_owners_kernel(own_ref, left_ref, far_ref, right_ref, mine_ref, theirs_ref, turned):
    core = lax.rem(lax.axis_index("pas"), 2)
    for p in range(own_ref.shape[0]):
        total = (own_ref[p] + left_ref[p].astype(F32)) + (
            far_ref[p].astype(F32) + right_ref[p].astype(F32)
        )
        turned[:, p * PLEN : (p + 1) * PLEN] = total.T.astype(BF)
    for z in range(SIDE):
        for ref, which in ((mine_ref, core), (theirs_ref, 1 - core)):
            at = pl.multiple_of(z * 2 * OUT_ROWS + which * OUT_ROWS, OUT_ROWS)
            ref[z * OUT_ROWS : (z + 1) * OUT_ROWS, :] = turned[pl.ds(at, OUT_ROWS), :]


def add_owners(parts):
    passages, length, width = parts[0].shape
    half = jax.ShapeDtypeStruct((width // 2, passages * length), BF)
    whole = pl.BlockSpec(memory_space=pltpu.VMEM)
    return pl.pallas_call(
        add_owners_kernel,
        out_shape=(half, half),
        in_specs=[whole] * SIDE,
        out_specs=(whole, whole),
        scratch_shapes=[pltpu.VMEM((width, passages * length), BF)],
        compiler_params=pltpu.CompilerParams(vmem_limit_bytes=32 * 2**20),
        cost_estimate=pl.CostEstimate(
            flops=4 * parts[0].size, bytes_accessed=12 * parts[0].size, transcendentals=0
        ),
        name="add_owners",
    )(*parts)


def requests(source_device, source_slot, owners, capacity):
    flat_device = source_device.reshape(-1)
    flat_slot = source_slot.reshape(-1)
    owner_hits = (flat_device[:, None] == jnp.arange(owners, dtype=jnp.int32)[None, :]).astype(
        jnp.int32
    )
    at = jnp.arange(flat_device.shape[0])
    earlier_same = jnp.logical_and(
        flat_device[:, None] == flat_device[None, :], at[None, :] < at[:, None]
    )
    ranking = jnp.sum(earlier_same.astype(jnp.int32), axis=1)
    slot_hits = (ranking[:, None] == jnp.arange(capacity, dtype=jnp.int32)[None, :]).astype(
        jnp.int32
    )
    placed = owner_hits[:, :, None] * slot_hits[:, None, :]
    table = jnp.sum(placed * (flat_slot + 1)[:, None, None], axis=0) - 1
    return flat_device, ranking, table


def ring_steps(y, z, core, to_y, to_z):
    back_y, back_z = (y - to_y) % SIDE, (z - to_z) % SIDE
    return jnp.where(core == 0, back_z, back_y), jnp.where(core == 0, back_y, back_z)


def own_places(flat_device, ranking, capacity):
    y, z, core, _ = here()
    owner_core = flat_device % 2
    ja, jb = ring_steps(
        y, z, owner_core, flat_device // (2 * SIDE), (flat_device // 2) % SIDE
    )
    block = ja * capacity + ranking
    same = owner_core == core
    return jnp.where(same, jb, SIDE), jnp.where(same, block, jb * SIDE * capacity + block)


def slots_served(tables, owners, capacity):
    y, z, core, _ = here()
    n = jnp.arange(SIDE * 2 * SIDE * capacity, dtype=jnp.int32)
    ja = (n // capacity) % SIDE
    owner = jnp.where(core == 0, device_at(y, (z - ja) % SIDE, 0), device_at((y - ja) % SIDE, z, 0))
    asks = n // (capacity * SIDE)
    at = (asks * owners + owner + core) * capacity + n % capacity
    return tables.reshape(-1)[at]


def per_device(passage_hidden, kv_weight, queries, query_kv, out_grad, source_device, source_slot):
    owners = lax.axis_size("pas")
    rows_local = passage_hidden.shape[0]
    local_width = query_kv.shape[1]
    passages_here = rows_local // PLEN
    queries_here = source_device.shape[0]
    capacity = 2

    flat_device, ranking, table = requests(source_device, source_slot, owners, capacity)
    shards = ring_gather(kv_weight, send_first)
    shards = ring_gather(jnp.concatenate(shards, axis=0), send_second)
    partial = project(passage_hidden, shards + [swap_cores(s) for s in shards], CHUNKS)
    partial, table = lax.optimization_barrier((partial, table))
    pair = jnp.concatenate([table, swap_cores(table)], axis=0)
    tables = jnp.stack([pair] + [send_second(pair, -k) for k in range(1, SIDE)])
    hidden_theirs = swap_cores(passage_hidden)
    buf_of, row_of = own_places(flat_device, ranking, capacity)
    served = slots_served(tables, owners, capacity)

    quarters = [partial[n * SIDE : (n + 1) * SIDE] for n in range(CHUNKS)]
    own = [reduce_heads(quarters[n : n + 2]) for n in range(0, CHUNKS, 2)]
    own = jnp.concatenate(own, axis=0).reshape(passages_here, PLEN, local_width)
    wanted = pick(served, ring_gather(own, send_first))
    got = [wanted[0]] + [send_second(wanted[k], k) for k in range(1, SIDE)]
    half = got[0].shape[0] // 2
    sources = got + [swap_cores(jnp.concatenate([g[half:] for g in got], axis=0))]
    grad_queries, own_grads, *grads = attention(
        queries,
        out_grad,
        query_kv,
        sources,
        [half] * SIDE + [SIDE * half],
        buf_of,
        row_of,
        queries_here,
    )
    mine, theirs = grads[:SIDE], swap_cores(grads[SIDE])
    theirs = [theirs[k * half : (k + 1) * half] for k in range(SIDE)]
    parts = [mine[0], theirs[0]]
    for k in range(1, SIDE):
        parts += [send_second(mine[k], -k), send_second(theirs[k], -k)]
    sums = add_blocks(served, parts, passages_here)
    mine, theirs = add_owners([sums[0]] + [send_first(sums[j], -j) for j in range(1, SIDE)])
    mine_heads = ring_gather_halves(mine, send_tp)
    theirs_heads = ring_gather_halves(swap_cores(theirs), send_tp)
    blocks = weight_product(mine_heads, theirs_heads, passage_hidden, hidden_theirs)
    return grad_queries, own_grads, reduce_owners(blocks)


def solution(mesh):
    in_specs = (
        P("pas", "tp"),
        P("pas", "tp"),
        P("pas", "tp"),
        P("pas", "tp"),
        P("pas", "tp"),
        P("pas", None),
        P("pas", None),
    )
    out_specs = (P("pas", "tp"), P("pas", "tp"), P("pas", "tp"))
    return jax.shard_map(
        per_device, mesh=mesh, in_specs=in_specs, out_specs=out_specs, check_vma=False
    )
```

```python
import functools
import math

import jax
import jax.numpy as jnp
from jax import lax
from jax.experimental import pallas as pl
from jax.experimental.pallas import tpu as pltpu
from jax.sharding import PartitionSpec as P

HD = 128
PLEN = 128
BF = jnp.bfloat16
F32 = jnp.float32
NT = (((1,), (1,)), ((), ()))
TN = (((0,), (0,)), ((), ()))
SIDE = 4
OUT_ROWS = 32


def device_at(y, z, core):
    return (y * SIDE + z) * 2 + core


def ring_pairs(order, k):
    pairs = []
    for y in range(SIDE):
        for z in range(SIDE):
            for core in range(2):
                if (order + core) % 2 == 0:
                    to = device_at(y, (z + k) % SIDE, core)
                else:
                    to = device_at((y + k) % SIDE, z, core)
                pairs.append((device_at(y, z, core), to))
    return pairs


def send_first(x, k):
    return lax.ppermute(x, "pas", ring_pairs(0, k))


def send_second(x, k):
    return lax.ppermute(x, "pas", ring_pairs(1, k))


def send_tp(x, k):
    return lax.ppermute(x, "tp", [(i, (i + k) % SIDE) for i in range(SIDE)])


def swap_cores(x):
    return lax.ppermute(x, "pas", [(i, i ^ 1) for i in range(2 * SIDE * SIDE)])


def ring_gather(x, send):
    left = send(x, 1)
    right = send(x, -1)
    return [x, left, send(x, 2), right]


def ring_gather_halves(x, send):
    half = x.shape[0] // 2
    left = send(x, 1)
    right = send(x, -1)
    return [x, left, send(left[:half], 1), send(right[half:], -1), right]


def here():
    pas = lax.axis_index("pas")
    return pas // (2 * SIDE), (pas // 2) % SIDE, pas % 2, lax.axis_index("tp")


def here_in_kernel():
    pas = lax.axis_index("pas")
    return (
        lax.div(pas, 2 * SIDE),
        lax.rem(lax.div(pas, 2), SIDE),
        lax.rem(pas, 2),
        lax.axis_index("tp"),
    )


def ring_mod(n):
    return lax.rem(n + 2 * SIDE, SIDE)


def project_kernel(h_ref, *rest):
    pieces, outs = rest[: 2 * SIDE], rest[2 * SIDE : 6 * SIDE]
    weights, rows, h_sem = rest[6 * SIDE :]
    step = pl.program_id(0)
    y, z, core, tp = here_in_kernel()
    block = rows.shape[1]
    head = weights.shape[0] // SIDE

    def hidden_copy(i):
        at = pl.ds(pl.multiple_of(i * block, block), block)
        return pltpu.make_async_copy(h_ref.at[at], rows.at[i], h_sem.at[i])

    @pl.when(step == 0)
    def _():
        for i in range(rows.shape[0]):
            hidden_copy(i).start()
        for src in range(2):
            which = core if src == 0 else 1 - core
            first = jnp.where(which == 0, z, y)
            second = jnp.where(which == 0, y, z)
            for jb in range(SIDE):
                for ja in range(SIDE):
                    a = ring_mod(first - ja)
                    b = ring_mod(second - jb)
                    place = ring_mod(jnp.where(which == 0, b, a) - tp)
                    part = (place * SIDE + jnp.where(which == 0, a, b)) * 2 + which
                    weights[pl.ds(pl.multiple_of(part * OUT_ROWS, OUT_ROWS), OUT_ROWS), :] = pieces[
                        SIDE * src + jb
                    ][ja * OUT_ROWS : (ja + 1) * OUT_ROWS, :]

    hidden_copy(step).wait()
    product = lax.dot_general(rows[step], weights[...], NT, preferred_element_type=F32)
    for i in range(4):

        @pl.when(step == i)
        def _():
            for j in range(SIDE):
                outs[i * SIDE + j][...] = product[:, j * head : (j + 1) * head]


def project(hidden, pieces):
    rows, depth = hidden.shape
    block = rows // 4
    columns = 2 * SIDE * SIDE * OUT_ROWS
    head = columns // SIDE
    whole = pl.BlockSpec(memory_space=pltpu.VMEM)
    return pl.pallas_call(
        project_kernel,
        out_shape=[jax.ShapeDtypeStruct((block, head), F32)] * (4 * SIDE),
        grid=(4,),
        in_specs=[pl.BlockSpec(memory_space=pltpu.HBM)] + [whole] * (2 * SIDE),
        out_specs=[whole] * (4 * SIDE),
        scratch_shapes=[
            pltpu.VMEM((columns, depth), BF),
            pltpu.VMEM((4, block, depth), BF),
            pltpu.SemaphoreType.DMA((4,)),
        ],
        compiler_params=pltpu.CompilerParams(vmem_limit_bytes=28 * 2**20),
        cost_estimate=pl.CostEstimate(
            flops=2 * rows * columns * depth,
            bytes_accessed=2 * (rows + columns) * depth + 4 * rows * columns,
            transcendentals=0,
        ),
        name="project",
    )(hidden, *pieces)


def reduce_heads(parts):
    down, up = parts[3], parts[SIDE + 1]
    for first, second in ((2, 2), (1, 3), (0, 0)):
        down = send_tp(down, 1) + parts[first]
        up = send_tp(up, -1) + parts[SIDE + second]
    return jnp.concatenate([down.astype(BF), up.astype(BF)], axis=0)


def weight_kernel(*refs):
    mine, theirs = refs[:5], refs[5:10]
    h_mine, h_theirs = refs[10:12]
    outs = refs[12 : 12 + SIDE]
    left, result = refs[12 + SIDE :]
    y, z, core, tp = here_in_kernel()
    rows = mine[0].shape[1]

    @pl.when(pl.program_id(0) == 0)
    def _():
        for half, refs_of in enumerate((mine, theirs)):
            at = 0
            for piece in refs_of:
                left[pl.ds(at, piece.shape[0]), half * rows : (half + 1) * rows] = piece[...]
                at += piece.shape[0]

    result[...] = jnp.dot(
        left[:, :rows], h_mine[...], preferred_element_type=F32
    ) + jnp.dot(left[:, rows:], h_theirs[...], preferred_element_type=F32)

    def block(ja, jb):
        a_z, a_y = ring_mod(z + ja), ring_mod(y + ja)
        b_z, b_y = ring_mod(z + jb), ring_mod(y + jb)
        y_of = jnp.where(core == 0, b_y, a_y)
        z_of = jnp.where(core == 0, a_z, b_z)
        at = ring_mod(tp - y_of) * SIDE * OUT_ROWS + z_of * OUT_ROWS
        return result[pl.ds(pl.multiple_of(at, OUT_ROWS), OUT_ROWS), :]

    tile = result.shape[1]
    columns = pl.ds(pl.multiple_of(pl.program_id(0) * tile, tile), tile)
    for ja in range(SIDE):
        for jb in range(SIDE):
            outs[ja][jb, :, columns] = block(ja, jb).astype(outs[ja].dtype)


def weight_product(mine, theirs, h_mine, h_theirs):
    rows, depth = h_mine.shape
    tile = 512
    heads_rows = SIDE * SIDE * OUT_ROWS
    whole = pl.BlockSpec(memory_space=pltpu.VMEM)
    return pl.pallas_call(
        weight_kernel,
        out_shape=[jax.ShapeDtypeStruct((SIDE, OUT_ROWS, depth), F32)]
        + [jax.ShapeDtypeStruct((SIDE, OUT_ROWS, depth), BF)] * (SIDE - 1),
        grid=(depth // tile,),
        in_specs=[whole] * 10 + [pl.BlockSpec((rows, tile), lambda i: (0, i))] * 2,
        out_specs=[whole] * SIDE,
        scratch_shapes=[
            pltpu.VMEM((heads_rows, 2 * rows), BF),
            pltpu.VMEM((heads_rows, tile), F32),
        ],
        compiler_params=pltpu.CompilerParams(vmem_limit_bytes=40 * 2**20),
        cost_estimate=pl.CostEstimate(
            flops=4 * heads_rows * rows * depth,
            bytes_accessed=4 * rows * depth + 4 * heads_rows * depth,
            transcendentals=0,
        ),
        name="weight_product",
    )(*mine, *theirs, h_mine, h_theirs)


def reduce_owners(blocks):
    own, one, two, three = blocks
    left = send_first(one, 1)
    right = send_first(three, -1)
    far = send_first(two, 2)
    total = (own + left.astype(F32)) + (right.astype(F32) + far.astype(F32))
    low = total[1:].astype(BF)
    left = send_second(low[0], 1)
    right = send_second(low[2], -1)
    far = send_second(low[1], 2)
    return (total[0] + left.astype(F32)) + (right.astype(F32) + far.astype(F32))


def attention_kernel(
    n_src, n_dst, taken_by, out_buf, out_row, q_ref, do_ref, own_ref, *rest
):
    srcs = rest[:n_src]
    dq_ref, down_ref = rest[n_src : n_src + 2]
    outs = rest[n_src + 2 : n_src + n_dst + 2]
    keys_at, values_at, q_st, do_st, p_t, ds_t = rest[n_src + n_dst + 2 :]
    step = pl.program_id(0)
    group = q_ref.shape[1] // HD
    keys = keys_at.shape[1]
    rows = keys - own_ref.shape[0]
    retrieved = rows // PLEN
    scaling = HD ** (-0.5)

    slots = taken_by.shape[0] // n_src

    @pl.when(step == 0)
    def _():
        for b in range(n_src):
            for m in range(slots):
                to = taken_by[b * slots + m]
                at = m if b < SIDE else slots + m

                @pl.when(to >= 0)
                def _():
                    query = lax.div(to, retrieved)
                    into = pl.ds(pl.multiple_of(lax.rem(to, retrieved) * PLEN, PLEN), PLEN)
                    keys_at[query, into, :] = srcs[b][at, :, :HD]
                    values_at[query, into, :] = srcs[b][at, :, HD:]

    for g in range(group):
        q_st[pl.ds(g * HD, HD), :] = q_ref[:, g * HD : (g + 1) * HD]
        do_st[pl.ds(g * HD, HD), :] = do_ref[:, g * HD : (g + 1) * HD]
    keys_at[step, pl.ds(rows, keys - rows), :] = own_ref[:, :HD]
    values_at[step, pl.ds(rows, keys - rows), :] = own_ref[:, HD:]
    k_all = keys_at[step]
    v_all = values_at[step]
    width = 2 * HD
    key_at = lax.broadcasted_iota(jnp.int32, (keys - rows, width), 0)
    tok_at = lax.broadcasted_iota(jnp.int32, (keys - rows, width), 1) % HD
    visible = key_at <= tok_at
    for g in range(0, group, 2):
        cols = pl.ds(g * HD, width)
        s = lax.dot_general(k_all, q_st[cols, :], NT, preferred_element_type=F32)
        s = jnp.concatenate(
            [s[:rows], jnp.where(visible, s[rows:], F32(-1e30))], axis=0
        )
        largest = jnp.max(s, axis=0, keepdims=True)
        e = jnp.exp2((s - largest) * F32(scaling * math.log2(math.e)))
        w = e * (1.0 / jnp.sum(e, axis=0, keepdims=True))
        w_low = w.astype(BF)
        p_t[:, cols] = w_low
        gw = lax.dot_general(v_all, do_st[cols, :], NT, preferred_element_type=F32)
        delta = jnp.sum(w_low.astype(F32) * gw, axis=0, keepdims=True)
        ds_t[:, cols] = (w * (gw - delta)).astype(BF)
    d_v = jnp.dot(p_t[...], do_st[...], preferred_element_type=F32)
    d_k = jnp.dot(ds_t[...], q_st[...], preferred_element_type=F32) * F32(scaling)
    dq_t = lax.dot_general(k_all, ds_t[...], TN, preferred_element_type=F32) * F32(scaling)
    for g in range(group):
        dq_ref[:, g * HD : (g + 1) * HD] = dq_t[:, g * HD : (g + 1) * HD].T.astype(BF)

    down_ref[:, :HD] = d_k[rows:].astype(BF)
    down_ref[:, HD:] = d_v[rows:].astype(BF)

    for j in range(retrieved):
        at = step * retrieved + j
        part = slice(j * PLEN, (j + 1) * PLEN)
        for b in range(n_dst):

            @pl.when(out_buf[at] == b)
            def _():
                outs[b][out_row[at], :, :HD] = d_k[part].astype(BF)
                outs[b][out_row[at], :, HD:] = d_v[part].astype(BF)


def attention(queries, out_grad, query_kv, sources, out_blocks, places, n_query):
    rows, width = queries.shape
    qlen = rows // n_query
    retrieved = places[1].shape[0] // n_query
    keys = retrieved * PLEN + qlen
    local = query_kv.shape[1]
    block = lambda w: pl.BlockSpec((qlen, w), lambda i, *_: (i, 0))
    whole = pl.BlockSpec(memory_space=pltpu.VMEM)
    return pl.pallas_call(
        functools.partial(attention_kernel, len(sources), len(out_blocks)),
        out_shape=(
            jax.ShapeDtypeStruct((rows, width), BF),
            jax.ShapeDtypeStruct((rows, local), BF),
        )
        + tuple(jax.ShapeDtypeStruct((n, PLEN, local), BF) for n in out_blocks),
        grid_spec=pltpu.PrefetchScalarGridSpec(
            num_scalar_prefetch=3,
            grid=(n_query,),
            in_specs=[block(width), block(width), block(local)] + [whole] * len(sources),
            out_specs=(block(width), block(local)) + (whole,) * len(out_blocks),
            scratch_shapes=[
                pltpu.VMEM((n_query, keys, HD), BF),
                pltpu.VMEM((n_query, keys, HD), BF),
                pltpu.VMEM((width, HD), BF),
                pltpu.VMEM((width, HD), BF),
                pltpu.VMEM((keys, width), BF),
                pltpu.VMEM((keys, width), BF),
            ],
        ),
        compiler_params=pltpu.CompilerParams(vmem_limit_bytes=44 * 2**20),
        cost_estimate=pl.CostEstimate(
            flops=10 * n_query * keys * qlen * width,
            bytes_accessed=8 * rows * width + 4 * n_query * keys * local,
            transcendentals=n_query * keys * width,
        ),
        name="attention",
    )(*places, queries, out_grad, query_kv, *sources)


def pick_kernel(slot_of, *rest):
    ring, outs = rest[:SIDE], rest[SIDE:]
    n = outs[0].shape[0]
    for k in range(SIDE):
        for m in range(n):
            outs[k][m] = ring[(m // 2) % SIDE][jnp.maximum(slot_of[k * n + m], 0)]


def pick(slot_of, ring):
    n = slot_of.shape[0] // SIDE
    whole = pl.BlockSpec(memory_space=pltpu.VMEM)
    shape = jax.ShapeDtypeStruct((n,) + ring[0].shape[1:], BF)
    return pl.pallas_call(
        pick_kernel,
        out_shape=[shape] * SIDE,
        grid_spec=pltpu.PrefetchScalarGridSpec(
            num_scalar_prefetch=1,
            in_specs=[whole] * SIDE,
            out_specs=[whole] * SIDE,
        ),
        compiler_params=pltpu.CompilerParams(vmem_limit_bytes=16 * 2**20),
        cost_estimate=pl.CostEstimate(
            flops=0, bytes_accessed=8 * SIDE * n * PLEN * HD, transcendentals=0
        ),
        name="pick",
    )(slot_of, *ring)


def add_blocks_kernel(slot_of, *rest):
    parts, outs, total = rest[: 2 * SIDE], rest[2 * SIDE : 3 * SIDE], rest[3 * SIDE]
    n = parts[0].shape[0]
    total[...] = jnp.zeros_like(total)
    for p, part in enumerate(parts):

        @pl.loop(0, n)
        def _(m):
            place = slot_of[p * n + m]

            @pl.when(place >= 0)
            def _():
                total[lax.div(m, 2), place] += part[m].astype(F32)

    outs[0][...] = total[0]
    for j in range(1, SIDE):
        outs[j][...] = total[j].astype(BF)


def add_blocks(slot_of, parts, passages):
    shape = (passages,) + parts[0].shape[1:]
    whole = pl.BlockSpec(memory_space=pltpu.VMEM)
    return pl.pallas_call(
        add_blocks_kernel,
        out_shape=[jax.ShapeDtypeStruct(shape, F32)]
        + [jax.ShapeDtypeStruct(shape, BF)] * (SIDE - 1),
        grid_spec=pltpu.PrefetchScalarGridSpec(
            num_scalar_prefetch=1,
            in_specs=[whole] * (2 * SIDE),
            out_specs=[whole] * SIDE,
            scratch_shapes=[pltpu.VMEM((SIDE,) + shape, F32)],
        ),
        compiler_params=pltpu.CompilerParams(vmem_limit_bytes=32 * 2**20),
        cost_estimate=pl.CostEstimate(
            flops=8 * parts[0].size, bytes_accessed=32 * parts[0].size, transcendentals=0
        ),
        name="add_blocks",
    )(slot_of, *parts)


def add_owners_kernel(own_ref, left_ref, far_ref, right_ref, mine_ref, theirs_ref, turned):
    core = lax.rem(lax.axis_index("pas"), 2)
    for p in range(own_ref.shape[0]):
        total = (own_ref[p] + left_ref[p].astype(F32)) + (
            far_ref[p].astype(F32) + right_ref[p].astype(F32)
        )
        turned[:, p * PLEN : (p + 1) * PLEN] = total.T.astype(BF)
    for z in range(SIDE):
        for ref, which in ((mine_ref, core), (theirs_ref, 1 - core)):
            at = pl.multiple_of(z * 2 * OUT_ROWS + which * OUT_ROWS, OUT_ROWS)
            ref[z * OUT_ROWS : (z + 1) * OUT_ROWS, :] = turned[pl.ds(at, OUT_ROWS), :]


def add_owners(parts):
    passages, length, width = parts[0].shape
    half = jax.ShapeDtypeStruct((width // 2, passages * length), BF)
    whole = pl.BlockSpec(memory_space=pltpu.VMEM)
    return pl.pallas_call(
        add_owners_kernel,
        out_shape=(half, half),
        in_specs=[whole] * SIDE,
        out_specs=(whole, whole),
        scratch_shapes=[pltpu.VMEM((width, passages * length), BF)],
        compiler_params=pltpu.CompilerParams(vmem_limit_bytes=32 * 2**20),
        cost_estimate=pl.CostEstimate(
            flops=4 * parts[0].size, bytes_accessed=12 * parts[0].size, transcendentals=0
        ),
        name="add_owners",
    )(*parts)


def requests(source_device, source_slot, owners, capacity):
    flat_device = source_device.reshape(-1)
    flat_slot = source_slot.reshape(-1)
    owner_hits = (flat_device[:, None] == jnp.arange(owners, dtype=jnp.int32)[None, :]).astype(
        jnp.int32
    )
    at = jnp.arange(flat_device.shape[0])
    earlier_same = jnp.logical_and(
        flat_device[:, None] == flat_device[None, :], at[None, :] < at[:, None]
    )
    ranking = jnp.sum(earlier_same.astype(jnp.int32), axis=1)
    slot_hits = (ranking[:, None] == jnp.arange(capacity, dtype=jnp.int32)[None, :]).astype(
        jnp.int32
    )
    placed = owner_hits[:, :, None] * slot_hits[:, None, :]
    table = jnp.sum(placed * (flat_slot + 1)[:, None, None], axis=0) - 1
    return flat_device, ranking, table


def ring_steps(y, z, core, to_y, to_z):
    back_y, back_z = (y - to_y) % SIDE, (z - to_z) % SIDE
    return jnp.where(core == 0, back_z, back_y), jnp.where(core == 0, back_y, back_z)


def own_places(flat_device, ranking, capacity):
    y, z, core, _ = here()
    owner_core = flat_device % 2
    ja, jb = ring_steps(
        y, z, owner_core, flat_device // (2 * SIDE), (flat_device // 2) % SIDE
    )
    n = SIDE * capacity
    block = ja * capacity + ranking
    same = owner_core == core
    named = jnp.where(same, jb, SIDE + jb) * n + block
    at = jnp.arange(2 * SIDE * n, dtype=jnp.int32)[:, None]
    request = jnp.arange(named.shape[0], dtype=jnp.int32)[None, :]
    taken_by = jnp.max(jnp.where(named[None, :] == at, request, -1), axis=1)
    return taken_by, jnp.where(same, jb, SIDE), jnp.where(same, block, jb * n + block)


def slots_served(tables, owners, capacity):
    y, z, core, _ = here()
    n = jnp.arange(SIDE * 2 * SIDE * capacity, dtype=jnp.int32)
    ja = (n // capacity) % SIDE
    owner = jnp.where(core == 0, device_at(y, (z - ja) % SIDE, 0), device_at((y - ja) % SIDE, z, 0))
    asks = n // (capacity * SIDE)
    at = (asks * owners + owner + core) * capacity + n % capacity
    return tables.reshape(-1)[at]


def per_device(passage_hidden, kv_weight, queries, query_kv, out_grad, source_device, source_slot):
    owners = lax.axis_size("pas")
    rows_local = passage_hidden.shape[0]
    local_width = query_kv.shape[1]
    passages_here = rows_local // PLEN
    queries_here = source_device.shape[0]
    capacity = 2

    flat_device, ranking, table = requests(source_device, source_slot, owners, capacity)
    shards = jnp.concatenate(ring_gather(kv_weight, send_first), axis=0)
    shards, table = lax.optimization_barrier((shards, table))
    weights = ring_gather(shards, send_second)
    weights = weights + [swap_cores(w) for w in weights]
    pair = jnp.concatenate([table, swap_cores(table)], axis=0)
    tables = jnp.stack([pair] + [send_second(pair, -k) for k in range(1, SIDE)])
    places = own_places(flat_device, ranking, capacity)
    served = slots_served(tables, owners, capacity)

    parts = project(passage_hidden, weights)
    own = [reduce_heads(parts[n : n + 2 * SIDE]) for n in (0, 2 * SIDE)]
    own = jnp.concatenate(own, axis=0).reshape(passages_here, PLEN, local_width)
    wanted = pick(served, ring_gather(own, send_first))
    got = [wanted[0]] + [send_second(wanted[k], k) for k in (1, 2, 3)]
    hidden_theirs = swap_cores(passage_hidden)
    half = SIDE * capacity
    grad_queries, own_grads, *grads = attention(
        queries,
        out_grad,
        query_kv,
        got + [swap_cores(g) for g in got],
        [half] * SIDE + [SIDE * half],
        places,
        queries_here,
    )
    mine, theirs = grads[:SIDE], swap_cores(grads[SIDE])
    theirs = [theirs[k * half : (k + 1) * half] for k in range(SIDE)]
    parts = [mine[0], theirs[0]]
    for k in range(1, SIDE):
        parts += [send_second(mine[k], -k), send_second(theirs[k], -k)]
    sums = add_blocks(served, parts, passages_here)
    mine, theirs = add_owners([sums[0]] + [send_first(sums[j], -j) for j in range(1, SIDE)])
    mine_heads = ring_gather_halves(mine, send_tp)
    theirs_heads = ring_gather_halves(swap_cores(theirs), send_tp)
    blocks = weight_product(mine_heads, theirs_heads, passage_hidden, hidden_theirs)
    return grad_queries, own_grads, reduce_owners(blocks)


def solution(mesh):
    in_specs = (
        P("pas", "tp"),
        P("pas", "tp"),
        P("pas", "tp"),
        P("pas", "tp"),
        P("pas", "tp"),
        P("pas", None),
        P("pas", None),
    )
    out_specs = (P("pas", "tp"), P("pas", "tp"), P("pas", "tp"))
    return jax.shard_map(
        per_device, mesh=mesh, in_specs=in_specs, out_specs=out_specs, check_vma=False
    )
```

```python
import functools
import math

import jax
import jax.numpy as jnp
from jax import lax
from jax.experimental import pallas as pl
from jax.experimental.pallas import tpu as pltpu
from jax.sharding import PartitionSpec as P

HD = 128
PLEN = 128
BF = jnp.bfloat16
F32 = jnp.float32
NT = (((1,), (1,)), ((), ()))
TN = (((0,), (0,)), ((), ()))
SIDE = 4
OUT_ROWS = 32


def device_at(y, z, core):
    return (y * SIDE + z) * 2 + core


def ring_pairs(order, k):
    pairs = []
    for y in range(SIDE):
        for z in range(SIDE):
            for core in range(2):
                if (order + core) % 2 == 0:
                    to = device_at(y, (z + k) % SIDE, core)
                else:
                    to = device_at((y + k) % SIDE, z, core)
                pairs.append((device_at(y, z, core), to))
    return pairs


def send_first(x, k):
    return lax.ppermute(x, "pas", ring_pairs(0, k))


def send_second(x, k):
    return lax.ppermute(x, "pas", ring_pairs(1, k))


def send_tp(x, k):
    return lax.ppermute(x, "tp", [(i, (i + k) % SIDE) for i in range(SIDE)])


def swap_cores(x):
    return lax.ppermute(x, "pas", [(i, i ^ 1) for i in range(2 * SIDE * SIDE)])


def ring_gather(x, send):
    left = send(x, 1)
    right = send(x, -1)
    return [x, left, send(x, 2), right]


def ring_gather_halves(x, send):
    half = x.shape[0] // 2
    left = send(x, 1)
    right = send(x, -1)
    return [x, left, send(left[:half], 1), send(right[half:], -1), right]


def here():
    pas = lax.axis_index("pas")
    return pas // (2 * SIDE), (pas // 2) % SIDE, pas % 2, lax.axis_index("tp")


def here_in_kernel():
    pas = lax.axis_index("pas")
    return (
        lax.div(pas, 2 * SIDE),
        lax.rem(lax.div(pas, 2), SIDE),
        lax.rem(pas, 2),
        lax.axis_index("tp"),
    )


def ring_mod(n):
    return lax.rem(n + 2 * SIDE, SIDE)


def gather_rows(pieces, weights):
    y, z, core, tp = here_in_kernel()
    for src in range(2):
        which = core if src == 0 else 1 - core
        first = jnp.where(which == 0, z, y)
        second = jnp.where(which == 0, y, z)
        for jb in range(SIDE):
            for ja in range(SIDE):
                a = ring_mod(first - ja)
                b = ring_mod(second - jb)
                place = ring_mod(jnp.where(which == 0, b, a) - tp)
                part = (place * SIDE + jnp.where(which == 0, a, b)) * 2 + which
                weights[pl.ds(pl.multiple_of(part * OUT_ROWS, OUT_ROWS), OUT_ROWS), :] = pieces[
                    SIDE * src + jb
                ][ja * OUT_ROWS : (ja + 1) * OUT_ROWS, :]


def project_kernel(first, n_in, h_ref, *rest):
    outs = rest[n_in : n_in + 2 * SIDE]
    step = pl.program_id(0)
    if first == 0:
        weights = rest[n_in + 2 * SIDE]

        @pl.when(step == 0)
        def _():
            gather_rows(rest[:n_in], weights)

    else:
        weights = rest[0]
    block, head = outs[0].shape
    at = pl.ds(pl.multiple_of((first + step) * block, block), block)
    product = lax.dot_general(h_ref[at, :], weights[...], NT, preferred_element_type=F32)
    for i in range(2):

        @pl.when(step == i)
        def _():
            for j in range(SIDE):
                outs[i * SIDE + j][...] = product[:, j * head : (j + 1) * head]


def project(hidden, pieces, first):
    rows, depth = hidden.shape
    block = rows // 4
    columns = 2 * SIDE * SIDE * OUT_ROWS
    head = columns // SIDE
    whole = pl.BlockSpec(memory_space=pltpu.VMEM)
    outs = [jax.ShapeDtypeStruct((block, head), F32)] * (2 * SIDE)
    if first == 0:
        outs += [jax.ShapeDtypeStruct((columns, depth), BF)]
    return pl.pallas_call(
        functools.partial(project_kernel, first, len(pieces)),
        out_shape=outs,
        grid=(2,),
        in_specs=[whole] * (1 + len(pieces)),
        out_specs=[whole] * len(outs),
        compiler_params=pltpu.CompilerParams(vmem_limit_bytes=20 * 2**20),
        cost_estimate=pl.CostEstimate(
            flops=rows * columns * depth,
            bytes_accessed=(rows + 2 * columns) * depth + 2 * rows * columns,
            transcendentals=0,
        ),
        name="project",
    )(hidden, *pieces)


def reduce_heads(parts):
    down, up = parts[3], parts[SIDE + 1]
    for first, second in ((2, 2), (1, 3), (0, 0)):
        down = send_tp(down, 1) + parts[first]
        up = send_tp(up, -1) + parts[SIDE + second]
    return jnp.concatenate([down.astype(BF), up.astype(BF)], axis=0)


def weight_kernel(*refs):
    mine, theirs = refs[:5], refs[5:10]
    h_mine, h_theirs = refs[10:12]
    outs = refs[12 : 12 + SIDE]
    left, result = refs[12 + SIDE :]
    y, z, core, tp = here_in_kernel()
    rows = mine[0].shape[1]

    @pl.when(pl.program_id(0) == 0)
    def _():
        for half, refs_of in enumerate((mine, theirs)):
            at = 0
            for piece in refs_of:
                left[pl.ds(at, piece.shape[0]), half * rows : (half + 1) * rows] = piece[...]
                at += piece.shape[0]

    result[...] = jnp.dot(
        left[:, :rows], h_mine[...], preferred_element_type=F32
    ) + jnp.dot(left[:, rows:], h_theirs[...], preferred_element_type=F32)

    def block(ja, jb):
        a_z, a_y = ring_mod(z + ja), ring_mod(y + ja)
        b_z, b_y = ring_mod(z + jb), ring_mod(y + jb)
        y_of = jnp.where(core == 0, b_y, a_y)
        z_of = jnp.where(core == 0, a_z, b_z)
        at = ring_mod(tp - y_of) * SIDE * OUT_ROWS + z_of * OUT_ROWS
        return result[pl.ds(pl.multiple_of(at, OUT_ROWS), OUT_ROWS), :]

    tile = result.shape[1]
    columns = pl.ds(pl.multiple_of(pl.program_id(0) * tile, tile), tile)
    for ja in range(SIDE):
        for jb in range(SIDE):
            outs[ja][jb, :, columns] = block(ja, jb).astype(outs[ja].dtype)


def weight_product(mine, theirs, h_mine, h_theirs):
    rows, depth = h_mine.shape
    tile = 512
    heads_rows = SIDE * SIDE * OUT_ROWS
    whole = pl.BlockSpec(memory_space=pltpu.VMEM)
    return pl.pallas_call(
        weight_kernel,
        out_shape=[jax.ShapeDtypeStruct((SIDE, OUT_ROWS, depth), F32)]
        + [jax.ShapeDtypeStruct((SIDE, OUT_ROWS, depth), BF)] * (SIDE - 1),
        grid=(depth // tile,),
        in_specs=[whole] * 10 + [pl.BlockSpec((rows, tile), lambda i: (0, i))] * 2,
        out_specs=[whole] * SIDE,
        scratch_shapes=[
            pltpu.VMEM((heads_rows, 2 * rows), BF),
            pltpu.VMEM((heads_rows, tile), F32),
        ],
        compiler_params=pltpu.CompilerParams(vmem_limit_bytes=40 * 2**20),
        cost_estimate=pl.CostEstimate(
            flops=4 * heads_rows * rows * depth,
            bytes_accessed=4 * rows * depth + 4 * heads_rows * depth,
            transcendentals=0,
        ),
        name="weight_product",
    )(*mine, *theirs, h_mine, h_theirs)


def reduce_owners(blocks):
    own, one, two, three = blocks
    left = send_first(one, 1)
    right = send_first(three, -1)
    far = send_first(two, 2)
    total = (own + left.astype(F32)) + (right.astype(F32) + far.astype(F32))
    low = total[1:].astype(BF)
    left = send_second(low[0], 1)
    right = send_second(low[2], -1)
    far = send_second(low[1], 2)
    return (total[0] + left.astype(F32)) + (right.astype(F32) + far.astype(F32))


def attention_kernel(
    n_src, n_dst, taken_by, out_buf, out_row, q_ref, do_ref, own_ref, *rest
):
    srcs = rest[:n_src]
    dq_ref, down_ref = rest[n_src : n_src + 2]
    outs = rest[n_src + 2 : n_src + n_dst + 2]
    keys_at, values_at, q_st, do_st, p_t, ds_t = rest[n_src + n_dst + 2 :]
    step = pl.program_id(0)
    group = q_ref.shape[1] // HD
    keys = keys_at.shape[1]
    rows = keys - own_ref.shape[0]
    retrieved = rows // PLEN
    scaling = HD ** (-0.5)

    slots = taken_by.shape[0] // n_src

    @pl.when(step == 0)
    def _():
        for b in range(n_src):
            for m in range(slots):
                to = taken_by[b * slots + m]

                @pl.when(to >= 0)
                def _():
                    query = lax.div(to, retrieved)
                    into = pl.ds(pl.multiple_of(lax.rem(to, retrieved) * PLEN, PLEN), PLEN)
                    keys_at[query, into, :] = srcs[b][m, :, :HD]
                    values_at[query, into, :] = srcs[b][m, :, HD:]

    for g in range(group):
        q_st[pl.ds(g * HD, HD), :] = q_ref[:, g * HD : (g + 1) * HD]
        do_st[pl.ds(g * HD, HD), :] = do_ref[:, g * HD : (g + 1) * HD]
    keys_at[step, pl.ds(rows, keys - rows), :] = own_ref[:, :HD]
    values_at[step, pl.ds(rows, keys - rows), :] = own_ref[:, HD:]
    k_all = keys_at[step]
    v_all = values_at[step]
    width = 2 * HD
    key_at = lax.broadcasted_iota(jnp.int32, (keys - rows, width), 0)
    tok_at = lax.broadcasted_iota(jnp.int32, (keys - rows, width), 1) % HD
    visible = key_at <= tok_at
    for g in range(0, group, 2):
        cols = pl.ds(g * HD, width)
        s = lax.dot_general(k_all, q_st[cols, :], NT, preferred_element_type=F32)
        s = jnp.concatenate(
            [s[:rows], jnp.where(visible, s[rows:], F32(-1e30))], axis=0
        )
        largest = jnp.max(s, axis=0, keepdims=True)
        e = jnp.exp2((s - largest) * F32(scaling * math.log2(math.e)))
        w = e * (1.0 / jnp.sum(e, axis=0, keepdims=True))
        w_low = w.astype(BF)
        p_t[:, cols] = w_low
        gw = lax.dot_general(v_all, do_st[cols, :], NT, preferred_element_type=F32)
        delta = jnp.sum(w_low.astype(F32) * gw, axis=0, keepdims=True)
        ds_t[:, cols] = (w * (gw - delta)).astype(BF)
    d_v = jnp.dot(p_t[...], do_st[...], preferred_element_type=F32)
    d_k = jnp.dot(ds_t[...], q_st[...], preferred_element_type=F32) * F32(scaling)
    d_q = lax.dot_general(ds_t[...], k_all, TN, preferred_element_type=F32) * F32(scaling)
    for g in range(group):
        dq_ref[:, g * HD : (g + 1) * HD] = d_q[g * HD : (g + 1) * HD].astype(BF)

    down_ref[:, :HD] = d_k[rows:].astype(BF)
    down_ref[:, HD:] = d_v[rows:].astype(BF)

    for j in range(retrieved):
        at = step * retrieved + j
        part = slice(j * PLEN, (j + 1) * PLEN)
        for b in range(n_dst):

            @pl.when(out_buf[at] == b)
            def _():
                outs[b][out_row[at], :, :HD] = d_k[part].astype(BF)
                outs[b][out_row[at], :, HD:] = d_v[part].astype(BF)


def attention(queries, out_grad, query_kv, sources, out_blocks, places, n_query):
    rows, width = queries.shape
    qlen = rows // n_query
    retrieved = places[1].shape[0] // n_query
    keys = retrieved * PLEN + qlen
    local = query_kv.shape[1]
    block = lambda w: pl.BlockSpec((qlen, w), lambda i, *_: (i, 0))
    whole = pl.BlockSpec(memory_space=pltpu.VMEM)
    return pl.pallas_call(
        functools.partial(attention_kernel, len(sources), len(out_blocks)),
        out_shape=(
            jax.ShapeDtypeStruct((rows, width), BF),
            jax.ShapeDtypeStruct((rows, local), BF),
        )
        + tuple(jax.ShapeDtypeStruct((n, PLEN, local), BF) for n in out_blocks),
        grid_spec=pltpu.PrefetchScalarGridSpec(
            num_scalar_prefetch=3,
            grid=(n_query,),
            in_specs=[block(width), block(width), block(local)] + [whole] * len(sources),
            out_specs=(block(width), block(local)) + (whole,) * len(out_blocks),
            scratch_shapes=[
                pltpu.VMEM((n_query, keys, HD), BF),
                pltpu.VMEM((n_query, keys, HD), BF),
                pltpu.VMEM((width, HD), BF),
                pltpu.VMEM((width, HD), BF),
                pltpu.VMEM((keys, width), BF),
                pltpu.VMEM((keys, width), BF),
            ],
        ),
        compiler_params=pltpu.CompilerParams(vmem_limit_bytes=44 * 2**20),
        cost_estimate=pl.CostEstimate(
            flops=10 * n_query * keys * qlen * width,
            bytes_accessed=8 * rows * width + 4 * n_query * keys * local,
            transcendentals=n_query * keys * width,
        ),
        name="attention",
    )(*places, queries, out_grad, query_kv, *sources)


def pick_kernel(slot_of, *rest):
    ring, outs = rest[:SIDE], rest[SIDE:]
    n = outs[0].shape[0]
    for k in range(2 * SIDE):
        for m in range(n):
            outs[k][m] = ring[m // 2][jnp.maximum(slot_of[k * n + m], 0)]


def pick(slot_of, ring):
    n = slot_of.shape[0] // (2 * SIDE)
    whole = pl.BlockSpec(memory_space=pltpu.VMEM)
    shape = jax.ShapeDtypeStruct((n,) + ring[0].shape[1:], BF)
    return pl.pallas_call(
        pick_kernel,
        out_shape=[shape] * (2 * SIDE),
        grid_spec=pltpu.PrefetchScalarGridSpec(
            num_scalar_prefetch=1,
            in_specs=[whole] * SIDE,
            out_specs=[whole] * (2 * SIDE),
        ),
        compiler_params=pltpu.CompilerParams(vmem_limit_bytes=16 * 2**20),
        cost_estimate=pl.CostEstimate(
            flops=0, bytes_accessed=16 * SIDE * n * PLEN * HD, transcendentals=0
        ),
        name="pick",
    )(slot_of, *ring)


def add_blocks_kernel(slot_of, *rest):
    parts, outs, total = rest[: 2 * SIDE], rest[2 * SIDE : 3 * SIDE], rest[3 * SIDE]
    n = parts[0].shape[0]
    total[...] = jnp.zeros_like(total)
    for p, part in enumerate(parts):

        @pl.loop(0, n)
        def _(m):
            place = slot_of[p * n + m]

            @pl.when(place >= 0)
            def _():
                total[lax.div(m, 2), place] += part[m].astype(F32)

    outs[0][...] = total[0]
    for j in range(1, SIDE):
        outs[j][...] = total[j].astype(BF)


def add_blocks(slot_of, parts, passages):
    shape = (passages,) + parts[0].shape[1:]
    whole = pl.BlockSpec(memory_space=pltpu.VMEM)
    return pl.pallas_call(
        add_blocks_kernel,
        out_shape=[jax.ShapeDtypeStruct(shape, F32)]
        + [jax.ShapeDtypeStruct(shape, BF)] * (SIDE - 1),
        grid_spec=pltpu.PrefetchScalarGridSpec(
            num_scalar_prefetch=1,
            in_specs=[whole] * (2 * SIDE),
            out_specs=[whole] * SIDE,
            scratch_shapes=[pltpu.VMEM((SIDE,) + shape, F32)],
        ),
        compiler_params=pltpu.CompilerParams(vmem_limit_bytes=32 * 2**20),
        cost_estimate=pl.CostEstimate(
            flops=8 * parts[0].size, bytes_accessed=32 * parts[0].size, transcendentals=0
        ),
        name="add_blocks",
    )(slot_of, *parts)


def add_owners_kernel(own_ref, left_ref, far_ref, right_ref, mine_ref, theirs_ref, turned):
    core = lax.rem(lax.axis_index("pas"), 2)
    for p in range(own_ref.shape[0]):
        total = (own_ref[p] + left_ref[p].astype(F32)) + (
            far_ref[p].astype(F32) + right_ref[p].astype(F32)
        )
        turned[:, p * PLEN : (p + 1) * PLEN] = total.T.astype(BF)
    for z in range(SIDE):
        for ref, which in ((mine_ref, core), (theirs_ref, 1 - core)):
            at = pl.multiple_of(z * 2 * OUT_ROWS + which * OUT_ROWS, OUT_ROWS)
            ref[z * OUT_ROWS : (z + 1) * OUT_ROWS, :] = turned[pl.ds(at, OUT_ROWS), :]


def add_owners(parts):
    passages, length, width = parts[0].shape
    half = jax.ShapeDtypeStruct((width // 2, passages * length), BF)
    whole = pl.BlockSpec(memory_space=pltpu.VMEM)
    return pl.pallas_call(
        add_owners_kernel,
        out_shape=(half, half),
        in_specs=[whole] * SIDE,
        out_specs=(whole, whole),
        scratch_shapes=[pltpu.VMEM((width, passages * length), BF)],
        compiler_params=pltpu.CompilerParams(vmem_limit_bytes=32 * 2**20),
        cost_estimate=pl.CostEstimate(
            flops=4 * parts[0].size, bytes_accessed=12 * parts[0].size, transcendentals=0
        ),
        name="add_owners",
    )(*parts)


def requests(source_device, source_slot, owners, capacity):
    flat_device = source_device.reshape(-1)
    flat_slot = source_slot.reshape(-1)
    owner_hits = (flat_device[:, None] == jnp.arange(owners, dtype=jnp.int32)[None, :]).astype(
        jnp.int32
    )
    at = jnp.arange(flat_device.shape[0])
    earlier_same = jnp.logical_and(
        flat_device[:, None] == flat_device[None, :], at[None, :] < at[:, None]
    )
    ranking = jnp.sum(earlier_same.astype(jnp.int32), axis=1)
    slot_hits = (ranking[:, None] == jnp.arange(capacity, dtype=jnp.int32)[None, :]).astype(
        jnp.int32
    )
    placed = owner_hits[:, :, None] * slot_hits[:, None, :]
    table = jnp.sum(placed * (flat_slot + 1)[:, None, None], axis=0) - 1
    return flat_device, ranking, table


def ring_steps(y, z, core, to_y, to_z):
    back_y, back_z = (y - to_y) % SIDE, (z - to_z) % SIDE
    return jnp.where(core == 0, back_z, back_y), jnp.where(core == 0, back_y, back_z)


def own_places(flat_device, ranking, capacity):
    y, z, core, _ = here()
    owner_core = flat_device % 2
    ja, jb = ring_steps(
        y, z, owner_core, flat_device // (2 * SIDE), (flat_device // 2) % SIDE
    )
    n = SIDE * capacity
    block = ja * capacity + ranking
    same = owner_core == core
    named = jnp.where(same, jb, SIDE + jb) * n + block
    at = jnp.arange(2 * SIDE * n, dtype=jnp.int32)[:, None]
    request = jnp.arange(named.shape[0], dtype=jnp.int32)[None, :]
    taken_by = jnp.max(jnp.where(named[None, :] == at, request, -1), axis=1)
    return taken_by, jnp.where(same, jb, SIDE), jnp.where(same, block, jb * n + block)


def slots_served(tables, owners, capacity):
    y, z, core, _ = here()
    n = jnp.arange(SIDE * 2 * SIDE * capacity, dtype=jnp.int32)
    ja = (n // capacity) % SIDE
    owner = jnp.where(core == 0, device_at(y, (z - ja) % SIDE, 0), device_at((y - ja) % SIDE, z, 0))
    asks = n // (capacity * SIDE)
    at = (asks * owners + owner + core) * capacity + n % capacity
    return tables.reshape(-1)[at]


def per_device(passage_hidden, kv_weight, queries, query_kv, out_grad, source_device, source_slot):
    owners = lax.axis_size("pas")
    rows_local = passage_hidden.shape[0]
    local_width = query_kv.shape[1]
    passages_here = rows_local // PLEN
    queries_here = source_device.shape[0]
    capacity = 2

    flat_device, ranking, table = requests(source_device, source_slot, owners, capacity)
    shards = jnp.concatenate(ring_gather(kv_weight, send_first), axis=0)
    shards, table = lax.optimization_barrier((shards, table))
    weights = ring_gather(shards, send_second)
    weights = weights + [swap_cores(w) for w in weights]
    pair = jnp.concatenate([table, swap_cores(table)], axis=0)
    tables = jnp.stack([pair] + [send_second(pair, -k) for k in range(1, SIDE)])
    places = own_places(flat_device, ranking, capacity)
    served = slots_served(tables, owners, capacity)

    *lower, weights = project(passage_hidden, weights, 0)
    upper = project(passage_hidden, [weights], 2)
    own = jnp.concatenate([reduce_heads(lower), reduce_heads(upper)], axis=0)
    own = own.reshape(passages_here, PLEN, local_width)
    wanted = pick(served, ring_gather(own, send_first))
    same, other = wanted[::2], wanted[1::2]
    other = [other[0]] + [send_second(other[k], k) for k in (1, 3, 2)]
    same = [same[0]] + [send_second(same[k], k) for k in (1, 3, 2)]
    for blocks in (other, same):
        blocks[2], blocks[3] = blocks[3], blocks[2]
    hidden_theirs = swap_cores(passage_hidden)
    half = SIDE * capacity
    grad_queries, own_grads, *grads = attention(
        queries,
        out_grad,
        query_kv,
        same + [swap_cores(g) for g in other],
        [half] * SIDE + [SIDE * half],
        places,
        queries_here,
    )
    mine, theirs = grads[:SIDE], swap_cores(grads[SIDE])
    theirs = [theirs[k * half : (k + 1) * half] for k in range(SIDE)]
    parts = [mine[0], theirs[0]]
    for k in range(1, SIDE):
        parts += [send_second(mine[k], -k), send_second(theirs[k], -k)]
    sums = add_blocks(served, parts, passages_here)
    mine, theirs = add_owners([sums[0]] + [send_first(sums[j], -j) for j in range(1, SIDE)])
    mine_heads = ring_gather_halves(mine, send_tp)
    theirs_heads = ring_gather_halves(swap_cores(theirs), send_tp)
    blocks = weight_product(mine_heads, theirs_heads, passage_hidden, hidden_theirs)
    return grad_queries, own_grads, reduce_owners(blocks)


def solution(mesh):
    in_specs = (
        P("pas", "tp"),
        P("pas", "tp"),
        P("pas", "tp"),
        P("pas", "tp"),
        P("pas", "tp"),
        P("pas", None),
        P("pas", None),
    )
    out_specs = (P("pas", "tp"), P("pas", "tp"), P("pas", "tp"))
    return jax.shard_map(
        per_device, mesh=mesh, in_specs=in_specs, out_specs=out_specs, check_vma=False
    )
```

```python
import functools
import math

import jax
import jax.numpy as jnp
from jax import lax
from jax.experimental import pallas as pl
from jax.experimental.pallas import tpu as pltpu
from jax.sharding import PartitionSpec as P

HD = 128
PLEN = 128
BF = jnp.bfloat16
F32 = jnp.float32
NT = (((1,), (1,)), ((), ()))
TN = (((0,), (0,)), ((), ()))
SIDE = 4
SENT_FIRST = (3, 1)
OUT_ROWS = 32


def device_at(y, z, core):
    return (y * SIDE + z) * 2 + core


def ring_pairs(order, k):
    pairs = []
    for y in range(SIDE):
        for z in range(SIDE):
            for core in range(2):
                if (order + core) % 2 == 0:
                    to = device_at(y, (z + k) % SIDE, core)
                else:
                    to = device_at((y + k) % SIDE, z, core)
                pairs.append((device_at(y, z, core), to))
    return pairs


def send_first(x, k):
    return lax.ppermute(x, "pas", ring_pairs(0, k))


def send_second(x, k):
    return lax.ppermute(x, "pas", ring_pairs(1, k))


def send_tp(x, k):
    return lax.ppermute(x, "tp", [(i, (i + k) % SIDE) for i in range(SIDE)])


def swap_cores(x):
    return lax.ppermute(x, "pas", [(i, i ^ 1) for i in range(2 * SIDE * SIDE)])


def ring_gather(x, send):
    left = send(x, 1)
    right = send(x, -1)
    return [x, left, send(x, 2), right]


def ring_gather_halves(x, send):
    half = x.shape[0] // 2
    left = send(x, 1)
    right = send(x, -1)
    return [x, left, send(left[:half], 1), send(right[half:], -1), right]


def here():
    pas = lax.axis_index("pas")
    return pas // (2 * SIDE), (pas // 2) % SIDE, pas % 2, lax.axis_index("tp")


def here_in_kernel():
    pas = lax.axis_index("pas")
    return (
        lax.div(pas, 2 * SIDE),
        lax.rem(lax.div(pas, 2), SIDE),
        lax.rem(pas, 2),
        lax.axis_index("tp"),
    )


def ring_mod(n):
    return lax.rem(n + 2 * SIDE, SIDE)


def pack(keys, values, out_ref):
    high = keys.astype(BF)
    out_ref[:, :HD] = high
    out_ref[:, HD : 2 * HD] = (keys - high.astype(F32)).astype(BF)
    out_ref[:, 2 * HD :] = values.astype(BF)


def gather_rows(pieces, weights):
    y, z, core, tp = here_in_kernel()
    for src in range(2):
        which = core if src == 0 else 1 - core
        first = jnp.where(which == 0, z, y)
        second = jnp.where(which == 0, y, z)
        for jb in range(SIDE):
            for ja in range(SIDE):
                a = ring_mod(first - ja)
                b = ring_mod(second - jb)
                place = ring_mod(jnp.where(which == 0, b, a) - tp)
                part = (place * SIDE + jnp.where(which == 0, a, b)) * 2 + which
                weights[pl.ds(pl.multiple_of(part * OUT_ROWS, OUT_ROWS), OUT_ROWS), :] = pieces[
                    SIDE * src + jb
                ][ja * OUT_ROWS : (ja + 1) * OUT_ROWS, :]


def project_kernel(first, n_in, h_ref, *rest):
    outs = rest[n_in : n_in + 2 * SIDE]
    step = pl.program_id(0)
    if first == 0:
        weights = rest[n_in + 2 * SIDE]

        @pl.when(step == 0)
        def _():
            gather_rows(rest[:n_in], weights)

    else:
        weights = rest[0]
    block, head = outs[0].shape
    at = pl.ds(pl.multiple_of((first + step) * block, block), block)
    product = lax.dot_general(h_ref[at, :], weights[...], NT, preferred_element_type=F32)
    for i in range(2):

        @pl.when(step == i)
        def _():
            for j in range(SIDE):
                part = product[:, j * head : (j + 1) * head]
                if j == SENT_FIRST[i]:
                    pack(part[:, :HD], part[:, HD:], outs[i * SIDE + j])
                else:
                    outs[i * SIDE + j][...] = part


def project(hidden, pieces, first):
    rows, depth = hidden.shape
    block = rows // 4
    columns = 2 * SIDE * SIDE * OUT_ROWS
    head = columns // SIDE
    whole = pl.BlockSpec(memory_space=pltpu.VMEM)
    outs = [jax.ShapeDtypeStruct((block, head), F32)] * (2 * SIDE)
    for i in range(2):
        outs[i * SIDE + SENT_FIRST[i]] = jax.ShapeDtypeStruct((block, 3 * HD), BF)
    if first == 0:
        outs += [jax.ShapeDtypeStruct((columns, depth), BF)]
    return pl.pallas_call(
        functools.partial(project_kernel, first, len(pieces)),
        out_shape=outs,
        grid=(2,),
        in_specs=[whole] * (1 + len(pieces)),
        out_specs=[whole] * len(outs),
        compiler_params=pltpu.CompilerParams(vmem_limit_bytes=10 * 2**20),
        cost_estimate=pl.CostEstimate(
            flops=rows * columns * depth,
            bytes_accessed=(rows + 2 * columns) * depth + 2 * rows * columns,
            transcendentals=0,
        ),
        name="project",
    )(hidden, *pieces)


def relay_kernel(got_ref, part_ref, out_ref):
    keys = (part_ref[:, :HD] + got_ref[:, :HD].astype(F32)) + got_ref[:, HD : 2 * HD].astype(F32)
    pack(keys, part_ref[:, HD:] + got_ref[:, 2 * HD :].astype(F32), out_ref)


def finish_kernel(*refs):
    n = (len(refs) - 1) // 2
    out_ref = refs[-1]
    for i in range(n):
        got_ref, part_ref = refs[i], refs[n + i]
        rows = slice(i * part_ref.shape[0], (i + 1) * part_ref.shape[0])
        keys = part_ref[:, :HD] + got_ref[:, :HD].astype(F32)
        out_ref[rows, :HD] = (keys + got_ref[:, HD : 2 * HD].astype(F32)).astype(BF)
        out_ref[rows, HD:] = (part_ref[:, HD:] + got_ref[:, 2 * HD :].astype(F32)).astype(BF)


def small_kernel(kernel, name, shape, *args):
    whole = pl.BlockSpec(memory_space=pltpu.VMEM)
    return pl.pallas_call(
        kernel,
        out_shape=jax.ShapeDtypeStruct(shape, BF),
        in_specs=[whole] * len(args),
        out_specs=whole,
        compiler_params=pltpu.CompilerParams(vmem_limit_bytes=2 * 2**20),
        cost_estimate=pl.CostEstimate(
            flops=4 * math.prod(shape), bytes_accessed=8 * math.prod(shape), transcendentals=0
        ),
        name=name,
    )(*args)


def reduce_heads(parts):
    down, up = parts[3], parts[SIDE + 1]
    for first, second in ((2, 2), (1, 3)):
        down = small_kernel(relay_kernel, "relay", down.shape, send_tp(down, 1), parts[first])
        up = small_kernel(relay_kernel, "relay", up.shape, send_tp(up, -1), parts[SIDE + second])
    return [send_tp(down, 1), send_tp(up, -1)], [parts[0], parts[SIDE]]


def weight_kernel(*refs):
    mine, theirs = refs[:5], refs[5:10]
    h_mine, h_theirs = refs[10:12]
    outs = refs[12 : 12 + SIDE]
    left, result = refs[12 + SIDE :]
    y, z, core, tp = here_in_kernel()
    rows = mine[0].shape[1]

    @pl.when(pl.program_id(0) == 0)
    def _():
        for half, refs_of in enumerate((mine, theirs)):
            at = 0
            for piece in refs_of:
                left[pl.ds(at, piece.shape[0]), half * rows : (half + 1) * rows] = piece[...]
                at += piece.shape[0]

    result[...] = jnp.dot(
        left[:, :rows], h_mine[...], preferred_element_type=F32
    ) + jnp.dot(left[:, rows:], h_theirs[...], preferred_element_type=F32)

    def block(ja, jb):
        a_z, a_y = ring_mod(z + ja), ring_mod(y + ja)
        b_z, b_y = ring_mod(z + jb), ring_mod(y + jb)
        y_of = jnp.where(core == 0, b_y, a_y)
        z_of = jnp.where(core == 0, a_z, b_z)
        at = ring_mod(tp - y_of) * SIDE * OUT_ROWS + z_of * OUT_ROWS
        return result[pl.ds(pl.multiple_of(at, OUT_ROWS), OUT_ROWS), :]

    tile = result.shape[1]
    columns = pl.ds(pl.multiple_of(pl.program_id(0) * tile, tile), tile)
    for ja in range(SIDE):
        for jb in range(SIDE):
            outs[ja][jb, :, columns] = block(ja, jb).astype(outs[ja].dtype)


def weight_product(mine, theirs, h_mine, h_theirs):
    rows, depth = h_mine.shape
    tile = 512
    heads_rows = SIDE * SIDE * OUT_ROWS
    whole = pl.BlockSpec(memory_space=pltpu.VMEM)
    return pl.pallas_call(
        weight_kernel,
        out_shape=[jax.ShapeDtypeStruct((SIDE, OUT_ROWS, depth), F32)]
        + [jax.ShapeDtypeStruct((SIDE, OUT_ROWS, depth), BF)] * (SIDE - 1),
        grid=(depth // tile,),
        in_specs=[whole] * 10 + [pl.BlockSpec((rows, tile), lambda i: (0, i))] * 2,
        out_specs=[whole] * SIDE,
        scratch_shapes=[
            pltpu.VMEM((heads_rows, 2 * rows), BF),
            pltpu.VMEM((heads_rows, tile), F32),
        ],
        compiler_params=pltpu.CompilerParams(vmem_limit_bytes=16 * 2**20),
        cost_estimate=pl.CostEstimate(
            flops=4 * heads_rows * rows * depth,
            bytes_accessed=4 * rows * depth + 4 * heads_rows * depth,
            transcendentals=0,
        ),
        name="weight_product",
    )(*mine, *theirs, h_mine, h_theirs)


def reduce_owners(blocks):
    own, one, two, three = blocks
    left = send_first(one, 1)
    right = send_first(three, -1)
    far = send_first(two, 2)
    total = (own + left.astype(F32)) + (right.astype(F32) + far.astype(F32))
    low = total[1:].astype(BF)
    left = send_second(low[0], 1)
    right = send_second(low[2], -1)
    far = send_second(low[1], 2)
    return (total[0] + left.astype(F32)) + (right.astype(F32) + far.astype(F32))


def attention_kernel(
    n_src, n_dst, taken_by, out_buf, out_row, q_ref, do_ref, own_ref, *rest
):
    srcs = rest[:n_src]
    dq_ref, down_ref = rest[n_src : n_src + 2]
    outs = rest[n_src + 2 : n_src + n_dst + 2]
    keys_at, values_at, q_st, do_st, p_t, ds_t = rest[n_src + n_dst + 2 :]
    step = pl.program_id(0)
    group = q_ref.shape[1] // HD
    keys = keys_at.shape[1]
    rows = keys - own_ref.shape[0]
    retrieved = rows // PLEN
    scaling = HD ** (-0.5)

    slots = taken_by.shape[0] // n_src

    @pl.when(step == 0)
    def _():
        for b in range(n_src):
            for m in range(slots):
                to = taken_by[b * slots + m]

                @pl.when(to >= 0)
                def _():
                    query = lax.div(to, retrieved)
                    into = pl.ds(pl.multiple_of(lax.rem(to, retrieved) * PLEN, PLEN), PLEN)
                    keys_at[query, into, :] = srcs[b][m, :, :HD]
                    values_at[query, into, :] = srcs[b][m, :, HD:]

    for g in range(group):
        q_st[pl.ds(g * HD, HD), :] = q_ref[:, g * HD : (g + 1) * HD]
        do_st[pl.ds(g * HD, HD), :] = do_ref[:, g * HD : (g + 1) * HD]
    keys_at[step, pl.ds(rows, keys - rows), :] = own_ref[:, :HD]
    values_at[step, pl.ds(rows, keys - rows), :] = own_ref[:, HD:]
    k_all = keys_at[step]
    v_all = values_at[step]
    width = 2 * HD
    key_at = lax.broadcasted_iota(jnp.int32, (keys - rows, width), 0)
    tok_at = lax.broadcasted_iota(jnp.int32, (keys - rows, width), 1) % HD
    visible = key_at <= tok_at
    for g in range(0, group, 2):
        cols = pl.ds(g * HD, width)
        s = lax.dot_general(k_all, q_st[cols, :], NT, preferred_element_type=F32)
        s = jnp.concatenate(
            [s[:rows], jnp.where(visible, s[rows:], F32(-1e30))], axis=0
        )
        largest = jnp.max(s, axis=0, keepdims=True)
        e = jnp.exp2((s - largest) * F32(scaling * math.log2(math.e)))
        w = e * (1.0 / jnp.sum(e, axis=0, keepdims=True))
        w_low = w.astype(BF)
        p_t[:, cols] = w_low
        gw = lax.dot_general(v_all, do_st[cols, :], NT, preferred_element_type=F32)
        delta = jnp.sum(w_low.astype(F32) * gw, axis=0, keepdims=True)
        ds_t[:, cols] = (w * (gw - delta)).astype(BF)
    d_v = jnp.dot(p_t[...], do_st[...], preferred_element_type=F32)
    d_k = jnp.dot(ds_t[...], q_st[...], preferred_element_type=F32) * F32(scaling)
    d_q = lax.dot_general(ds_t[...], k_all, TN, preferred_element_type=F32) * F32(scaling)
    for g in range(group):
        dq_ref[:, g * HD : (g + 1) * HD] = d_q[g * HD : (g + 1) * HD].astype(BF)

    down_ref[:, :HD] = d_k[rows:].astype(BF)
    down_ref[:, HD:] = d_v[rows:].astype(BF)

    for j in range(retrieved):
        at = step * retrieved + j
        part = slice(j * PLEN, (j + 1) * PLEN)
        for b in range(n_dst):

            @pl.when(out_buf[at] == b)
            def _():
                outs[b][out_row[at], :, :HD] = d_k[part].astype(BF)
                outs[b][out_row[at], :, HD:] = d_v[part].astype(BF)


def attention(queries, out_grad, query_kv, sources, out_blocks, places, n_query):
    rows, width = queries.shape
    qlen = rows // n_query
    retrieved = places[1].shape[0] // n_query
    keys = retrieved * PLEN + qlen
    local = query_kv.shape[1]
    block = lambda w: pl.BlockSpec((qlen, w), lambda i, *_: (i, 0))
    whole = pl.BlockSpec(memory_space=pltpu.VMEM)
    return pl.pallas_call(
        functools.partial(attention_kernel, len(sources), len(out_blocks)),
        out_shape=(
            jax.ShapeDtypeStruct((rows, width), BF),
            jax.ShapeDtypeStruct((rows, local), BF),
        )
        + tuple(jax.ShapeDtypeStruct((n, PLEN, local), BF) for n in out_blocks),
        grid_spec=pltpu.PrefetchScalarGridSpec(
            num_scalar_prefetch=3,
            grid=(n_query,),
            in_specs=[block(width), block(width), block(local)] + [whole] * len(sources),
            out_specs=(block(width), block(local)) + (whole,) * len(out_blocks),
            scratch_shapes=[
                pltpu.VMEM((n_query, keys, HD), BF),
                pltpu.VMEM((n_query, keys, HD), BF),
                pltpu.VMEM((width, HD), BF),
                pltpu.VMEM((width, HD), BF),
                pltpu.VMEM((keys, width), BF),
                pltpu.VMEM((keys, width), BF),
            ],
        ),
        compiler_params=pltpu.CompilerParams(vmem_limit_bytes=26 * 2**20),
        cost_estimate=pl.CostEstimate(
            flops=10 * n_query * keys * qlen * width,
            bytes_accessed=8 * rows * width + 4 * n_query * keys * local,
            transcendentals=n_query * keys * width,
        ),
        name="attention",
    )(*places, queries, out_grad, query_kv, *sources)


def pick_kernel(slot_of, *rest):
    ring, outs = rest[:SIDE], rest[SIDE:]
    n = outs[0].shape[0]
    for k in range(2 * SIDE):
        for m in range(n):
            outs[k][m] = ring[m // 2][jnp.maximum(slot_of[k * n + m], 0)]


def pick(slot_of, ring):
    n = slot_of.shape[0] // (2 * SIDE)
    whole = pl.BlockSpec(memory_space=pltpu.VMEM)
    shape = jax.ShapeDtypeStruct((n,) + ring[0].shape[1:], BF)
    return pl.pallas_call(
        pick_kernel,
        out_shape=[shape] * (2 * SIDE),
        grid_spec=pltpu.PrefetchScalarGridSpec(
            num_scalar_prefetch=1,
            in_specs=[whole] * SIDE,
            out_specs=[whole] * (2 * SIDE),
        ),
        compiler_params=pltpu.CompilerParams(vmem_limit_bytes=2 * 2**20),
        cost_estimate=pl.CostEstimate(
            flops=0, bytes_accessed=16 * SIDE * n * PLEN * HD, transcendentals=0
        ),
        name="pick",
    )(slot_of, *ring)


def add_blocks_kernel(slot_of, *rest):
    parts, outs, total = rest[: 2 * SIDE], rest[2 * SIDE : 3 * SIDE], rest[3 * SIDE]
    n = parts[0].shape[0]
    total[...] = jnp.zeros_like(total)
    for p, part in enumerate(parts):

        @pl.loop(0, n)
        def _(m):
            place = slot_of[p * n + m]

            @pl.when(place >= 0)
            def _():
                total[lax.div(m, 2), place] += part[m].astype(F32)

    outs[0][...] = total[0]
    for j in range(1, SIDE):
        outs[j][...] = total[j].astype(BF)


def add_blocks(slot_of, parts, passages):
    shape = (passages,) + parts[0].shape[1:]
    whole = pl.BlockSpec(memory_space=pltpu.VMEM)
    return pl.pallas_call(
        add_blocks_kernel,
        out_shape=[jax.ShapeDtypeStruct(shape, F32)]
        + [jax.ShapeDtypeStruct(shape, BF)] * (SIDE - 1),
        grid_spec=pltpu.PrefetchScalarGridSpec(
            num_scalar_prefetch=1,
            in_specs=[whole] * (2 * SIDE),
            out_specs=[whole] * SIDE,
            scratch_shapes=[pltpu.VMEM((SIDE,) + shape, F32)],
        ),
        compiler_params=pltpu.CompilerParams(vmem_limit_bytes=9 * 2**20),
        cost_estimate=pl.CostEstimate(
            flops=8 * parts[0].size, bytes_accessed=32 * parts[0].size, transcendentals=0
        ),
        name="add_blocks",
    )(slot_of, *parts)


def add_owners_kernel(own_ref, left_ref, far_ref, right_ref, mine_ref, theirs_ref, turned):
    core = lax.rem(lax.axis_index("pas"), 2)
    for p in range(own_ref.shape[0]):
        total = (own_ref[p] + left_ref[p].astype(F32)) + (
            far_ref[p].astype(F32) + right_ref[p].astype(F32)
        )
        turned[:, p * PLEN : (p + 1) * PLEN] = total.T.astype(BF)
    for z in range(SIDE):
        for ref, which in ((mine_ref, core), (theirs_ref, 1 - core)):
            at = pl.multiple_of(z * 2 * OUT_ROWS + which * OUT_ROWS, OUT_ROWS)
            ref[z * OUT_ROWS : (z + 1) * OUT_ROWS, :] = turned[pl.ds(at, OUT_ROWS), :]


def add_owners(parts):
    passages, length, width = parts[0].shape
    half = jax.ShapeDtypeStruct((width // 2, passages * length), BF)
    whole = pl.BlockSpec(memory_space=pltpu.VMEM)
    return pl.pallas_call(
        add_owners_kernel,
        out_shape=(half, half),
        in_specs=[whole] * SIDE,
        out_specs=(whole, whole),
        scratch_shapes=[pltpu.VMEM((width, passages * length), BF)],
        compiler_params=pltpu.CompilerParams(vmem_limit_bytes=5 * 2**20),
        cost_estimate=pl.CostEstimate(
            flops=4 * parts[0].size, bytes_accessed=12 * parts[0].size, transcendentals=0
        ),
        name="add_owners",
    )(*parts)


def requests(source_device, source_slot, owners, capacity):
    flat_device = source_device.reshape(-1)
    flat_slot = source_slot.reshape(-1)
    owner_hits = (flat_device[:, None] == jnp.arange(owners, dtype=jnp.int32)[None, :]).astype(
        jnp.int32
    )
    at = jnp.arange(flat_device.shape[0])
    earlier_same = jnp.logical_and(
        flat_device[:, None] == flat_device[None, :], at[None, :] < at[:, None]
    )
    ranking = jnp.sum(earlier_same.astype(jnp.int32), axis=1)
    slot_hits = (ranking[:, None] == jnp.arange(capacity, dtype=jnp.int32)[None, :]).astype(
        jnp.int32
    )
    placed = owner_hits[:, :, None] * slot_hits[:, None, :]
    table = jnp.sum(placed * (flat_slot + 1)[:, None, None], axis=0) - 1
    return flat_device, ranking, table


def ring_steps(y, z, core, to_y, to_z):
    back_y, back_z = (y - to_y) % SIDE, (z - to_z) % SIDE
    return jnp.where(core == 0, back_z, back_y), jnp.where(core == 0, back_y, back_z)


def own_places(flat_device, ranking, capacity):
    y, z, core, _ = here()
    owner_core = flat_device % 2
    ja, jb = ring_steps(
        y, z, owner_core, flat_device // (2 * SIDE), (flat_device // 2) % SIDE
    )
    n = SIDE * capacity
    block = ja * capacity + ranking
    same = owner_core == core
    named = jnp.where(same, jb, SIDE + jb) * n + block
    at = jnp.arange(2 * SIDE * n, dtype=jnp.int32)[:, None]
    request = jnp.arange(named.shape[0], dtype=jnp.int32)[None, :]
    taken_by = jnp.max(jnp.where(named[None, :] == at, request, -1), axis=1)
    return taken_by, jnp.where(same, jb, SIDE), jnp.where(same, block, jb * n + block)


def slots_served(tables, owners, capacity):
    y, z, core, _ = here()
    n = jnp.arange(SIDE * 2 * SIDE * capacity, dtype=jnp.int32)
    ja = (n // capacity) % SIDE
    owner = jnp.where(core == 0, device_at(y, (z - ja) % SIDE, 0), device_at((y - ja) % SIDE, z, 0))
    asks = n // (capacity * SIDE)
    at = (asks * owners + owner + core) * capacity + n % capacity
    return tables.reshape(-1)[at]


def per_device(passage_hidden, kv_weight, queries, query_kv, out_grad, source_device, source_slot):
    owners = lax.axis_size("pas")
    rows_local = passage_hidden.shape[0]
    local_width = query_kv.shape[1]
    passages_here = rows_local // PLEN
    queries_here = source_device.shape[0]
    capacity = 2

    flat_device, ranking, table = requests(source_device, source_slot, owners, capacity)
    shards = jnp.concatenate(ring_gather(kv_weight, send_first), axis=0)
    shards, table = lax.optimization_barrier((shards, table))
    weights = ring_gather(shards, send_second)
    weights = weights + [swap_cores(w) for w in weights]
    pair = jnp.concatenate([table, swap_cores(table)], axis=0)
    tables = jnp.stack([pair] + [send_second(pair, -k) for k in range(1, SIDE)])
    places = own_places(flat_device, ranking, capacity)
    served = slots_served(tables, owners, capacity)

    *lower, weights = project(passage_hidden, weights, 0)
    upper = project(passage_hidden, [weights], 2)
    lower_got, lower_own = reduce_heads(lower)
    upper_got, upper_own = reduce_heads(upper)
    own = small_kernel(
        finish_kernel,
        "finish",
        (rows_local, local_width),
        *lower_got,
        *upper_got,
        *lower_own,
        *upper_own,
    )
    own = own.reshape(passages_here, PLEN, local_width)
    wanted = pick(served, ring_gather(own, send_first))
    same, other = wanted[::2], wanted[1::2]
    other = [other[0]] + [send_second(other[k], k) for k in (1, 3, 2)]
    same = [same[0]] + [send_second(same[k], k) for k in (1, 3, 2)]
    for blocks in (other, same):
        blocks[2], blocks[3] = blocks[3], blocks[2]
    hidden_theirs = swap_cores(passage_hidden)
    half = SIDE * capacity
    grad_queries, own_grads, *grads = attention(
        queries,
        out_grad,
        query_kv,
        same + [swap_cores(g) for g in other],
        [half] * SIDE + [SIDE * half],
        places,
        queries_here,
    )
    mine, theirs = grads[:SIDE], swap_cores(grads[SIDE])
    theirs = [theirs[k * half : (k + 1) * half] for k in range(SIDE)]
    mine[1:] = [send_second(mine[k], -k) for k in range(1, SIDE)]
    theirs[1:] = [send_second(theirs[k], -k) for k in range(1, SIDE)]
    parts = [blocks for pair in zip(mine, theirs) for blocks in pair]
    sums = add_blocks(served, parts, passages_here)
    mine, theirs = add_owners([sums[0]] + [send_first(sums[j], -j) for j in range(1, SIDE)])
    mine_heads = ring_gather_halves(mine, send_tp)
    theirs_heads = ring_gather_halves(swap_cores(theirs), send_tp)
    blocks = weight_product(mine_heads, theirs_heads, passage_hidden, hidden_theirs)
    return grad_queries, own_grads, reduce_owners(blocks)


def solution(mesh):
    in_specs = (
        P("pas", "tp"),
        P("pas", "tp"),
        P("pas", "tp"),
        P("pas", "tp"),
        P("pas", "tp"),
        P("pas", None),
        P("pas", None),
    )
    out_specs = (P("pas", "tp"), P("pas", "tp"), P("pas", "tp"))
    return jax.shard_map(
        per_device, mesh=mesh, in_specs=in_specs, out_specs=out_specs, check_vma=False
    )
```

```python
import functools
import math

import jax
import jax.numpy as jnp
from jax import lax
from jax.experimental import pallas as pl
from jax.experimental.pallas import tpu as pltpu
from jax.sharding import PartitionSpec as P

HD = 128
PLEN = 128
BF = jnp.bfloat16
F32 = jnp.float32
NT = (((1,), (1,)), ((), ()))
TN = (((0,), (0,)), ((), ()))
SIDE = 4
SENT_FIRST = (3, 1)
OUT_ROWS = 32


def device_at(y, z, core):
    return (y * SIDE + z) * 2 + core


def ring_pairs(order, k):
    pairs = []
    for y in range(SIDE):
        for z in range(SIDE):
            for core in range(2):
                if (order + core) % 2 == 0:
                    to = device_at(y, (z + k) % SIDE, core)
                else:
                    to = device_at((y + k) % SIDE, z, core)
                pairs.append((device_at(y, z, core), to))
    return pairs


def send_first(x, k):
    return lax.ppermute(x, "pas", ring_pairs(0, k))


def send_second(x, k):
    return lax.ppermute(x, "pas", ring_pairs(1, k))


def send_tp(x, k):
    return lax.ppermute(x, "tp", [(i, (i + k) % SIDE) for i in range(SIDE)])


def swap_cores(x):
    return lax.ppermute(x, "pas", [(i, i ^ 1) for i in range(2 * SIDE * SIDE)])


def ring_gather(x, send):
    left = send(x, 1)
    right = send(x, -1)
    return [x, left, send(x, 2), right]


def ring_gather_halves(x, send):
    half = x.shape[0] // 2
    left = send(x, 1)
    right = send(x, -1)
    return [x, left, send(left[:half], 1), send(right[half:], -1), right]


def here():
    pas = lax.axis_index("pas")
    return pas // (2 * SIDE), (pas // 2) % SIDE, pas % 2, lax.axis_index("tp")


def here_in_kernel():
    pas = lax.axis_index("pas")
    return (
        lax.div(pas, 2 * SIDE),
        lax.rem(lax.div(pas, 2), SIDE),
        lax.rem(pas, 2),
        lax.axis_index("tp"),
    )


def ring_mod(n):
    return lax.rem(n + 2 * SIDE, SIDE)


def pack(keys, values, out_ref):
    high = keys.astype(BF)
    out_ref[:, :HD] = high
    out_ref[:, HD : 2 * HD] = (keys - high.astype(F32)).astype(BF)
    out_ref[:, 2 * HD :] = values.astype(BF)


def gather_rows(pieces, weights):
    y, z, core, tp = here_in_kernel()
    for src in range(2):
        which = core if src == 0 else 1 - core
        first = jnp.where(which == 0, z, y)
        second = jnp.where(which == 0, y, z)
        for jb in range(SIDE):
            for ja in range(SIDE):
                a = ring_mod(first - ja)
                b = ring_mod(second - jb)
                place = ring_mod(jnp.where(which == 0, b, a) - tp)
                part = (place * SIDE + jnp.where(which == 0, a, b)) * 2 + which
                weights[pl.ds(pl.multiple_of(part * OUT_ROWS, OUT_ROWS), OUT_ROWS), :] = pieces[
                    SIDE * src + jb
                ][ja * OUT_ROWS : (ja + 1) * OUT_ROWS, :]


def project_kernel(first, n_in, h_ref, *rest):
    outs = rest[n_in : n_in + 2 * SIDE]
    step = pl.program_id(0)
    if first == 0:
        weights = rest[n_in + 2 * SIDE]

        @pl.when(step == 0)
        def _():
            gather_rows(rest[:n_in], weights)

    else:
        weights = rest[0]
    block, head = outs[0].shape
    at = pl.ds(pl.multiple_of((first + step) * block, block), block)
    product = lax.dot_general(h_ref[at, :], weights[...], NT, preferred_element_type=F32)
    for i in range(2):

        @pl.when(step == i)
        def _():
            for j in range(SIDE):
                part = product[:, j * head : (j + 1) * head]
                if j == SENT_FIRST[i]:
                    pack(part[:, :HD], part[:, HD:], outs[i * SIDE + j])
                else:
                    outs[i * SIDE + j][...] = part


def project(hidden, pieces, first):
    rows, depth = hidden.shape
    block = rows // 4
    columns = 2 * SIDE * SIDE * OUT_ROWS
    head = columns // SIDE
    whole = pl.BlockSpec(memory_space=pltpu.VMEM)
    outs = [jax.ShapeDtypeStruct((block, head), F32)] * (2 * SIDE)
    for i in range(2):
        outs[i * SIDE + SENT_FIRST[i]] = jax.ShapeDtypeStruct((block, 3 * HD), BF)
    if first == 0:
        outs += [jax.ShapeDtypeStruct((columns, depth), BF)]
    return pl.pallas_call(
        functools.partial(project_kernel, first, len(pieces)),
        out_shape=outs,
        grid=(2,),
        in_specs=[whole] * (1 + len(pieces)),
        out_specs=[whole] * len(outs),
        compiler_params=pltpu.CompilerParams(vmem_limit_bytes=10 * 2**20),
        cost_estimate=pl.CostEstimate(
            flops=rows * columns * depth,
            bytes_accessed=(rows + 2 * columns) * depth + 2 * rows * columns,
            transcendentals=0,
        ),
        name="project",
    )(hidden, *pieces)


def relay_kernel(got_ref, part_ref, out_ref):
    keys = (part_ref[:, :HD] + got_ref[:, :HD].astype(F32)) + got_ref[:, HD : 2 * HD].astype(F32)
    pack(keys, part_ref[:, HD:] + got_ref[:, 2 * HD :].astype(F32), out_ref)


def finish_kernel(*refs):
    n = (len(refs) - 1) // 2
    out_ref = refs[-1]
    for i in range(n):
        got_ref, part_ref = refs[i], refs[n + i]
        rows = slice(i * part_ref.shape[0], (i + 1) * part_ref.shape[0])
        keys = part_ref[:, :HD] + got_ref[:, :HD].astype(F32)
        out_ref[rows, :HD] = (keys + got_ref[:, HD : 2 * HD].astype(F32)).astype(BF)
        out_ref[rows, HD:] = (part_ref[:, HD:] + got_ref[:, 2 * HD :].astype(F32)).astype(BF)


def small_kernel(kernel, name, shape, *args):
    whole = pl.BlockSpec(memory_space=pltpu.VMEM)
    return pl.pallas_call(
        kernel,
        out_shape=jax.ShapeDtypeStruct(shape, BF),
        in_specs=[whole] * len(args),
        out_specs=whole,
        compiler_params=pltpu.CompilerParams(vmem_limit_bytes=2 * 2**20),
        cost_estimate=pl.CostEstimate(
            flops=4 * math.prod(shape), bytes_accessed=8 * math.prod(shape), transcendentals=0
        ),
        name=name,
    )(*args)


def reduce_heads(parts):
    down, up = parts[3], parts[SIDE + 1]
    for first, second in ((2, 2), (1, 3)):
        down = small_kernel(relay_kernel, "relay", down.shape, send_tp(down, 1), parts[first])
        up = small_kernel(relay_kernel, "relay", up.shape, send_tp(up, -1), parts[SIDE + second])
    return [send_tp(down, 1), send_tp(up, -1)], [parts[0], parts[SIDE]]


def stack_heads(pieces, left):
    at = 0
    for piece in pieces:
        left[pl.ds(at, piece.shape[0]), :] = piece[...]
        at += piece.shape[0]


def columns_of_step(tile):
    return pl.ds(pl.multiple_of(pl.program_id(0) * tile, tile), tile)


def first_weight_kernel(*refs):
    h_ref, out_ref, left = refs[5:]

    @pl.when(pl.program_id(0) == 0)
    def _():
        stack_heads(refs[:5], left)

    out_ref[:, columns_of_step(h_ref.shape[1])] = jnp.dot(
        left[...], h_ref[...], preferred_element_type=F32
    )


def second_weight_kernel(*refs):
    h_ref, so_far = refs[5:7]
    outs = refs[7 : 7 + SIDE]
    left, result = refs[7 + SIDE :]
    y, z, core, tp = here_in_kernel()
    columns = columns_of_step(h_ref.shape[1])

    @pl.when(pl.program_id(0) == 0)
    def _():
        stack_heads(refs[:5], left)

    result[...] = so_far[:, columns] + jnp.dot(
        left[...], h_ref[...], preferred_element_type=F32
    )

    def block(ja, jb):
        a_z, a_y = ring_mod(z + ja), ring_mod(y + ja)
        b_z, b_y = ring_mod(z + jb), ring_mod(y + jb)
        y_of = jnp.where(core == 0, b_y, a_y)
        z_of = jnp.where(core == 0, a_z, b_z)
        at = ring_mod(tp - y_of) * SIDE * OUT_ROWS + z_of * OUT_ROWS
        return result[pl.ds(pl.multiple_of(at, OUT_ROWS), OUT_ROWS), :]

    for ja in range(SIDE):
        for jb in range(SIDE):
            outs[ja][jb, :, columns] = block(ja, jb).astype(outs[ja].dtype)


def weight_product(mine, theirs, h_mine, h_theirs):
    rows, depth = h_mine.shape
    tile = 512
    heads_rows = SIDE * SIDE * OUT_ROWS
    whole = pl.BlockSpec(memory_space=pltpu.VMEM)
    left = pltpu.VMEM((heads_rows, rows), BF)
    common = dict(
        grid=(depth // tile,),
        compiler_params=pltpu.CompilerParams(vmem_limit_bytes=12 * 2**20),
        cost_estimate=pl.CostEstimate(
            flops=2 * heads_rows * rows * depth,
            bytes_accessed=2 * rows * depth + 4 * heads_rows * depth,
            transcendentals=0,
        ),
    )
    in_specs = [whole] * 5 + [pl.BlockSpec((rows, tile), lambda i: (0, i))]
    so_far = pl.pallas_call(
        first_weight_kernel,
        out_shape=jax.ShapeDtypeStruct((heads_rows, depth), F32),
        in_specs=in_specs,
        out_specs=whole,
        scratch_shapes=[left],
        name="first_weight_product",
        **common,
    )(*mine, h_mine)
    return pl.pallas_call(
        second_weight_kernel,
        out_shape=[jax.ShapeDtypeStruct((SIDE, OUT_ROWS, depth), F32)]
        + [jax.ShapeDtypeStruct((SIDE, OUT_ROWS, depth), BF)] * (SIDE - 1),
        in_specs=in_specs + [whole],
        out_specs=[whole] * SIDE,
        scratch_shapes=[left, pltpu.VMEM((heads_rows, tile), F32)],
        name="second_weight_product",
        **common,
    )(*theirs, h_theirs, so_far)


def reduce_owners(blocks):
    own, one, two, three = blocks
    left = send_first(one, 1)
    right = send_first(three, -1)
    far = send_first(two, 2)
    total = (own + left.astype(F32)) + (right.astype(F32) + far.astype(F32))
    low = total[1:].astype(BF)
    left = send_second(low[0], 1)
    right = send_second(low[2], -1)
    far = send_second(low[1], 2)
    return (total[0] + left.astype(F32)) + (right.astype(F32) + far.astype(F32))


def attention_kernel(
    n_src, n_dst, taken_by, out_buf, out_row, q_ref, do_ref, own_ref, *rest
):
    srcs = rest[:n_src]
    dq_ref, down_ref = rest[n_src : n_src + 2]
    outs = rest[n_src + 2 : n_src + n_dst + 2]
    keys_at, values_at, q_st, do_st, p_t, ds_t = rest[n_src + n_dst + 2 :]
    step = pl.program_id(0)
    group = q_ref.shape[1] // HD
    keys = keys_at.shape[1]
    rows = keys - own_ref.shape[0]
    retrieved = rows // PLEN
    scaling = HD ** (-0.5)

    slots = taken_by.shape[0] // n_src

    @pl.when(step == 0)
    def _():
        for b in range(n_src):
            for m in range(slots):
                to = taken_by[b * slots + m]

                @pl.when(to >= 0)
                def _():
                    query = lax.div(to, retrieved)
                    into = pl.ds(pl.multiple_of(lax.rem(to, retrieved) * PLEN, PLEN), PLEN)
                    keys_at[query, into, :] = srcs[b][m, :, :HD]
                    values_at[query, into, :] = srcs[b][m, :, HD:]

    for g in range(group):
        q_st[pl.ds(g * HD, HD), :] = q_ref[:, g * HD : (g + 1) * HD]
        do_st[pl.ds(g * HD, HD), :] = do_ref[:, g * HD : (g + 1) * HD]
    keys_at[step, pl.ds(rows, keys - rows), :] = own_ref[:, :HD]
    values_at[step, pl.ds(rows, keys - rows), :] = own_ref[:, HD:]
    k_all = keys_at[step]
    v_all = values_at[step]
    width = 2 * HD
    key_at = lax.broadcasted_iota(jnp.int32, (keys - rows, width), 0)
    tok_at = lax.broadcasted_iota(jnp.int32, (keys - rows, width), 1) % HD
    visible = key_at <= tok_at
    for g in range(0, group, 2):
        cols = pl.ds(g * HD, width)
        s = lax.dot_general(k_all, q_st[cols, :], NT, preferred_element_type=F32)
        s = jnp.concatenate(
            [s[:rows], jnp.where(visible, s[rows:], F32(-1e30))], axis=0
        )
        largest = jnp.max(s, axis=0, keepdims=True)
        e = jnp.exp2((s - largest) * F32(scaling * math.log2(math.e)))
        w = e * (1.0 / jnp.sum(e, axis=0, keepdims=True))
        w_low = w.astype(BF)
        p_t[:, cols] = w_low
        gw = lax.dot_general(v_all, do_st[cols, :], NT, preferred_element_type=F32)
        delta = jnp.sum(w_low.astype(F32) * gw, axis=0, keepdims=True)
        ds_t[:, cols] = (w * (gw - delta)).astype(BF)
    d_v = jnp.dot(p_t[...], do_st[...], preferred_element_type=F32)
    d_k = jnp.dot(ds_t[...], q_st[...], preferred_element_type=F32) * F32(scaling)
    d_q = lax.dot_general(ds_t[...], k_all, TN, preferred_element_type=F32) * F32(scaling)
    for g in range(group):
        dq_ref[:, g * HD : (g + 1) * HD] = d_q[g * HD : (g + 1) * HD].astype(BF)

    down_ref[:, :HD] = d_k[rows:].astype(BF)
    down_ref[:, HD:] = d_v[rows:].astype(BF)

    for j in range(retrieved):
        at = step * retrieved + j
        part = slice(j * PLEN, (j + 1) * PLEN)
        for b in range(n_dst):

            @pl.when(out_buf[at] == b)
            def _():
                outs[b][out_row[at], :, :HD] = d_k[part].astype(BF)
                outs[b][out_row[at], :, HD:] = d_v[part].astype(BF)


def attention(queries, out_grad, query_kv, sources, out_blocks, places, n_query):
    rows, width = queries.shape
    qlen = rows // n_query
    retrieved = places[1].shape[0] // n_query
    keys = retrieved * PLEN + qlen
    local = query_kv.shape[1]
    block = lambda w: pl.BlockSpec((qlen, w), lambda i, *_: (i, 0))
    whole = pl.BlockSpec(memory_space=pltpu.VMEM)
    return pl.pallas_call(
        functools.partial(attention_kernel, len(sources), len(out_blocks)),
        out_shape=(
            jax.ShapeDtypeStruct((rows, width), BF),
            jax.ShapeDtypeStruct((rows, local), BF),
        )
        + tuple(jax.ShapeDtypeStruct((n, PLEN, local), BF) for n in out_blocks),
        grid_spec=pltpu.PrefetchScalarGridSpec(
            num_scalar_prefetch=3,
            grid=(n_query,),
            in_specs=[block(width), block(width), block(local)] + [whole] * len(sources),
            out_specs=(block(width), block(local)) + (whole,) * len(out_blocks),
            scratch_shapes=[
                pltpu.VMEM((n_query, keys, HD), BF),
                pltpu.VMEM((n_query, keys, HD), BF),
                pltpu.VMEM((width, HD), BF),
                pltpu.VMEM((width, HD), BF),
                pltpu.VMEM((keys, width), BF),
                pltpu.VMEM((keys, width), BF),
            ],
        ),
        compiler_params=pltpu.CompilerParams(vmem_limit_bytes=22 * 2**20),
        cost_estimate=pl.CostEstimate(
            flops=10 * n_query * keys * qlen * width,
            bytes_accessed=8 * rows * width + 4 * n_query * keys * local,
            transcendentals=n_query * keys * width,
        ),
        name="attention",
    )(*places, queries, out_grad, query_kv, *sources)


def pick_kernel(other, slot_of, *rest):
    ring, outs = rest[:SIDE], rest[-SIDE:]
    n = outs[0].shape[0]
    for k in range(SIDE):
        for m in range(n):
            at = (2 * k + other) * n + m
            outs[k][m] = ring[m // 2][jnp.maximum(slot_of[at], 0)]


def pick(slot_of, ring, other, *earlier):
    n = slot_of.shape[0] // (2 * SIDE)
    whole = pl.BlockSpec(memory_space=pltpu.VMEM)
    shape = jax.ShapeDtypeStruct((n,) + ring[0].shape[1:], BF)
    return pl.pallas_call(
        functools.partial(pick_kernel, other),
        out_shape=[shape] * SIDE,
        grid_spec=pltpu.PrefetchScalarGridSpec(
            num_scalar_prefetch=1,
            in_specs=[whole] * (SIDE + len(earlier)),
            out_specs=[whole] * SIDE,
        ),
        compiler_params=pltpu.CompilerParams(vmem_limit_bytes=2 * 2**20),
        cost_estimate=pl.CostEstimate(
            flops=0, bytes_accessed=8 * SIDE * n * PLEN * HD, transcendentals=0
        ),
        name="pick",
    )(slot_of, *ring, *earlier)


def add_blocks_kernel(slot_of, *rest):
    parts, outs, total = rest[: 2 * SIDE], rest[2 * SIDE : 3 * SIDE], rest[3 * SIDE]
    n = parts[0].shape[0]
    total[...] = jnp.zeros_like(total)
    for p, part in enumerate(parts):

        @pl.loop(0, n)
        def _(m):
            place = slot_of[p * n + m]

            @pl.when(place >= 0)
            def _():
                total[lax.div(m, 2), place] += part[m].astype(F32)

    outs[0][...] = total[0]
    for j in range(1, SIDE):
        outs[j][...] = total[j].astype(BF)


def add_blocks(slot_of, parts, passages):
    shape = (passages,) + parts[0].shape[1:]
    whole = pl.BlockSpec(memory_space=pltpu.VMEM)
    return pl.pallas_call(
        add_blocks_kernel,
        out_shape=[jax.ShapeDtypeStruct(shape, F32)]
        + [jax.ShapeDtypeStruct(shape, BF)] * (SIDE - 1),
        grid_spec=pltpu.PrefetchScalarGridSpec(
            num_scalar_prefetch=1,
            in_specs=[whole] * (2 * SIDE),
            out_specs=[whole] * SIDE,
            scratch_shapes=[pltpu.VMEM((SIDE,) + shape, F32)],
        ),
        compiler_params=pltpu.CompilerParams(vmem_limit_bytes=9 * 2**20),
        cost_estimate=pl.CostEstimate(
            flops=8 * parts[0].size, bytes_accessed=32 * parts[0].size, transcendentals=0
        ),
        name="add_blocks",
    )(slot_of, *parts)


def add_owners_kernel(own_ref, left_ref, far_ref, right_ref, mine_ref, theirs_ref, turned):
    core = lax.rem(lax.axis_index("pas"), 2)
    for p in range(own_ref.shape[0]):
        total = (own_ref[p] + left_ref[p].astype(F32)) + (
            far_ref[p].astype(F32) + right_ref[p].astype(F32)
        )
        turned[:, p * PLEN : (p + 1) * PLEN] = total.T.astype(BF)
    for z in range(SIDE):
        for ref, which in ((mine_ref, core), (theirs_ref, 1 - core)):
            at = pl.multiple_of(z * 2 * OUT_ROWS + which * OUT_ROWS, OUT_ROWS)
            ref[z * OUT_ROWS : (z + 1) * OUT_ROWS, :] = turned[pl.ds(at, OUT_ROWS), :]


def add_owners(parts):
    passages, length, width = parts[0].shape
    half = jax.ShapeDtypeStruct((width // 2, passages * length), BF)
    whole = pl.BlockSpec(memory_space=pltpu.VMEM)
    return pl.pallas_call(
        add_owners_kernel,
        out_shape=(half, half),
        in_specs=[whole] * SIDE,
        out_specs=(whole, whole),
        scratch_shapes=[pltpu.VMEM((width, passages * length), BF)],
        compiler_params=pltpu.CompilerParams(vmem_limit_bytes=5 * 2**20),
        cost_estimate=pl.CostEstimate(
            flops=4 * parts[0].size, bytes_accessed=12 * parts[0].size, transcendentals=0
        ),
        name="add_owners",
    )(*parts)


def requests(source_device, source_slot, owners, capacity):
    flat_device = source_device.reshape(-1)
    flat_slot = source_slot.reshape(-1)
    owner_hits = (flat_device[:, None] == jnp.arange(owners, dtype=jnp.int32)[None, :]).astype(
        jnp.int32
    )
    at = jnp.arange(flat_device.shape[0])
    earlier_same = jnp.logical_and(
        flat_device[:, None] == flat_device[None, :], at[None, :] < at[:, None]
    )
    ranking = jnp.sum(earlier_same.astype(jnp.int32), axis=1)
    slot_hits = (ranking[:, None] == jnp.arange(capacity, dtype=jnp.int32)[None, :]).astype(
        jnp.int32
    )
    placed = owner_hits[:, :, None] * slot_hits[:, None, :]
    table = jnp.sum(placed * (flat_slot + 1)[:, None, None], axis=0) - 1
    return flat_device, ranking, table


def ring_steps(y, z, core, to_y, to_z):
    back_y, back_z = (y - to_y) % SIDE, (z - to_z) % SIDE
    return jnp.where(core == 0, back_z, back_y), jnp.where(core == 0, back_y, back_z)


def own_places(flat_device, ranking, capacity):
    y, z, core, _ = here()
    owner_core = flat_device % 2
    ja, jb = ring_steps(
        y, z, owner_core, flat_device // (2 * SIDE), (flat_device // 2) % SIDE
    )
    n = SIDE * capacity
    block = ja * capacity + ranking
    same = owner_core == core
    named = jnp.where(same, jb, SIDE + jb) * n + block
    at = jnp.arange(2 * SIDE * n, dtype=jnp.int32)[:, None]
    request = jnp.arange(named.shape[0], dtype=jnp.int32)[None, :]
    taken_by = jnp.max(jnp.where(named[None, :] == at, request, -1), axis=1)
    return taken_by, jnp.where(same, jb, SIDE), jnp.where(same, block, jb * n + block)


def slots_served(tables, owners, capacity):
    y, z, core, _ = here()
    n = jnp.arange(SIDE * 2 * SIDE * capacity, dtype=jnp.int32)
    ja = (n // capacity) % SIDE
    owner = jnp.where(core == 0, device_at(y, (z - ja) % SIDE, 0), device_at((y - ja) % SIDE, z, 0))
    asks = n // (capacity * SIDE)
    at = (asks * owners + owner + core) * capacity + n % capacity
    return tables.reshape(-1)[at]


def per_device(passage_hidden, kv_weight, queries, query_kv, out_grad, source_device, source_slot):
    owners = lax.axis_size("pas")
    rows_local = passage_hidden.shape[0]
    local_width = query_kv.shape[1]
    passages_here = rows_local // PLEN
    queries_here = source_device.shape[0]
    capacity = 2

    flat_device, ranking, table = requests(source_device, source_slot, owners, capacity)
    shards = jnp.concatenate(ring_gather(kv_weight, send_first), axis=0)
    shards, table = lax.optimization_barrier((shards, table))
    weights = ring_gather(shards, send_second)
    weights = weights + [swap_cores(w) for w in weights]
    pair = jnp.concatenate([table, swap_cores(table)], axis=0)
    tables = jnp.stack([pair] + [send_second(pair, -k) for k in range(1, SIDE)])
    places = own_places(flat_device, ranking, capacity)
    served = slots_served(tables, owners, capacity)

    *lower, weights = project(passage_hidden, weights, 0)
    upper = project(passage_hidden, [weights], 2)
    lower_got, lower_own = reduce_heads(lower)
    upper_got, upper_own = reduce_heads(upper)
    own = small_kernel(
        finish_kernel,
        "finish",
        (rows_local, local_width),
        *lower_got,
        *upper_got,
        *lower_own,
        *upper_own,
    )
    own = own.reshape(passages_here, PLEN, local_width)
    ring = ring_gather(own, send_first)
    other = pick(served, ring, 1, places[0])
    swapped = [swap_cores(other[0])] + [swap_cores(send_second(other[k], k)) for k in range(1, SIDE)]
    same = pick(served, ring, 0, swapped[0])
    same = [same[0]] + [send_second(same[k], k) for k in range(1, SIDE)]
    hidden_theirs = swap_cores(passage_hidden)
    half = SIDE * capacity
    grad_queries, own_grads, *grads = attention(
        queries,
        out_grad,
        query_kv,
        same + swapped,
        [half] * SIDE + [SIDE * half],
        places,
        queries_here,
    )
    mine, theirs = grads[:SIDE], swap_cores(grads[SIDE])
    theirs = [theirs[k * half : (k + 1) * half] for k in range(SIDE)]
    mine[1:] = [send_second(mine[k], -k) for k in range(1, SIDE)]
    theirs[1:] = [send_second(theirs[k], -k) for k in range(1, SIDE)]
    parts = [blocks for pair in zip(mine, theirs) for blocks in pair]
    sums = add_blocks(served, parts, passages_here)
    mine, theirs = add_owners([sums[0]] + [send_first(sums[j], -j) for j in range(1, SIDE)])
    mine_heads = ring_gather_halves(mine, send_tp)
    theirs_heads = ring_gather_halves(swap_cores(theirs), send_tp)
    blocks = weight_product(mine_heads, theirs_heads, passage_hidden, hidden_theirs)
    return grad_queries, own_grads, reduce_owners(blocks)


def solution(mesh):
    in_specs = (
        P("pas", "tp"),
        P("pas", "tp"),
        P("pas", "tp"),
        P("pas", "tp"),
        P("pas", "tp"),
        P("pas", None),
        P("pas", None),
    )
    out_specs = (P("pas", "tp"), P("pas", "tp"), P("pas", "tp"))
    return jax.shard_map(
        per_device, mesh=mesh, in_specs=in_specs, out_specs=out_specs, check_vma=False
    )
```

```python
import functools
import math

import jax
import jax.numpy as jnp
from jax import lax
from jax.experimental import pallas as pl
from jax.experimental.pallas import tpu as pltpu
from jax.sharding import PartitionSpec as P

HD = 128
PLEN = 128
BF = jnp.bfloat16
F32 = jnp.float32
NT = (((1,), (1,)), ((), ()))
TN = (((0,), (0,)), ((), ()))
SIDE = 4
SENT_FIRST = (3, 1)
OUT_ROWS = 32


def device_at(y, z, core):
    return (y * SIDE + z) * 2 + core


def ring_pairs(order, k):
    pairs = []
    for y in range(SIDE):
        for z in range(SIDE):
            for core in range(2):
                if (order + core) % 2 == 0:
                    to = device_at(y, (z + k) % SIDE, core)
                else:
                    to = device_at((y + k) % SIDE, z, core)
                pairs.append((device_at(y, z, core), to))
    return pairs


def send_first(x, k):
    return lax.ppermute(x, "pas", ring_pairs(0, k))


def send_second(x, k):
    return lax.ppermute(x, "pas", ring_pairs(1, k))


def send_tp(x, k):
    return lax.ppermute(x, "tp", [(i, (i + k) % SIDE) for i in range(SIDE)])


def swap_cores(x):
    return lax.ppermute(x, "pas", [(i, i ^ 1) for i in range(2 * SIDE * SIDE)])


def ring_gather(x, send):
    left = send(x, 1)
    right = send(x, -1)
    return [x, left, send(x, 2), right]


def ring_gather_halves(x, send):
    half = x.shape[0] // 2
    left = send(x, 1)
    right = send(x, -1)
    return [x, left, send(left[:half], 1), send(right[half:], -1), right]


def here():
    pas = lax.axis_index("pas")
    return pas // (2 * SIDE), (pas // 2) % SIDE, pas % 2, lax.axis_index("tp")


def here_in_kernel():
    pas = lax.axis_index("pas")
    return (
        lax.div(pas, 2 * SIDE),
        lax.rem(lax.div(pas, 2), SIDE),
        lax.rem(pas, 2),
        lax.axis_index("tp"),
    )


def ring_mod(n):
    return lax.rem(n + 2 * SIDE, SIDE)


def pack(keys, values, out_ref):
    high = keys.astype(BF)
    out_ref[:, :HD] = high
    out_ref[:, HD : 2 * HD] = (keys - high.astype(F32)).astype(BF)
    out_ref[:, 2 * HD :] = values.astype(BF)


def gather_rows(pieces, weights):
    y, z, core, tp = here_in_kernel()
    for src in range(2):
        which = core if src == 0 else 1 - core
        first = jnp.where(which == 0, z, y)
        second = jnp.where(which == 0, y, z)
        for jb in range(SIDE):
            for ja in range(SIDE):
                a = ring_mod(first - ja)
                b = ring_mod(second - jb)
                place = ring_mod(jnp.where(which == 0, b, a) - tp)
                part = (place * SIDE + jnp.where(which == 0, a, b)) * 2 + which
                weights[pl.ds(pl.multiple_of(part * OUT_ROWS, OUT_ROWS), OUT_ROWS), :] = pieces[
                    SIDE * src + jb
                ][ja * OUT_ROWS : (ja + 1) * OUT_ROWS, :]


def project_kernel(first, n_in, h_ref, *rest):
    outs = rest[n_in : n_in + 2 * SIDE]
    step = pl.program_id(0)
    if first == 0:
        weights = rest[n_in + 2 * SIDE]

        @pl.when(step == 0)
        def _():
            gather_rows(rest[:n_in], weights)

    else:
        weights = rest[0]
    block, head = outs[0].shape
    at = pl.ds(pl.multiple_of((first + step) * block, block), block)
    product = lax.dot_general(h_ref[at, :], weights[...], NT, preferred_element_type=F32)
    for i in range(2):

        @pl.when(step == i)
        def _():
            for j in range(SIDE):
                part = product[:, j * head : (j + 1) * head]
                if j == SENT_FIRST[i]:
                    pack(part[:, :HD], part[:, HD:], outs[i * SIDE + j])
                else:
                    outs[i * SIDE + j][...] = part


def project(hidden, pieces, first):
    rows, depth = hidden.shape
    block = rows // 4
    columns = 2 * SIDE * SIDE * OUT_ROWS
    head = columns // SIDE
    whole = pl.BlockSpec(memory_space=pltpu.VMEM)
    outs = [jax.ShapeDtypeStruct((block, head), F32)] * (2 * SIDE)
    for i in range(2):
        outs[i * SIDE + SENT_FIRST[i]] = jax.ShapeDtypeStruct((block, 3 * HD), BF)
    if first == 0:
        outs += [jax.ShapeDtypeStruct((columns, depth), BF)]
    return pl.pallas_call(
        functools.partial(project_kernel, first, len(pieces)),
        out_shape=outs,
        grid=(2,),
        in_specs=[whole] * (1 + len(pieces)),
        out_specs=[whole] * len(outs),
        compiler_params=pltpu.CompilerParams(vmem_limit_bytes=10 * 2**20),
        cost_estimate=pl.CostEstimate(
            flops=rows * columns * depth,
            bytes_accessed=(rows + 2 * columns) * depth + 2 * rows * columns,
            transcendentals=0,
        ),
        name="project",
    )(hidden, *pieces)


def relay_kernel(got_ref, part_ref, out_ref):
    keys = (part_ref[:, :HD] + got_ref[:, :HD].astype(F32)) + got_ref[:, HD : 2 * HD].astype(F32)
    pack(keys, part_ref[:, HD:] + got_ref[:, 2 * HD :].astype(F32), out_ref)


def finish_kernel(*refs):
    n = (len(refs) - 1) // 2
    out_ref = refs[-1]
    for i in range(n):
        got_ref, part_ref = refs[i], refs[n + i]
        rows = slice(i * part_ref.shape[0], (i + 1) * part_ref.shape[0])
        keys = part_ref[:, :HD] + got_ref[:, :HD].astype(F32)
        out_ref[rows, :HD] = (keys + got_ref[:, HD : 2 * HD].astype(F32)).astype(BF)
        out_ref[rows, HD:] = (part_ref[:, HD:] + got_ref[:, 2 * HD :].astype(F32)).astype(BF)


def small_kernel(kernel, name, shape, *args):
    whole = pl.BlockSpec(memory_space=pltpu.VMEM)
    return pl.pallas_call(
        kernel,
        out_shape=jax.ShapeDtypeStruct(shape, BF),
        in_specs=[whole] * len(args),
        out_specs=whole,
        compiler_params=pltpu.CompilerParams(vmem_limit_bytes=2 * 2**20),
        cost_estimate=pl.CostEstimate(
            flops=4 * math.prod(shape), bytes_accessed=8 * math.prod(shape), transcendentals=0
        ),
        name=name,
    )(*args)


def reduce_heads(parts):
    down, up = parts[3], parts[SIDE + 1]
    for first, second in ((2, 2), (1, 3)):
        down = small_kernel(relay_kernel, "relay", down.shape, send_tp(down, 1), parts[first])
        up = small_kernel(relay_kernel, "relay", up.shape, send_tp(up, -1), parts[SIDE + second])
    return [send_tp(down, 1), send_tp(up, -1)], [parts[0], parts[SIDE]]


def stack_heads(pieces, left):
    at = 0
    for piece in pieces:
        left[pl.ds(at, piece.shape[0]), :] = piece[...]
        at += piece.shape[0]


def columns_of_step(tile):
    return pl.ds(pl.multiple_of(pl.program_id(0) * tile, tile), tile)


def first_weight_kernel(*refs):
    h_ref, out_ref, left = refs[5:]

    @pl.when(pl.program_id(0) == 0)
    def _():
        stack_heads(refs[:5], left)

    out_ref[:, columns_of_step(h_ref.shape[1])] = jnp.dot(
        left[...], h_ref[...], preferred_element_type=F32
    )


def second_weight_kernel(*refs):
    h_ref, so_far = refs[5:7]
    outs = refs[7 : 7 + SIDE]
    left, result = refs[7 + SIDE :]
    y, z, core, tp = here_in_kernel()
    columns = columns_of_step(h_ref.shape[1])

    @pl.when(pl.program_id(0) == 0)
    def _():
        stack_heads(refs[:5], left)

    result[...] = so_far[:, columns] + jnp.dot(
        left[...], h_ref[...], preferred_element_type=F32
    )

    def block(ja, jb):
        a_z, a_y = ring_mod(z + ja), ring_mod(y + ja)
        b_z, b_y = ring_mod(z + jb), ring_mod(y + jb)
        y_of = jnp.where(core == 0, b_y, a_y)
        z_of = jnp.where(core == 0, a_z, b_z)
        at = ring_mod(tp - y_of) * SIDE * OUT_ROWS + z_of * OUT_ROWS
        return result[pl.ds(pl.multiple_of(at, OUT_ROWS), OUT_ROWS), :]

    for ja in range(SIDE):
        for jb in range(SIDE):
            outs[ja][jb, :, columns] = block(ja, jb).astype(outs[ja].dtype)


def weight_product(mine, theirs, h_mine, h_theirs):
    rows, depth = h_mine.shape
    tile = 512
    heads_rows = SIDE * SIDE * OUT_ROWS
    whole = pl.BlockSpec(memory_space=pltpu.VMEM)
    left = pltpu.VMEM((heads_rows, rows), BF)
    common = dict(
        grid=(depth // tile,),
        compiler_params=pltpu.CompilerParams(vmem_limit_bytes=12 * 2**20),
        cost_estimate=pl.CostEstimate(
            flops=2 * heads_rows * rows * depth,
            bytes_accessed=2 * rows * depth + 4 * heads_rows * depth,
            transcendentals=0,
        ),
    )
    in_specs = [whole] * 5 + [pl.BlockSpec((rows, tile), lambda i: (0, i))]
    so_far = pl.pallas_call(
        first_weight_kernel,
        out_shape=jax.ShapeDtypeStruct((heads_rows, depth), F32),
        in_specs=in_specs,
        out_specs=whole,
        scratch_shapes=[left],
        name="first_weight_product",
        **common,
    )(*mine, h_mine)
    return pl.pallas_call(
        second_weight_kernel,
        out_shape=[jax.ShapeDtypeStruct((SIDE, OUT_ROWS, depth), F32)]
        + [jax.ShapeDtypeStruct((SIDE, OUT_ROWS, depth), BF)] * (SIDE - 1),
        in_specs=in_specs + [whole],
        out_specs=[whole] * SIDE,
        scratch_shapes=[left, pltpu.VMEM((heads_rows, tile), F32)],
        name="second_weight_product",
        **common,
    )(*theirs, h_theirs, so_far)


def reduce_owners(blocks):
    own, one, two, three = blocks
    left = send_first(one, 1)
    right = send_first(three, -1)
    far = send_first(two, 2)
    total = (own + left.astype(F32)) + (right.astype(F32) + far.astype(F32))
    low = total[1:].astype(BF)
    left = send_second(low[0], 1)
    right = send_second(low[2], -1)
    far = send_second(low[1], 2)
    return (total[0] + left.astype(F32)) + (right.astype(F32) + far.astype(F32))


def attention_kernel(
    n_src, n_dst, taken_by, out_buf, out_row, q_ref, do_ref, own_ref, *rest
):
    srcs = rest[:n_src]
    dq_ref, down_ref = rest[n_src : n_src + 2]
    outs = rest[n_src + 2 : n_src + n_dst + 2]
    keys_at, values_at, q_st, do_st, p_t, ds_t = rest[n_src + n_dst + 2 :]
    step = pl.program_id(0)
    group = q_ref.shape[1] // HD
    keys = keys_at.shape[1]
    rows = keys - own_ref.shape[0]
    retrieved = rows // PLEN
    scaling = HD ** (-0.5)

    slots = taken_by.shape[0] // n_src

    @pl.when(step == 0)
    def _():
        for b in range(n_src):
            for m in range(slots):
                to = taken_by[b * slots + m]

                @pl.when(to >= 0)
                def _():
                    query = lax.div(to, retrieved)
                    into = pl.ds(pl.multiple_of(lax.rem(to, retrieved) * PLEN, PLEN), PLEN)
                    at = slots + m if b == 2 else m
                    keys_at[query, into, :] = srcs[b][at, :, :HD]
                    values_at[query, into, :] = srcs[b][at, :, HD:]

    for g in range(group):
        q_st[pl.ds(g * HD, HD), :] = q_ref[:, g * HD : (g + 1) * HD]
        do_st[pl.ds(g * HD, HD), :] = do_ref[:, g * HD : (g + 1) * HD]
    keys_at[step, pl.ds(rows, keys - rows), :] = own_ref[:, :HD]
    values_at[step, pl.ds(rows, keys - rows), :] = own_ref[:, HD:]
    k_all = keys_at[step]
    v_all = values_at[step]
    width = 2 * HD
    key_at = lax.broadcasted_iota(jnp.int32, (keys - rows, width), 0)
    tok_at = lax.broadcasted_iota(jnp.int32, (keys - rows, width), 1) % HD
    visible = key_at <= tok_at
    for g in range(0, group, 2):
        cols = pl.ds(g * HD, width)
        s = lax.dot_general(k_all, q_st[cols, :], NT, preferred_element_type=F32)
        s = jnp.concatenate(
            [s[:rows], jnp.where(visible, s[rows:], F32(-1e30))], axis=0
        )
        largest = jnp.max(s, axis=0, keepdims=True)
        e = jnp.exp2((s - largest) * F32(scaling * math.log2(math.e)))
        w = e * (1.0 / jnp.sum(e, axis=0, keepdims=True))
        w_low = w.astype(BF)
        p_t[:, cols] = w_low
        gw = lax.dot_general(v_all, do_st[cols, :], NT, preferred_element_type=F32)
        delta = jnp.sum(w_low.astype(F32) * gw, axis=0, keepdims=True)
        ds_t[:, cols] = (w * (gw - delta)).astype(BF)
    d_v = jnp.dot(p_t[...], do_st[...], preferred_element_type=F32)
    d_k = jnp.dot(ds_t[...], q_st[...], preferred_element_type=F32) * F32(scaling)
    d_q = lax.dot_general(ds_t[...], k_all, TN, preferred_element_type=F32) * F32(scaling)
    for g in range(group):
        dq_ref[:, g * HD : (g + 1) * HD] = d_q[g * HD : (g + 1) * HD].astype(BF)

    down_ref[:, :HD] = d_k[rows:].astype(BF)
    down_ref[:, HD:] = d_v[rows:].astype(BF)

    for j in range(retrieved):
        at = step * retrieved + j
        part = slice(j * PLEN, (j + 1) * PLEN)
        for b in range(n_dst):

            @pl.when(out_buf[at] == b)
            def _():
                outs[b][out_row[at], :, :HD] = d_k[part].astype(BF)
                outs[b][out_row[at], :, HD:] = d_v[part].astype(BF)


def attention(queries, out_grad, query_kv, sources, out_blocks, places, n_query):
    rows, width = queries.shape
    qlen = rows // n_query
    retrieved = places[1].shape[0] // n_query
    keys = retrieved * PLEN + qlen
    local = query_kv.shape[1]
    block = lambda w: pl.BlockSpec((qlen, w), lambda i, *_: (i, 0))
    whole = pl.BlockSpec(memory_space=pltpu.VMEM)
    return pl.pallas_call(
        functools.partial(attention_kernel, len(sources), len(out_blocks)),
        out_shape=(
            jax.ShapeDtypeStruct((rows, width), BF),
            jax.ShapeDtypeStruct((rows, local), BF),
        )
        + tuple(jax.ShapeDtypeStruct((n, PLEN, local), BF) for n in out_blocks),
        grid_spec=pltpu.PrefetchScalarGridSpec(
            num_scalar_prefetch=3,
            grid=(n_query,),
            in_specs=[block(width), block(width), block(local)] + [whole] * len(sources),
            out_specs=(block(width), block(local)) + (whole,) * len(out_blocks),
            scratch_shapes=[
                pltpu.VMEM((n_query, keys, HD), BF),
                pltpu.VMEM((n_query, keys, HD), BF),
                pltpu.VMEM((width, HD), BF),
                pltpu.VMEM((width, HD), BF),
                pltpu.VMEM((keys, width), BF),
                pltpu.VMEM((keys, width), BF),
            ],
        ),
        compiler_params=pltpu.CompilerParams(vmem_limit_bytes=22 * 2**20),
        cost_estimate=pl.CostEstimate(
            flops=10 * n_query * keys * qlen * width,
            bytes_accessed=8 * rows * width + 4 * n_query * keys * local,
            transcendentals=n_query * keys * width,
        ),
        name="attention",
    )(*places, queries, out_grad, query_kv, *sources)


def pick_kernel(groups, slot_of, *rest):
    ring, outs = rest[:SIDE], rest[-len(groups) :]
    n = slot_of.shape[0] // (2 * SIDE)
    for group, out in zip(groups, outs):
        for i, (k, other) in enumerate(group):
            for m in range(n):
                place = jnp.maximum(slot_of[(2 * k + other) * n + m], 0)
                out[i * n + m] = ring[m // 2][place]


def pick(slot_of, ring, groups, *earlier):
    n = slot_of.shape[0] // (2 * SIDE)
    whole = pl.BlockSpec(memory_space=pltpu.VMEM)
    shapes = [
        jax.ShapeDtypeStruct((len(group) * n,) + ring[0].shape[1:], BF) for group in groups
    ]
    return pl.pallas_call(
        functools.partial(pick_kernel, groups),
        out_shape=shapes,
        grid_spec=pltpu.PrefetchScalarGridSpec(
            num_scalar_prefetch=1,
            in_specs=[whole] * (SIDE + len(earlier)),
            out_specs=[whole] * len(groups),
        ),
        compiler_params=pltpu.CompilerParams(vmem_limit_bytes=2 * 2**20),
        cost_estimate=pl.CostEstimate(
            flops=0, bytes_accessed=8 * SIDE * n * PLEN * HD, transcendentals=0
        ),
        name="pick",
    )(slot_of, *ring, *earlier)


def add_blocks_kernel(slot_of, *rest):
    parts, outs, total = rest[: -SIDE - 1], rest[-SIDE - 1 : -1], rest[-1]
    owners = SIDE * 2
    total[...] = jnp.zeros_like(total)
    first = 0
    for part in parts:

        @pl.loop(0, part.shape[0])
        def _(m):
            place = slot_of[first + m]

            @pl.when(place >= 0)
            def _():
                total[lax.div(lax.rem(m, owners), 2), place] += part[m].astype(F32)

        first += part.shape[0]

    outs[0][...] = total[0]
    for j in range(1, SIDE):
        outs[j][...] = total[j].astype(BF)


def add_blocks(slot_of, parts, passages):
    shape = (passages,) + parts[0].shape[1:]
    whole = pl.BlockSpec(memory_space=pltpu.VMEM)
    return pl.pallas_call(
        add_blocks_kernel,
        out_shape=[jax.ShapeDtypeStruct(shape, F32)]
        + [jax.ShapeDtypeStruct(shape, BF)] * (SIDE - 1),
        grid_spec=pltpu.PrefetchScalarGridSpec(
            num_scalar_prefetch=1,
            in_specs=[whole] * len(parts),
            out_specs=[whole] * SIDE,
            scratch_shapes=[pltpu.VMEM((SIDE,) + shape, F32)],
        ),
        compiler_params=pltpu.CompilerParams(vmem_limit_bytes=9 * 2**20),
        cost_estimate=pl.CostEstimate(
            flops=8 * parts[0].size, bytes_accessed=32 * parts[0].size, transcendentals=0
        ),
        name="add_blocks",
    )(slot_of, *parts)


def add_owners_kernel(own_ref, left_ref, far_ref, right_ref, mine_ref, theirs_ref, turned):
    core = lax.rem(lax.axis_index("pas"), 2)
    for p in range(own_ref.shape[0]):
        total = (own_ref[p] + left_ref[p].astype(F32)) + (
            far_ref[p].astype(F32) + right_ref[p].astype(F32)
        )
        turned[:, p * PLEN : (p + 1) * PLEN] = total.T.astype(BF)
    for z in range(SIDE):
        for ref, which in ((mine_ref, core), (theirs_ref, 1 - core)):
            at = pl.multiple_of(z * 2 * OUT_ROWS + which * OUT_ROWS, OUT_ROWS)
            ref[z * OUT_ROWS : (z + 1) * OUT_ROWS, :] = turned[pl.ds(at, OUT_ROWS), :]


def add_owners(parts):
    passages, length, width = parts[0].shape
    half = jax.ShapeDtypeStruct((width // 2, passages * length), BF)
    whole = pl.BlockSpec(memory_space=pltpu.VMEM)
    return pl.pallas_call(
        add_owners_kernel,
        out_shape=(half, half),
        in_specs=[whole] * SIDE,
        out_specs=(whole, whole),
        scratch_shapes=[pltpu.VMEM((width, passages * length), BF)],
        compiler_params=pltpu.CompilerParams(vmem_limit_bytes=5 * 2**20),
        cost_estimate=pl.CostEstimate(
            flops=4 * parts[0].size, bytes_accessed=12 * parts[0].size, transcendentals=0
        ),
        name="add_owners",
    )(*parts)


def requests(source_device, source_slot, owners, capacity):
    flat_device = source_device.reshape(-1)
    flat_slot = source_slot.reshape(-1)
    owner_hits = (flat_device[:, None] == jnp.arange(owners, dtype=jnp.int32)[None, :]).astype(
        jnp.int32
    )
    at = jnp.arange(flat_device.shape[0])
    earlier_same = jnp.logical_and(
        flat_device[:, None] == flat_device[None, :], at[None, :] < at[:, None]
    )
    ranking = jnp.sum(earlier_same.astype(jnp.int32), axis=1)
    slot_hits = (ranking[:, None] == jnp.arange(capacity, dtype=jnp.int32)[None, :]).astype(
        jnp.int32
    )
    placed = owner_hits[:, :, None] * slot_hits[:, None, :]
    table = jnp.sum(placed * (flat_slot + 1)[:, None, None], axis=0) - 1
    return flat_device, ranking, table


def ring_steps(y, z, core, to_y, to_z):
    back_y, back_z = (y - to_y) % SIDE, (z - to_z) % SIDE
    return jnp.where(core == 0, back_z, back_y), jnp.where(core == 0, back_y, back_z)


def own_places(flat_device, ranking, capacity):
    y, z, core, _ = here()
    owner_core = flat_device % 2
    ja, jb = ring_steps(
        y, z, owner_core, flat_device // (2 * SIDE), (flat_device // 2) % SIDE
    )
    n = SIDE * capacity
    block = ja * capacity + ranking
    same = owner_core == core
    named = jnp.where(same, jb, SIDE + jb) * n + block
    at = jnp.arange(2 * SIDE * n, dtype=jnp.int32)[:, None]
    request = jnp.arange(named.shape[0], dtype=jnp.int32)[None, :]
    taken_by = jnp.max(jnp.where(named[None, :] == at, request, -1), axis=1)
    return taken_by, jnp.where(same, jb, SIDE), jnp.where(same, block, jb * n + block)


def slots_served(tables, owners, capacity):
    y, z, core, _ = here()
    n = jnp.arange(SIDE * 2 * SIDE * capacity, dtype=jnp.int32)
    ja = (n // capacity) % SIDE
    owner = jnp.where(core == 0, device_at(y, (z - ja) % SIDE, 0), device_at((y - ja) % SIDE, z, 0))
    asks = n // (capacity * SIDE)
    at = (asks * owners + owner + core) * capacity + n % capacity
    return tables.reshape(-1)[at]


def per_device(passage_hidden, kv_weight, queries, query_kv, out_grad, source_device, source_slot):
    owners = lax.axis_size("pas")
    rows_local = passage_hidden.shape[0]
    local_width = query_kv.shape[1]
    passages_here = rows_local // PLEN
    queries_here = source_device.shape[0]
    capacity = 2

    flat_device, ranking, table = requests(source_device, source_slot, owners, capacity)
    shards = jnp.concatenate(ring_gather(kv_weight, send_first), axis=0)
    shards, table = lax.optimization_barrier((shards, table))
    weights = ring_gather(shards, send_second)
    weights = weights + [swap_cores(w) for w in weights]
    pair = jnp.concatenate([table, swap_cores(table)], axis=0)
    tables = jnp.stack([pair] + [send_second(pair, -k) for k in range(1, SIDE)])
    places = own_places(flat_device, ranking, capacity)
    served = slots_served(tables, owners, capacity)

    *lower, weights = project(passage_hidden, weights, 0)
    upper = project(passage_hidden, [weights], 2)
    lower_got, lower_own = reduce_heads(lower)
    upper_got, upper_own = reduce_heads(upper)
    own = small_kernel(
        finish_kernel,
        "finish",
        (rows_local, local_width),
        *lower_got,
        *upper_got,
        *lower_own,
        *upper_own,
    )
    own = own.reshape(passages_here, PLEN, local_width)
    ring = ring_gather(own, send_first)
    both, *other = pick(served, ring, [[(2, 1), (2, 0)], [(0, 1)], [(1, 1)], [(3, 1)]])
    both = send_second(both, 2)
    swapped = [
        swap_cores(other[0]),
        swap_cores(send_second(other[1], 1)),
        swap_cores(both),
        swap_cores(send_second(other[2], 3)),
    ]
    same = pick(served, ring, [[(0, 0)], [(1, 0)], [(3, 0)]], swapped[0])
    same = [same[0], send_second(same[1], 1), both, send_second(same[2], 3)]
    hidden_theirs = swap_cores(passage_hidden)
    half = SIDE * capacity
    grad_queries, own_grads, *grads = attention(
        queries,
        out_grad,
        query_kv,
        same + swapped,
        [half] * SIDE + [SIDE * half],
        places,
        queries_here,
    )
    mine, theirs = grads[:SIDE], swap_cores(grads[SIDE])
    theirs = [theirs[k * half : (k + 1) * half] for k in range(SIDE)]
    mine[1:] = [send_second(mine[k], -k) for k in range(1, SIDE)]
    theirs[1:] = [send_second(theirs[k], -k) for k in range(1, SIDE)]
    parts = [blocks for pair in zip(mine, theirs) for blocks in pair]
    sums = add_blocks(served, parts, passages_here)
    mine, theirs = add_owners([sums[0]] + [send_first(sums[j], -j) for j in range(1, SIDE)])
    mine_heads = ring_gather_halves(mine, send_tp)
    theirs_heads = ring_gather_halves(swap_cores(theirs), send_tp)
    blocks = weight_product(mine_heads, theirs_heads, passage_hidden, hidden_theirs)
    return grad_queries, own_grads, reduce_owners(blocks)


def solution(mesh):
    in_specs = (
        P("pas", "tp"),
        P("pas", "tp"),
        P("pas", "tp"),
        P("pas", "tp"),
        P("pas", "tp"),
        P("pas", None),
        P("pas", None),
    )
    out_specs = (P("pas", "tp"), P("pas", "tp"), P("pas", "tp"))
    return jax.shard_map(
        per_device, mesh=mesh, in_specs=in_specs, out_specs=out_specs, check_vma=False
    )
```

```python
import functools
import math

import jax
import jax.numpy as jnp
from jax import lax
from jax.experimental import pallas as pl
from jax.experimental.pallas import tpu as pltpu
from jax.sharding import PartitionSpec as P

HD = 128
PLEN = 128
BF = jnp.bfloat16
F32 = jnp.float32
NT = (((1,), (1,)), ((), ()))
TN = (((0,), (0,)), ((), ()))
SIDE = 4
SENT_FIRST = (3, 1)
OUT_ROWS = 32


def device_at(y, z, core):
    return (y * SIDE + z) * 2 + core


def ring_pairs(order, k):
    pairs = []
    for y in range(SIDE):
        for z in range(SIDE):
            for core in range(2):
                if (order + core) % 2 == 0:
                    to = device_at(y, (z + k) % SIDE, core)
                else:
                    to = device_at((y + k) % SIDE, z, core)
                pairs.append((device_at(y, z, core), to))
    return pairs


def send_first(x, k):
    return lax.ppermute(x, "pas", ring_pairs(0, k))


def send_second(x, k):
    return lax.ppermute(x, "pas", ring_pairs(1, k))


def send_tp(x, k):
    return lax.ppermute(x, "tp", [(i, (i + k) % SIDE) for i in range(SIDE)])


def swap_cores(x):
    return lax.ppermute(x, "pas", [(i, i ^ 1) for i in range(2 * SIDE * SIDE)])


def ring_gather(x, send):
    left = send(x, 1)
    right = send(x, -1)
    return [x, left, send(x, 2), right]


def ring_gather_halves(x, send):
    half = x.shape[0] // 2
    left = send(x, 1)
    right = send(x, -1)
    return [x, left, send(left[:half], 1), send(right[half:], -1), right]


def here():
    pas = lax.axis_index("pas")
    return pas // (2 * SIDE), (pas // 2) % SIDE, pas % 2, lax.axis_index("tp")


def here_in_kernel():
    pas = lax.axis_index("pas")
    return (
        lax.div(pas, 2 * SIDE),
        lax.rem(lax.div(pas, 2), SIDE),
        lax.rem(pas, 2),
        lax.axis_index("tp"),
    )


def ring_mod(n):
    return lax.rem(n + 2 * SIDE, SIDE)


def pack(keys, values, out_ref):
    high = keys.astype(BF)
    out_ref[:, :HD] = high
    out_ref[:, HD : 2 * HD] = (keys - high.astype(F32)).astype(BF)
    out_ref[:, 2 * HD :] = values.astype(BF)


def gather_rows(pieces, weights):
    y, z, core, tp = here_in_kernel()
    for src in range(2):
        which = core if src == 0 else 1 - core
        first = jnp.where(which == 0, z, y)
        second = jnp.where(which == 0, y, z)
        for jb in range(SIDE):
            for ja in range(SIDE):
                a = ring_mod(first - ja)
                b = ring_mod(second - jb)
                place = ring_mod(jnp.where(which == 0, b, a) - tp)
                part = (place * SIDE + jnp.where(which == 0, a, b)) * 2 + which
                weights[pl.ds(pl.multiple_of(part * OUT_ROWS, OUT_ROWS), OUT_ROWS), :] = pieces[
                    SIDE * src + jb
                ][ja * OUT_ROWS : (ja + 1) * OUT_ROWS, :]


def project_kernel(first, n_in, h_ref, *rest):
    outs = rest[n_in : n_in + 2 * SIDE]
    step = pl.program_id(0)
    if first == 0:
        weights = rest[n_in + 2 * SIDE]

        @pl.when(step == 0)
        def _():
            gather_rows(rest[:n_in], weights)

    else:
        weights = rest[0]
    block, head = outs[0].shape
    at = pl.ds(pl.multiple_of((first + step) * block, block), block)
    product = lax.dot_general(h_ref[at, :], weights[...], NT, preferred_element_type=F32)
    for i in range(2):

        @pl.when(step == i)
        def _():
            for j in range(SIDE):
                part = product[:, j * head : (j + 1) * head]
                if j == SENT_FIRST[i]:
                    pack(part[:, :HD], part[:, HD:], outs[i * SIDE + j])
                else:
                    outs[i * SIDE + j][...] = part


def project(hidden, pieces, first):
    rows, depth = hidden.shape
    block = rows // 4
    columns = 2 * SIDE * SIDE * OUT_ROWS
    head = columns // SIDE
    whole = pl.BlockSpec(memory_space=pltpu.VMEM)
    outs = [jax.ShapeDtypeStruct((block, head), F32)] * (2 * SIDE)
    for i in range(2):
        outs[i * SIDE + SENT_FIRST[i]] = jax.ShapeDtypeStruct((block, 3 * HD), BF)
    if first == 0:
        outs += [jax.ShapeDtypeStruct((columns, depth), BF)]
    return pl.pallas_call(
        functools.partial(project_kernel, first, len(pieces)),
        out_shape=outs,
        grid=(2,),
        in_specs=[whole] * (1 + len(pieces)),
        out_specs=[whole] * len(outs),
        compiler_params=pltpu.CompilerParams(vmem_limit_bytes=10 * 2**20),
        cost_estimate=pl.CostEstimate(
            flops=rows * columns * depth,
            bytes_accessed=(rows + 2 * columns) * depth + 2 * rows * columns,
            transcendentals=0,
        ),
        name="project",
    )(hidden, *pieces)


def relay_kernel(got_ref, part_ref, out_ref):
    keys = (part_ref[:, :HD] + got_ref[:, :HD].astype(F32)) + got_ref[:, HD : 2 * HD].astype(F32)
    pack(keys, part_ref[:, HD:] + got_ref[:, 2 * HD :].astype(F32), out_ref)


def finish_kernel(*refs):
    n = (len(refs) - 1) // 2
    out_ref = refs[-1]
    for i in range(n):
        got_ref, part_ref = refs[i], refs[n + i]
        rows = slice(i * part_ref.shape[0], (i + 1) * part_ref.shape[0])
        keys = part_ref[:, :HD] + got_ref[:, :HD].astype(F32)
        out_ref[rows, :HD] = (keys + got_ref[:, HD : 2 * HD].astype(F32)).astype(BF)
        out_ref[rows, HD:] = (part_ref[:, HD:] + got_ref[:, 2 * HD :].astype(F32)).astype(BF)


def small_kernel(kernel, name, shape, *args):
    whole = pl.BlockSpec(memory_space=pltpu.VMEM)
    return pl.pallas_call(
        kernel,
        out_shape=jax.ShapeDtypeStruct(shape, BF),
        in_specs=[whole] * len(args),
        out_specs=whole,
        compiler_params=pltpu.CompilerParams(vmem_limit_bytes=2 * 2**20),
        cost_estimate=pl.CostEstimate(
            flops=4 * math.prod(shape), bytes_accessed=8 * math.prod(shape), transcendentals=0
        ),
        name=name,
    )(*args)


def reduce_heads(parts):
    down, up = parts[3], parts[SIDE + 1]
    for first, second in ((2, 2), (1, 3)):
        down = small_kernel(relay_kernel, "relay", down.shape, send_tp(down, 1), parts[first])
        up = small_kernel(relay_kernel, "relay", up.shape, send_tp(up, -1), parts[SIDE + second])
    return [send_tp(down, 1), send_tp(up, -1)], [parts[0], parts[SIDE]]


def stack_heads(pieces, left):
    at = 0
    for piece in pieces:
        left[pl.ds(at, piece.shape[0]), :] = piece[...]
        at += piece.shape[0]


def columns_of_step(tile):
    return pl.ds(pl.multiple_of(pl.program_id(0) * tile, tile), tile)


def first_weight_kernel(*refs):
    h_ref, out_ref, left = refs[5:]

    @pl.when(pl.program_id(0) == 0)
    def _():
        stack_heads(refs[:5], left)

    out_ref[:, columns_of_step(h_ref.shape[1])] = jnp.dot(
        left[...], h_ref[...], preferred_element_type=F32
    )


def second_weight_kernel(*refs):
    h_ref, so_far = refs[5:7]
    outs = refs[7 : 7 + SIDE]
    left, result = refs[7 + SIDE :]
    y, z, core, tp = here_in_kernel()
    columns = columns_of_step(h_ref.shape[1])

    @pl.when(pl.program_id(0) == 0)
    def _():
        stack_heads(refs[:5], left)

    result[...] = so_far[:, columns] + jnp.dot(
        left[...], h_ref[...], preferred_element_type=F32
    )

    def block(ja, jb):
        a_z, a_y = ring_mod(z + ja), ring_mod(y + ja)
        b_z, b_y = ring_mod(z + jb), ring_mod(y + jb)
        y_of = jnp.where(core == 0, b_y, a_y)
        z_of = jnp.where(core == 0, a_z, b_z)
        at = ring_mod(tp - y_of) * SIDE * OUT_ROWS + z_of * OUT_ROWS
        return result[pl.ds(pl.multiple_of(at, OUT_ROWS), OUT_ROWS), :]

    for ja in range(SIDE):
        for jb in range(SIDE):
            outs[ja][jb, :, columns] = block(ja, jb).astype(outs[ja].dtype)


def weight_product(mine, theirs, h_mine, h_theirs):
    rows, depth = h_mine.shape
    tile = 512
    heads_rows = SIDE * SIDE * OUT_ROWS
    whole = pl.BlockSpec(memory_space=pltpu.VMEM)
    left = pltpu.VMEM((heads_rows, rows), BF)
    common = dict(
        grid=(depth // tile,),
        compiler_params=pltpu.CompilerParams(vmem_limit_bytes=12 * 2**20),
        cost_estimate=pl.CostEstimate(
            flops=2 * heads_rows * rows * depth,
            bytes_accessed=2 * rows * depth + 4 * heads_rows * depth,
            transcendentals=0,
        ),
    )
    in_specs = [whole] * 5 + [pl.BlockSpec((rows, tile), lambda i: (0, i))]
    so_far = pl.pallas_call(
        first_weight_kernel,
        out_shape=jax.ShapeDtypeStruct((heads_rows, depth), F32),
        in_specs=in_specs,
        out_specs=whole,
        scratch_shapes=[left],
        name="first_weight_product",
        **common,
    )(*mine, h_mine)
    return pl.pallas_call(
        second_weight_kernel,
        out_shape=[jax.ShapeDtypeStruct((SIDE, OUT_ROWS, depth), F32)]
        + [jax.ShapeDtypeStruct((SIDE, OUT_ROWS, depth), BF)] * (SIDE - 1),
        in_specs=in_specs + [whole],
        out_specs=[whole] * SIDE,
        scratch_shapes=[left, pltpu.VMEM((heads_rows, tile), F32)],
        name="second_weight_product",
        **common,
    )(*theirs, h_theirs, so_far)


def reduce_owners(blocks):
    own, one, two, three = blocks
    left = send_first(one, 1)
    right = send_first(three, -1)
    far = send_first(two, 2)
    total = (own + left.astype(F32)) + (right.astype(F32) + far.astype(F32))
    low = total[1:].astype(BF)
    left = send_second(low[0], 1)
    right = send_second(low[2], -1)
    far = send_second(low[1], 2)
    return (total[0] + left.astype(F32)) + (right.astype(F32) + far.astype(F32))


def attention_kernel(
    n_src, n_dst, taken_by, out_buf, out_row, q_ref, do_ref, own_ref, *rest
):
    srcs = rest[:n_src]
    dq_ref, down_ref = rest[n_src : n_src + 2]
    outs = rest[n_src + 2 : n_src + n_dst + 2]
    keys_at, values_at, q_st, do_st, p_t, ds_t = rest[n_src + n_dst + 2 :]
    step = pl.program_id(0)
    group = q_ref.shape[1] // HD
    keys = keys_at.shape[1]
    rows = keys - own_ref.shape[0]
    retrieved = rows // PLEN
    scaling = HD ** (-0.5)

    slots = taken_by.shape[0] // n_src

    @pl.when(step == 0)
    def _():
        for b in range(n_src):
            for m in range(slots):
                to = taken_by[b * slots + m]

                @pl.when(to >= 0)
                def _():
                    query = lax.div(to, retrieved)
                    into = pl.ds(pl.multiple_of(lax.rem(to, retrieved) * PLEN, PLEN), PLEN)
                    keys_at[query, into, :] = srcs[b][m, :, :HD]
                    values_at[query, into, :] = srcs[b][m, :, HD:]

    for g in range(group):
        q_st[pl.ds(g * HD, HD), :] = q_ref[:, g * HD : (g + 1) * HD]
        do_st[pl.ds(g * HD, HD), :] = do_ref[:, g * HD : (g + 1) * HD]
    keys_at[step, pl.ds(rows, keys - rows), :] = own_ref[:, :HD]
    values_at[step, pl.ds(rows, keys - rows), :] = own_ref[:, HD:]
    k_all = keys_at[step]
    v_all = values_at[step]
    width = 2 * HD
    key_at = lax.broadcasted_iota(jnp.int32, (keys - rows, width), 0)
    tok_at = lax.broadcasted_iota(jnp.int32, (keys - rows, width), 1) % HD
    visible = key_at <= tok_at
    for g in range(0, group, 2):
        cols = pl.ds(g * HD, width)
        s = lax.dot_general(k_all, q_st[cols, :], NT, preferred_element_type=F32)
        s = jnp.concatenate(
            [s[:rows], jnp.where(visible, s[rows:], F32(-1e30))], axis=0
        )
        largest = jnp.max(s, axis=0, keepdims=True)
        e = jnp.exp2((s - largest) * F32(scaling * math.log2(math.e)))
        w = e * (1.0 / jnp.sum(e, axis=0, keepdims=True))
        w_low = w.astype(BF)
        p_t[:, cols] = w_low
        gw = lax.dot_general(v_all, do_st[cols, :], NT, preferred_element_type=F32)
        delta = jnp.sum(w_low.astype(F32) * gw, axis=0, keepdims=True)
        ds_t[:, cols] = (w * (gw - delta)).astype(BF)
    d_v = jnp.dot(p_t[...], do_st[...], preferred_element_type=F32)
    d_k = jnp.dot(ds_t[...], q_st[...], preferred_element_type=F32) * F32(scaling)
    d_q = lax.dot_general(ds_t[...], k_all, TN, preferred_element_type=F32) * F32(scaling)
    for g in range(group):
        dq_ref[:, g * HD : (g + 1) * HD] = d_q[g * HD : (g + 1) * HD].astype(BF)

    down_ref[:, :HD] = d_k[rows:].astype(BF)
    down_ref[:, HD:] = d_v[rows:].astype(BF)

    for j in range(retrieved):
        at = step * retrieved + j
        part = slice(j * PLEN, (j + 1) * PLEN)
        for b in range(n_dst):

            @pl.when(out_buf[at] == b)
            def _():
                outs[b][out_row[at], :, :HD] = d_k[part].astype(BF)
                outs[b][out_row[at], :, HD:] = d_v[part].astype(BF)


def attention(queries, out_grad, query_kv, sources, out_blocks, places, n_query):
    rows, width = queries.shape
    qlen = rows // n_query
    retrieved = places[1].shape[0] // n_query
    keys = retrieved * PLEN + qlen
    local = query_kv.shape[1]
    block = lambda w: pl.BlockSpec((qlen, w), lambda i, *_: (i, 0))
    whole = pl.BlockSpec(memory_space=pltpu.VMEM)
    return pl.pallas_call(
        functools.partial(attention_kernel, len(sources), len(out_blocks)),
        out_shape=(
            jax.ShapeDtypeStruct((rows, width), BF),
            jax.ShapeDtypeStruct((rows, local), BF),
        )
        + tuple(jax.ShapeDtypeStruct((n, PLEN, local), BF) for n in out_blocks),
        grid_spec=pltpu.PrefetchScalarGridSpec(
            num_scalar_prefetch=3,
            grid=(n_query,),
            in_specs=[block(width), block(width), block(local)] + [whole] * len(sources),
            out_specs=(block(width), block(local)) + (whole,) * len(out_blocks),
            scratch_shapes=[
                pltpu.VMEM((n_query, keys, HD), BF),
                pltpu.VMEM((n_query, keys, HD), BF),
                pltpu.VMEM((width, HD), BF),
                pltpu.VMEM((width, HD), BF),
                pltpu.VMEM((keys, width), BF),
                pltpu.VMEM((keys, width), BF),
            ],
        ),
        compiler_params=pltpu.CompilerParams(vmem_limit_bytes=22 * 2**20),
        cost_estimate=pl.CostEstimate(
            flops=10 * n_query * keys * qlen * width,
            bytes_accessed=8 * rows * width + 4 * n_query * keys * local,
            transcendentals=n_query * keys * width,
        ),
        name="attention",
    )(*places, queries, out_grad, query_kv, *sources)


def pick_kernel(other, slot_of, *rest):
    ring, outs = rest[:SIDE], rest[-SIDE:]
    n = outs[0].shape[0]
    for k in range(SIDE):
        for m in range(n):
            at = (2 * k + other) * n + m
            outs[k][m] = ring[m // 2][jnp.maximum(slot_of[at], 0)]


def pick(slot_of, ring, other, *earlier):
    n = slot_of.shape[0] // (2 * SIDE)
    whole = pl.BlockSpec(memory_space=pltpu.VMEM)
    shape = jax.ShapeDtypeStruct((n,) + ring[0].shape[1:], BF)
    return pl.pallas_call(
        functools.partial(pick_kernel, other),
        out_shape=[shape] * SIDE,
        grid_spec=pltpu.PrefetchScalarGridSpec(
            num_scalar_prefetch=1,
            in_specs=[whole] * (SIDE + len(earlier)),
            out_specs=[whole] * SIDE,
        ),
        compiler_params=pltpu.CompilerParams(vmem_limit_bytes=2 * 2**20),
        cost_estimate=pl.CostEstimate(
            flops=0, bytes_accessed=8 * SIDE * n * PLEN * HD, transcendentals=0
        ),
        name="pick",
    )(slot_of, *ring, *earlier)


def add_blocks_kernel(slot_of, *rest):
    parts, outs, total = rest[: 2 * SIDE], rest[2 * SIDE : 3 * SIDE], rest[3 * SIDE]
    n = parts[0].shape[0]
    total[...] = jnp.zeros_like(total)
    for p, part in enumerate(parts):

        @pl.loop(0, n)
        def _(m):
            place = slot_of[p * n + m]

            @pl.when(place >= 0)
            def _():
                total[lax.div(m, 2), place] += part[m].astype(F32)

    outs[0][...] = total[0]
    for j in range(1, SIDE):
        outs[j][...] = total[j].astype(BF)


def add_blocks(slot_of, parts, passages):
    shape = (passages,) + parts[0].shape[1:]
    whole = pl.BlockSpec(memory_space=pltpu.VMEM)
    return pl.pallas_call(
        add_blocks_kernel,
        out_shape=[jax.ShapeDtypeStruct(shape, F32)]
        + [jax.ShapeDtypeStruct(shape, BF)] * (SIDE - 1),
        grid_spec=pltpu.PrefetchScalarGridSpec(
            num_scalar_prefetch=1,
            in_specs=[whole] * (2 * SIDE),
            out_specs=[whole] * SIDE,
            scratch_shapes=[pltpu.VMEM((SIDE,) + shape, F32)],
        ),
        compiler_params=pltpu.CompilerParams(vmem_limit_bytes=9 * 2**20),
        cost_estimate=pl.CostEstimate(
            flops=8 * parts[0].size, bytes_accessed=32 * parts[0].size, transcendentals=0
        ),
        name="add_blocks",
    )(slot_of, *parts)


def add_owners_kernel(own_ref, left_ref, far_ref, right_ref, mine_ref, theirs_ref, turned):
    core = lax.rem(lax.axis_index("pas"), 2)
    for p in range(own_ref.shape[0]):
        total = (own_ref[p] + left_ref[p].astype(F32)) + (
            far_ref[p].astype(F32) + right_ref[p].astype(F32)
        )
        turned[:, p * PLEN : (p + 1) * PLEN] = total.T.astype(BF)
    for z in range(SIDE):
        for ref, which in ((mine_ref, core), (theirs_ref, 1 - core)):
            at = pl.multiple_of(z * 2 * OUT_ROWS + which * OUT_ROWS, OUT_ROWS)
            ref[z * OUT_ROWS : (z + 1) * OUT_ROWS, :] = turned[pl.ds(at, OUT_ROWS), :]


def add_owners(parts):
    passages, length, width = parts[0].shape
    half = jax.ShapeDtypeStruct((width // 2, passages * length), BF)
    whole = pl.BlockSpec(memory_space=pltpu.VMEM)
    return pl.pallas_call(
        add_owners_kernel,
        out_shape=(half, half),
        in_specs=[whole] * SIDE,
        out_specs=(whole, whole),
        scratch_shapes=[pltpu.VMEM((width, passages * length), BF)],
        compiler_params=pltpu.CompilerParams(vmem_limit_bytes=5 * 2**20),
        cost_estimate=pl.CostEstimate(
            flops=4 * parts[0].size, bytes_accessed=12 * parts[0].size, transcendentals=0
        ),
        name="add_owners",
    )(*parts)


def requests(source_device, source_slot, owners, capacity):
    flat_device = source_device.reshape(-1)
    flat_slot = source_slot.reshape(-1)
    owner_hits = (flat_device[:, None] == jnp.arange(owners, dtype=jnp.int32)[None, :]).astype(
        jnp.int32
    )
    at = jnp.arange(flat_device.shape[0])
    earlier_same = jnp.logical_and(
        flat_device[:, None] == flat_device[None, :], at[None, :] < at[:, None]
    )
    ranking = jnp.sum(earlier_same.astype(jnp.int32), axis=1)
    slot_hits = (ranking[:, None] == jnp.arange(capacity, dtype=jnp.int32)[None, :]).astype(
        jnp.int32
    )
    placed = owner_hits[:, :, None] * slot_hits[:, None, :]
    table = jnp.sum(placed * (flat_slot + 1)[:, None, None], axis=0) - 1
    return flat_device, ranking, table


def ring_steps(y, z, core, to_y, to_z):
    back_y, back_z = (y - to_y) % SIDE, (z - to_z) % SIDE
    return jnp.where(core == 0, back_z, back_y), jnp.where(core == 0, back_y, back_z)


def own_places(flat_device, ranking, capacity):
    y, z, core, _ = here()
    owner_core = flat_device % 2
    ja, jb = ring_steps(
        y, z, owner_core, flat_device // (2 * SIDE), (flat_device // 2) % SIDE
    )
    n = SIDE * capacity
    block = ja * capacity + ranking
    same = owner_core == core
    named = jnp.where(same, jb, SIDE + jb) * n + block
    at = jnp.arange(2 * SIDE * n, dtype=jnp.int32)[:, None]
    request = jnp.arange(named.shape[0], dtype=jnp.int32)[None, :]
    taken_by = jnp.max(jnp.where(named[None, :] == at, request, -1), axis=1)
    return taken_by, jnp.where(same, jb, SIDE), jnp.where(same, block, jb * n + block)


def slots_served(tables, owners, capacity):
    y, z, core, _ = here()
    n = jnp.arange(SIDE * 2 * SIDE * capacity, dtype=jnp.int32)
    ja = (n // capacity) % SIDE
    owner = jnp.where(core == 0, device_at(y, (z - ja) % SIDE, 0), device_at((y - ja) % SIDE, z, 0))
    asks = n // (capacity * SIDE)
    at = (asks * owners + owner + core) * capacity + n % capacity
    return tables.reshape(-1)[at]


def per_device(passage_hidden, kv_weight, queries, query_kv, out_grad, source_device, source_slot):
    owners = lax.axis_size("pas")
    rows_local = passage_hidden.shape[0]
    local_width = query_kv.shape[1]
    passages_here = rows_local // PLEN
    queries_here = source_device.shape[0]
    capacity = 2

    flat_device, ranking, table = requests(source_device, source_slot, owners, capacity)
    shards = jnp.concatenate(ring_gather(kv_weight, send_first), axis=0)
    shards, table = lax.optimization_barrier((shards, table))
    weights = ring_gather(shards, send_second)
    weights = weights + [swap_cores(w) for w in weights]
    pair = jnp.concatenate([table, swap_cores(table)], axis=0)
    tables = jnp.stack([pair] + [send_second(pair, -k) for k in range(1, SIDE)])
    places = own_places(flat_device, ranking, capacity)
    served = slots_served(tables, owners, capacity)

    *lower, weights = project(passage_hidden, weights, 0)
    upper = project(passage_hidden, [weights], 2)
    lower_got, lower_own = reduce_heads(lower)
    upper_got, upper_own = reduce_heads(upper)
    own = small_kernel(
        finish_kernel,
        "finish",
        (rows_local, local_width),
        *lower_got,
        *upper_got,
        *lower_own,
        *upper_own,
    )
    own = own.reshape(passages_here, PLEN, local_width)
    ring = ring_gather(own, send_first)
    other = pick(served, ring, 1)
    swapped = [swap_cores(other[0])] + [swap_cores(send_second(other[k], k)) for k in range(1, SIDE)]
    same = pick(served, ring, 0, swapped[0], places[0])
    same = [same[0]] + [send_second(same[k], k) for k in range(1, SIDE)]
    hidden_theirs = swap_cores(passage_hidden)
    half = SIDE * capacity
    grad_queries, own_grads, *grads = attention(
        queries,
        out_grad,
        query_kv,
        same + swapped,
        [half] * SIDE + [SIDE * half],
        places,
        queries_here,
    )
    mine, theirs = grads[:SIDE], swap_cores(grads[SIDE])
    theirs = [theirs[k * half : (k + 1) * half] for k in range(SIDE)]
    mine[1:] = [send_second(mine[k], -k) for k in range(1, SIDE)]
    theirs[1:] = [send_second(theirs[k], -k) for k in range(1, SIDE)]
    parts = [blocks for pair in zip(mine, theirs) for blocks in pair]
    sums = add_blocks(served, parts, passages_here)
    mine, theirs = add_owners([sums[0]] + [send_first(sums[j], -j) for j in range(1, SIDE)])
    mine_heads = ring_gather_halves(mine, send_tp)
    theirs_heads = ring_gather_halves(swap_cores(theirs), send_tp)
    blocks = weight_product(mine_heads, theirs_heads, passage_hidden, hidden_theirs)
    return grad_queries, own_grads, reduce_owners(blocks)


def solution(mesh):
    in_specs = (
        P("pas", "tp"),
        P("pas", "tp"),
        P("pas", "tp"),
        P("pas", "tp"),
        P("pas", "tp"),
        P("pas", None),
        P("pas", None),
    )
    out_specs = (P("pas", "tp"), P("pas", "tp"), P("pas", "tp"))
    return jax.shard_map(
        per_device, mesh=mesh, in_specs=in_specs, out_specs=out_specs, check_vma=False
    )
```
